32 devices in a mesh: img: 8 (over y, x, core), txt: 4 (over z).
Axes of the slice: x: 2, y: 2, z: 4, core: 2. Of those that a mesh axis runs over, the one named last changes fastest.
Arguments:
- image_embeds: bfloat16 [512, 1152], P(('img', 'txt')), may hold values from -0.1875 to 0.1875
- text_embeds: bfloat16 [512, 1152], P(('txt', 'img')), may hold values from -0.1875 to 0.1875
- pair_ids: int32 [512], P('img'), may hold values from 0 to 511, each once
Outputs:
- image_grad: float32 [512, 1152], P(('img', 'txt'))
- text_grad: float32 [512, 1152], P(('txt', 'img'))
The draws below stay inside these ranges and needn't reach their ends.
Inputs may be any that keep to these rules, and one draw needn't show every extreme that they name: pair_ids is a permutation of the text rows.
All inputs are finite; a program needn't handle non-finite values.
Results may differ from the reference program's by a relative error of at most 0.0036.
Values may be sent and summed in bfloat16 or wider, within the bound.
No kernel may reach another device: no remote copies, remote signals or barrier semaphores. Data moves between devices by JAX's collectives and lax.ppermute only.
A program may use at most 64 MiB of HBM per device.

```python
import jax
import jax.numpy as jnp
from jax import lax

D = 1152
ROW_DEV = 16
PAIRS = 512
N_TXT = 4


def levels(stream_key, dims, cuts, low, largest):
    gain = 1.0
    for position, parts in cuts:
        draws = jax.random.uniform(jax.random.fold_in(jax.random.fold_in(stream_key, 6), position), (parts,), jnp.float32, low / len(cuts), largest / len(cuts))
        gain = gain * jnp.repeat(jnp.exp(draws), dims[position] // parts).reshape((-1,) + (1,) * (len(dims) - 1 - position))
    return gain


def bell_draw(own_key, shape, width, bound, pieces=(), kind=jnp.bfloat16):
    factor_of = levels(own_key, shape, pieces, -0.22, 0.18) if pieces else 1.0
    values = jax.random.normal(own_key, shape, jnp.float32) * width * factor_of
    return jnp.minimum(jnp.maximum(values, -bound), bound).astype(kind)


def setup_inputs(seed: int = 0) -> dict:
    seeds = jax.random.split(jax.random.key(seed), 4)
    image_embeds = bell_draw(seeds[0], (PAIRS, D), 0.03, 0.1875, ((0, 32),))
    text_embeds = bell_draw(seeds[1], (PAIRS, D), 0.03, 0.1875, ((0, 32),))
    pair_ids = jax.random.permutation(seeds[2], PAIRS).astype(jnp.int32)
    return dict(image_embeds=image_embeds, text_embeds=text_embeds, pair_ids=pair_ids)


scale_logit = 8.0
shift_logit = -4.0
epsilon = 1e-06

def normalize(raw):
    values = raw.astype(jnp.float32)
    inverse = lax.rsqrt(lax.optimization_barrier(jnp.sum(values * values, axis=-1, keepdims=True)) + epsilon)
    return (values * inverse, inverse)

def back_norm(unit, inverse, grad):
    inner = lax.optimization_barrier(jnp.sum(unit * grad, axis=-1, keepdims=True))
    return inverse * (grad - unit * inner)

def reference(image_embeds, text_embeds, pair_ids):
    img_unit, img_inv = normalize(image_embeds)
    txt_unit, txt_inv = normalize(text_embeds)
    img_low = img_unit.astype(jnp.bfloat16)
    txt_low = txt_unit.astype(jnp.bfloat16)
    block = ROW_DEV * N_TXT
    count = PAIRS // block
    columns = jnp.arange(PAIRS, dtype=jnp.int32)

    def step(txt_acc, index):
        rows = lax.dynamic_slice_in_dim(img_low, (index * block).astype(jnp.int32), block, 0)
        ids = lax.dynamic_slice_in_dim(pair_ids, (index * block).astype(jnp.int32), block, 0)
        scores = lax.dot_general(rows, txt_low, (((1,), (1,)), ((), ())), preferred_element_type=jnp.float32)
        logit = scale_logit * scores + shift_logit
        label = jnp.where(ids[:, None] == columns[None, :], 1.0, -1.0).astype(jnp.float32)
        coeff = (-scale_logit * label * jax.nn.sigmoid(-label * logit)).astype(jnp.bfloat16)
        img_part = jnp.dot(coeff, txt_low, preferred_element_type=jnp.float32)
        txt_acc = txt_acc + lax.dot_general(coeff, rows, (((0,), (0,)), ((), ())), preferred_element_type=jnp.float32)
        return (txt_acc, img_part)
    txt_grad_z, img_parts = lax.scan(step, jnp.zeros((PAIRS, D), jnp.float32), jnp.arange(count, dtype=jnp.int32))
    img_grad_z = img_parts.reshape(PAIRS, D)
    return (back_norm(img_unit, img_inv, img_grad_z), back_norm(txt_unit, txt_inv, txt_grad_z))
```

```python
import jax
import jax.numpy as jnp
from jax import lax
from jax.sharding import PartitionSpec as P

scale_logit = 8.0
shift_logit = -4.0
epsilon = 1e-06


def normalize(raw):
    values = raw.astype(jnp.float32)
    inverse = lax.rsqrt(jnp.sum(values * values, axis=-1, keepdims=True) + epsilon)
    return (values * inverse, inverse)


def back_norm(unit, inverse, grad):
    inner = jnp.sum(unit * grad, axis=-1, keepdims=True)
    return inverse * (grad - unit * inner)


def pair_coeff(logit, same):
    label = jnp.where(same, 1.0, -1.0).astype(jnp.float32)
    return (-scale_logit * label * jax.nn.sigmoid(-label * logit)).astype(jnp.bfloat16)


def swap(block, axis, distance):
    size = lax.axis_size(axis)
    return lax.ppermute(block, axis, [(i, i ^ distance) for i in range(size)])


def local(image_embeds, text_embeds, pair_ids):
    rows = image_embeds.shape[0]
    n_img = lax.axis_size("img")
    n_txt = lax.axis_size("txt")
    me_img = lax.axis_index("img")
    me_txt = lax.axis_index("txt")
    txt_raw = [text_embeds] + [swap(text_embeds, "img", k) for k in range(1, n_img)]
    img_raw = [image_embeds] + [swap(image_embeds, "txt", k) for k in range(1, n_txt)]
    img_owner = jnp.arange(n_txt, dtype=jnp.int32) ^ me_txt
    txt_owner = jnp.arange(n_img, dtype=jnp.int32) ^ me_img
    ids = pair_ids.reshape(n_txt, rows)[img_owner].reshape(-1)
    columns = (
        (me_txt * n_img + txt_owner)[:, None] * rows + jnp.arange(rows, dtype=jnp.int32)[None, :]
    ).reshape(-1)
    img_unit, img_inv = normalize(jnp.concatenate(img_raw))
    txt_unit, txt_inv = normalize(jnp.concatenate(txt_raw))
    img_low = img_unit.astype(jnp.bfloat16)
    txt_low = txt_unit.astype(jnp.bfloat16)
    scores = lax.dot_general(
        img_low, txt_low, (((1,), (1,)), ((), ())), preferred_element_type=jnp.float32
    )
    logit = scale_logit * scores + shift_logit
    coeff = pair_coeff(logit, ids[:, None] == columns[None, :])
    img_part = jnp.dot(coeff, txt_low, preferred_element_type=jnp.float32)
    txt_part = lax.dot_general(
        coeff, img_low, (((0,), (0,)), ((), ())), preferred_element_type=jnp.float32
    )
    txt_send = txt_part.astype(jnp.bfloat16)
    img_send = img_part.astype(jnp.bfloat16)
    txt_got = [swap(txt_send[k * rows:(k + 1) * rows], "img", k) for k in range(1, n_img)]
    img_got = [swap(img_send[k * rows:(k + 1) * rows], "txt", k) for k in range(1, n_txt)]
    txt_sum = txt_part[:rows]
    for block in txt_got:
        txt_sum = txt_sum + block.astype(jnp.float32)
    img_sum = img_part[:rows]
    for block in img_got:
        img_sum = img_sum + block.astype(jnp.float32)
    return (
        back_norm(img_unit[:rows], img_inv[:rows], img_sum),
        back_norm(txt_unit[:rows], txt_inv[:rows], txt_sum),
    )


def solution(mesh):
    return jax.shard_map(
        local,
        mesh=mesh,
        in_specs=(P(("img", "txt"), None), P(("txt", "img"), None), P("img")),
        out_specs=(P(("img", "txt"), None), P(("txt", "img"), None)),
        check_vma=False,
    )
```

```python
import jax
import jax.numpy as jnp
from jax import lax
from jax.sharding import PartitionSpec as P

scale_logit = 8.0
shift_logit = -4.0
epsilon = 1e-06


def normalize(raw):
    values = raw.astype(jnp.float32)
    inverse = lax.rsqrt(jnp.sum(values * values, axis=-1, keepdims=True) + epsilon)
    return (values * inverse, inverse)


def back_norm(unit, inverse, grad):
    inner = jnp.sum(unit * grad, axis=-1, keepdims=True)
    return inverse * (grad - unit * inner)


def pair_coeff(logit, same):
    label = jnp.where(same, 1.0, -1.0).astype(jnp.float32)
    return (-scale_logit * label * jax.nn.sigmoid(-label * logit)).astype(jnp.bfloat16)


def spread(block, axis):
    copies = jnp.broadcast_to(block[None], (lax.axis_size(axis),) + block.shape)
    got = lax.all_to_all(copies, axis, split_axis=0, concat_axis=0)
    return got.reshape(-1, block.shape[1])


def local(image_embeds, text_embeds, pair_ids):
    rows = image_embeds.shape[0]
    n_img = lax.axis_size("img")
    n_txt = lax.axis_size("txt")
    me_img = lax.axis_index("img")
    me_txt = lax.axis_index("txt")
    txt_raw = spread(text_embeds, "img")
    img_raw = spread(image_embeds, "txt")
    columns = me_txt * n_img * rows + jnp.arange(n_img * rows, dtype=jnp.int32)
    img_unit, _ = normalize(img_raw)
    txt_unit, _ = normalize(txt_raw)
    img_low = img_unit.astype(jnp.bfloat16)
    txt_low = txt_unit.astype(jnp.bfloat16)
    scores = lax.dot_general(
        img_low, txt_low, (((1,), (1,)), ((), ())), preferred_element_type=jnp.float32
    )
    logit = scale_logit * scores + shift_logit
    coeff = pair_coeff(logit, pair_ids[:, None] == columns[None, :])
    img_part = jnp.dot(coeff, txt_low, preferred_element_type=jnp.float32)
    txt_part = lax.dot_general(
        coeff, img_low, (((0,), (0,)), ((), ())), preferred_element_type=jnp.float32
    )
    txt_send = txt_part.astype(jnp.bfloat16)
    img_send = img_part.astype(jnp.bfloat16)
    txt_got = lax.all_to_all(txt_send, "img", split_axis=0, concat_axis=0, tiled=True)
    img_got = lax.all_to_all(img_send, "txt", split_axis=0, concat_axis=0, tiled=True)
    txt_sum = jnp.sum(txt_got.reshape(n_img, rows, -1).astype(jnp.float32), axis=0)
    img_sum = jnp.sum(img_got.reshape(n_txt, rows, -1).astype(jnp.float32), axis=0)
    own_img = normalize(image_embeds)
    own_txt = normalize(text_embeds)
    return (back_norm(*own_img, img_sum), back_norm(*own_txt, txt_sum))


def solution(mesh):
    return jax.shard_map(
        local,
        mesh=mesh,
        in_specs=(P(("img", "txt"), None), P(("txt", "img"), None), P("img")),
        out_specs=(P(("img", "txt"), None), P(("txt", "img"), None)),
        check_vma=False,
    )
```

```python
import functools

import jax
import jax.numpy as jnp
from jax import lax
from jax.experimental import pallas as pl
from jax.experimental.pallas import tpu as pltpu
from jax.sharding import PartitionSpec as P

scale_logit = 8.0
shift_logit = -4.0
epsilon = 1e-06
f32 = jnp.float32
bf16 = jnp.bfloat16


def normalize(raw):
    values = raw.astype(f32)
    inverse = lax.rsqrt(jnp.sum(values * values, axis=-1, keepdims=True) + epsilon)
    return (values * inverse, inverse)


def back_norm(unit, inverse, grad):
    inner = jnp.sum(unit * grad, axis=-1, keepdims=True)
    return inverse * (grad - unit * inner)


def pair_coeff(logit, same):
    label = jnp.where(same, 1.0, -1.0).astype(f32)
    return (-scale_logit * label * jax.nn.sigmoid(-label * logit)).astype(bf16)


def swap(block, axis, distance):
    size = lax.axis_size(axis)
    return lax.ppermute(block, axis, [(i, i ^ distance) for i in range(size)])


def call(kernel, outs, args, scratch=()):
    vmem = pl.BlockSpec(memory_space=pltpu.VMEM)
    sizes = [a.size * a.dtype.itemsize for a in list(args) + list(outs)]
    return pl.pallas_call(
        kernel,
        out_shape=outs,
        in_specs=[vmem] * len(args),
        out_specs=[vmem] * len(outs),
        compiler_params=pltpu.CompilerParams(
            vmem_limit_bytes=min(48 * 2**20, 8 * 2**20 + 6 * sum(sizes))
        ),
    )(*args)


def low_kernel(*refs):
    out_ref = refs[-1]
    rows = refs[0].shape[0]
    for k, ref in enumerate(refs[:-1]):
        out_ref[k * rows:(k + 1) * rows, :] = normalize(ref[...])[0].astype(bf16)


def low_rows(pieces):
    rows, width = pieces[0].shape
    out = jax.ShapeDtypeStruct((len(pieces) * rows, width), bf16)
    return call(low_kernel, [out], pieces)[0]


def coeff_kernel(rows, odd, ids_ref, img_ref, txt_ref, coeff_ref):
    me_img = lax.axis_index("img")
    me_txt = lax.axis_index("txt")
    n_img = lax.axis_size("img")
    height = img_ref.shape[0]
    width = txt_ref.shape[0]
    row = lax.broadcasted_iota(jnp.int32, (height, height), 0)
    source = ((row // rows) ^ me_txt) * rows + row % rows
    here = lax.broadcasted_iota(jnp.int32, (height, height), 1) == source
    ids = jnp.sum(jnp.where(here, ids_ref[...], 0), axis=1, keepdims=True)
    column = lax.broadcasted_iota(jnp.int32, (height, width), 1)
    owner = (2 * (column // rows) + odd) ^ me_img
    same = ids == (me_txt * n_img + owner) * rows + column % rows
    scores = lax.dot_general(
        img_ref[...], txt_ref[...], (((1,), (1,)), ((), ())), preferred_element_type=f32
    )
    coeff_ref[...] = pair_coeff(scale_logit * scores + shift_logit, same)


def pair_block(rows, odd, ids, img_low, txt_low):
    out = jax.ShapeDtypeStruct((img_low.shape[0], txt_low.shape[0]), bf16)
    return call(functools.partial(coeff_kernel, rows, odd), [out], [ids, img_low, txt_low])[0]


def txt_kernel(coeff_ref, img_ref, out_ref):
    out_ref[...] = lax.dot_general(
        coeff_ref[...], img_ref[...], (((0,), (0,)), ((), ())), preferred_element_type=f32
    ).astype(out_ref.dtype)


def txt_part(coeff, img_low, dtype):
    out = jax.ShapeDtypeStruct((coeff.shape[1], img_low.shape[1]), dtype)
    return call(txt_kernel, [out], [coeff, img_low])[0]


def img_kernel(even_ref, odd_ref, txt_even_ref, txt_odd_ref, own_ref, *send_refs):
    rows = own_ref.shape[0]
    part = jnp.dot(even_ref[...], txt_even_ref[...], preferred_element_type=f32)
    part = part + jnp.dot(odd_ref[...], txt_odd_ref[...], preferred_element_type=f32)
    own_ref[...] = part[:rows]
    for k, ref in enumerate(send_refs):
        ref[...] = part[(k + 1) * rows:(k + 2) * rows].astype(bf16)


def add_kernel(own_ref, got_ref, keep_ref, *send_refs):
    rows = keep_ref.shape[0]
    keep_ref[...] = own_ref[:rows, :] + got_ref[:rows, :].astype(f32)
    for k, ref in enumerate(send_refs):
        block = slice((k + 1) * rows, (k + 2) * rows)
        ref[...] = (own_ref[block, :] + got_ref[block, :].astype(f32)).astype(bf16)


def last_kernel(raw_ref, own_ref, *refs):
    total = own_ref[...]
    for ref in refs[:-1]:
        total = total + ref[...].astype(f32)
    refs[-1][...] = back_norm(*normalize(raw_ref[...]), total)


def finish(raw, own, got):
    return call(last_kernel, [jax.ShapeDtypeStruct(raw.shape, f32)], [raw, own, *got])[0]


def local(image_embeds, text_embeds, pair_ids):
    rows, width = image_embeds.shape
    n_img = lax.axis_size("img")
    n_txt = lax.axis_size("txt")
    half = n_img // 2
    piece = jax.ShapeDtypeStruct((rows, width), bf16)
    total = jax.ShapeDtypeStruct((rows, width), f32)
    ids = pair_ids.reshape(1, -1)
    txt_even = low_rows([text_embeds] + [swap(text_embeds, "img", 2 * k) for k in range(1, half)])
    txt_odd = swap(txt_even, "img", 1)
    img_low = low_rows([image_embeds] + [swap(image_embeds, "txt", k) for k in range(1, n_txt)])
    even = pair_block(rows, 0, ids, img_low, txt_even)
    own = txt_part(even, img_low, f32)
    odd = pair_block(rows, 1, ids, img_low, txt_odd)
    got = swap(txt_part(odd, img_low, bf16), "img", 1)
    img_own, *img_send = call(
        img_kernel, [total] + [piece] * (n_txt - 1), [even, odd, txt_even, txt_odd]
    )
    txt_own, *txt_send = call(add_kernel, [total] + [piece] * (half - 1), [own, got])
    img_got = [swap(block, "txt", k + 1) for k, block in enumerate(img_send)]
    txt_got = [swap(block, "img", 2 * k + 2) for k, block in enumerate(txt_send)]
    return finish(image_embeds, img_own, img_got), finish(text_embeds, txt_own, txt_got)


def solution(mesh):
    return jax.shard_map(
        local,
        mesh=mesh,
        in_specs=(P(("img", "txt"), None), P(("txt", "img"), None), P("img")),
        out_specs=(P(("img", "txt"), None), P(("txt", "img"), None)),
        check_vma=False,
    )
```

```python
import functools

import jax
import jax.numpy as jnp
from jax import lax
from jax.experimental import pallas as pl
from jax.experimental.pallas import tpu as pltpu
from jax.sharding import PartitionSpec as P

scale_logit = 8.0
shift_logit = -4.0
epsilon = 1e-06
LONG = pl.CostEstimate(flops=10**10, bytes_accessed=10**7, transcendentals=0)
f32 = jnp.float32
bf16 = jnp.bfloat16


def normalize(raw):
    values = raw.astype(f32)
    inverse = lax.rsqrt(jnp.sum(values * values, axis=-1, keepdims=True) + epsilon)
    return (values * inverse, inverse)


def back_norm(unit, inverse, grad):
    inner = jnp.sum(unit * grad, axis=-1, keepdims=True)
    return inverse * (grad - unit * inner)


def pair_coeff(logit, same):
    label = jnp.where(same, 1.0, -1.0).astype(f32)
    return (-scale_logit * label * jax.nn.sigmoid(-label * logit)).astype(bf16)


def swap(block, axis, distance):
    size = lax.axis_size(axis)
    return lax.ppermute(block, axis, [(i, i ^ distance) for i in range(size)])


def call(kernel, outs, args, cost=None):
    vmem = pl.BlockSpec(memory_space=pltpu.VMEM)
    sizes = [a.size * a.dtype.itemsize for a in list(args) + list(outs)]
    return pl.pallas_call(
        kernel,
        out_shape=outs,
        in_specs=[vmem] * len(args),
        out_specs=[vmem] * len(outs),
        cost_estimate=cost,
        compiler_params=pltpu.CompilerParams(
            vmem_limit_bytes=min(48 * 2**20, 8 * 2**20 + 6 * sum(sizes))
        ),
    )(*args)


def low_kernel(*refs):
    out_ref = refs[-1]
    rows = refs[0].shape[0]
    for k, ref in enumerate(refs[:-1]):
        out_ref[k * rows:(k + 1) * rows, :] = normalize(ref[...])[0].astype(bf16)


def low_rows(pieces):
    rows, width = pieces[0].shape
    out = jax.ShapeDtypeStruct((len(pieces) * rows, width), bf16)
    return call(low_kernel, [out], pieces)[0]


def block_coeff(rows, odd, ids, img_low, txt_low):
    me_img = lax.axis_index("img")
    me_txt = lax.axis_index("txt")
    n_img = lax.axis_size("img")
    height = img_low.shape[0]
    width = txt_low.shape[0]
    row = lax.broadcasted_iota(jnp.int32, (height, height), 0)
    source = ((row // rows) ^ me_txt) * rows + row % rows
    here = lax.broadcasted_iota(jnp.int32, (height, height), 1) == source
    ids = jnp.sum(jnp.where(here, ids, 0), axis=1, keepdims=True)
    column = lax.broadcasted_iota(jnp.int32, (height, width), 1)
    owner = (2 * (column // rows) + odd) ^ me_img
    same = ids == (me_txt * n_img + owner) * rows + column % rows
    scores = lax.dot_general(
        img_low, txt_low, (((1,), (1,)), ((), ())), preferred_element_type=f32
    )
    return pair_coeff(scale_logit * scores + shift_logit, same)


def even_kernel(ids_ref, txt_ref, *refs):
    *raw_refs, img_ref, coeff_ref = refs
    rows = raw_refs[0].shape[0]
    low_kernel(*raw_refs, img_ref)
    coeff_ref[...] = block_coeff(rows, 0, ids_ref[...], img_ref[...], txt_ref[...])


def odd_kernel(rows, ids_ref, img_ref, txt_ref, coeff_ref, part_ref):
    coeff = block_coeff(rows, 1, ids_ref[...], img_ref[...], txt_ref[...])
    coeff_ref[...] = coeff
    part_ref[...] = lax.dot_general(
        coeff, img_ref[...], (((0,), (0,)), ((), ())), preferred_element_type=f32
    ).astype(bf16)


def txt_kernel(coeff_ref, img_ref, out_ref):
    out_ref[...] = lax.dot_general(
        coeff_ref[...], img_ref[...], (((0,), (0,)), ((), ())), preferred_element_type=f32
    ).astype(out_ref.dtype)


def txt_part(coeff, img_low, dtype):
    out = jax.ShapeDtypeStruct((coeff.shape[1], img_low.shape[1]), dtype)
    return call(txt_kernel, [out], [coeff, img_low])[0]


def img_kernel(even_ref, odd_ref, txt_even_ref, txt_odd_ref, own_ref, *send_refs):
    rows = own_ref.shape[0]
    part = jnp.dot(even_ref[...], txt_even_ref[...], preferred_element_type=f32)
    part = part + jnp.dot(odd_ref[...], txt_odd_ref[...], preferred_element_type=f32)
    own_ref[...] = part[:rows]
    for k, ref in enumerate(send_refs):
        ref[...] = part[(k + 1) * rows:(k + 2) * rows].astype(bf16)


def add_kernel(own_ref, got_ref, keep_ref, *send_refs):
    rows = keep_ref.shape[0]
    keep_ref[...] = own_ref[:rows, :] + got_ref[:rows, :].astype(f32)
    for k, ref in enumerate(send_refs):
        block = slice((k + 1) * rows, (k + 2) * rows)
        ref[...] = (own_ref[block, :] + got_ref[block, :].astype(f32)).astype(bf16)


def last_kernel(raw_ref, own_ref, *refs):
    total = own_ref[...]
    for ref in refs[:-1]:
        total = total + ref[...].astype(f32)
    refs[-1][...] = back_norm(*normalize(raw_ref[...]), total)


def finish(raw, own, got):
    return call(last_kernel, [jax.ShapeDtypeStruct(raw.shape, f32)], [raw, own, *got])[0]


def local(image_embeds, text_embeds, pair_ids):
    rows, width = image_embeds.shape
    n_img = lax.axis_size("img")
    n_txt = lax.axis_size("txt")
    half = n_img // 2
    piece = jax.ShapeDtypeStruct((rows, width), bf16)
    total = jax.ShapeDtypeStruct((rows, width), f32)
    ids = pair_ids.reshape(1, -1)
    txt_even = low_rows([text_embeds] + [swap(text_embeds, "img", 2 * k) for k in range(1, half)])
    txt_odd = swap(txt_even, "img", 1)
    img_raw = [image_embeds] + [swap(image_embeds, "txt", k) for k in range(1, n_txt)]
    low = jax.ShapeDtypeStruct((n_txt * rows, width), bf16)
    wide = jax.ShapeDtypeStruct((half * rows, width), bf16)
    coeff = jax.ShapeDtypeStruct((n_txt * rows, half * rows), bf16)
    img_low, even = call(even_kernel, [low, coeff], [ids, txt_even, *img_raw], LONG)
    odd, odd_part = call(
        functools.partial(odd_kernel, rows), [coeff, wide], [ids, img_low, txt_odd]
    )
    got = swap(odd_part, "img", 1)
    own = txt_part(even, img_low, f32)
    img_own, *img_send = call(
        img_kernel, [total] + [piece] * (n_txt - 1), [even, odd, txt_even, txt_odd]
    )
    txt_own, *txt_send = call(add_kernel, [total] + [piece] * (half - 1), [own, got])
    img_got = [swap(block, "txt", k + 1) for k, block in enumerate(img_send)]
    txt_got = [swap(block, "img", 2 * k + 2) for k, block in enumerate(txt_send)]
    return finish(image_embeds, img_own, img_got), finish(text_embeds, txt_own, txt_got)


def solution(mesh):
    return jax.shard_map(
        local,
        mesh=mesh,
        in_specs=(P(("img", "txt"), None), P(("txt", "img"), None), P("img")),
        out_specs=(P(("img", "txt"), None), P(("txt", "img"), None)),
        check_vma=False,
    )
```

```python
import functools

import jax
import jax.numpy as jnp
from jax import lax
from jax.experimental import pallas as pl
from jax.experimental.pallas import tpu as pltpu
from jax.sharding import PartitionSpec as P

scale_logit = 8.0
shift_logit = -4.0
epsilon = 1e-06
f32 = jnp.float32
bf16 = jnp.bfloat16
VMEM = pl.BlockSpec(memory_space=pltpu.VMEM)
LONG = pl.CostEstimate(flops=10**10, bytes_accessed=10**7, transcendentals=0)


def normalize(raw):
    values = raw.astype(f32)
    inverse = lax.rsqrt(jnp.sum(values * values, axis=-1, keepdims=True) + epsilon)
    return (values * inverse, inverse)


def back_norm(unit, inverse, grad):
    inner = jnp.sum(unit * grad, axis=-1, keepdims=True)
    return inverse * (grad - unit * inner)


def pair_coeff(logit, same):
    label = jnp.where(same, 1.0, -1.0).astype(f32)
    return (-scale_logit * label * jax.nn.sigmoid(-label * logit)).astype(bf16)


def core_swap(block):
    size = lax.axis_size("img")
    return lax.ppermute(block, "img", [(i, i ^ 1) for i in range(size)])


def chip_swap(block, distance):
    n_img, n_txt = lax.axis_size("img"), lax.axis_size("txt")
    pairs = []
    for img in range(n_img):
        for txt in range(n_txt):
            if img % 2 == 0 and distance < n_img // 2:
                pairs.append((img * n_txt + txt, (img ^ (2 * distance)) * n_txt + txt))
            if img % 2 == 1 and distance < n_txt:
                pairs.append((img * n_txt + txt, img * n_txt + (txt ^ distance)))
    return lax.ppermute(block, ("img", "txt"), pairs)


def is_even():
    return lax.axis_index("img") % 2 == 0


def call(kernel, outs, args, cost=None):
    sizes = [a.size * a.dtype.itemsize for a in list(args) + list(outs)]
    return pl.pallas_call(
        kernel,
        out_shape=outs,
        in_specs=[VMEM] * len(args),
        out_specs=[VMEM] * len(outs),
        cost_estimate=cost,
        compiler_params=pltpu.CompilerParams(
            vmem_limit_bytes=min(48 * 2**20, 8 * 2**20 + 6 * sum(sizes))
        ),
    )(*args)


def sides_kernel(own_ref, txt_ref, img_ref, mine_ref, other_ref, raw_ref):
    rows = txt_ref.shape[0]
    even = is_even()
    own = normalize(own_ref[...])[0].astype(bf16)
    own_txt, own_img = own[:rows], own[rows:]
    far_txt = normalize(txt_ref[...])[0].astype(bf16)
    far_img = normalize(img_ref[...])[0].astype(bf16)
    mine_ref[:rows, :] = jnp.where(even, own_txt, far_img)
    mine_ref[rows:, :] = jnp.where(even, far_txt, own_img)
    other_ref[:rows, :] = jnp.where(even, own_img, far_txt)
    other_ref[rows:, :] = jnp.where(even, far_img, own_txt)
    raw_ref[:rows, :] = jnp.where(even, own_ref[:rows, :], img_ref[...])
    raw_ref[rows:, :] = jnp.where(even, txt_ref[...], own_ref[rows:, :])


def row_ids(rows, ids, far_ids, count):
    me_img = lax.axis_index("img")
    me_txt = lax.axis_index("txt")
    n_img = lax.axis_size("img")
    row = lax.broadcasted_iota(jnp.int32, (count, 1), 0)
    chip, core, j = row // (2 * rows), row // rows % 2, row % rows
    txt_ids = (me_txt * n_img + (((me_img // 2) ^ chip) * 2 + core)) * rows + j
    source = (me_txt ^ chip) * rows + j
    here = lax.broadcasted_iota(jnp.int32, (count, ids.shape[1]), 1) == source
    per_core = jnp.where(core == me_img % 2, ids, far_ids)
    img_ids = jnp.sum(jnp.where(here, per_core, 0), axis=1, keepdims=True)
    return txt_ids, img_ids


def ids_kernel(ids_ref, far_ids_ref, piece_ref, mine_ids_ref, other_ids_ref, out_ref):
    height = piece_ref.shape[0]
    count = mine_ids_ref.shape[0]
    even = is_even()
    txt_ids, img_ids = row_ids(height // 2, ids_ref[...], far_ids_ref[...], count)
    mine_ids_ref[...] = jnp.where(even, txt_ids, img_ids)
    other_ids = jnp.where(even, img_ids, txt_ids)
    diagonal = lax.broadcasted_iota(jnp.int32, (count, count), 0) == lax.broadcasted_iota(
        jnp.int32, (count, count), 1
    )
    other_ids_ref[...] = jnp.sum(jnp.where(diagonal, other_ids, 0), axis=0, keepdims=True)
    out_ref[...] = piece_ref[...]


def part_of(mine_refs, other_refs, mine_ids_ref, other_ids):
    mine = jnp.concatenate([ref[...] for ref in mine_refs], axis=0)
    other = jnp.concatenate([ref[...] for ref in other_refs], axis=0)
    scores = lax.dot_general(
        mine, other, (((1,), (1,)), ((), ())), preferred_element_type=f32
    )
    same = mine_ids_ref[...] == other_ids
    coeff = pair_coeff(scale_logit * scores + shift_logit, same)
    return jnp.dot(coeff, other, preferred_element_type=f32)


def most_kernel(blocks, mine_ids_ref, other_ids_ref, *refs):
    mine_refs, other_refs, part_ref = refs[:blocks], refs[blocks:-1], refs[-1]
    width = (blocks - 1) * mine_refs[0].shape[0]
    part_ref[...] = part_of(mine_refs, other_refs, mine_ids_ref, other_ids_ref[:, :width])


def rest_kernel(blocks, mine_ids_ref, other_ids_ref, part_ref, *refs):
    mine_refs, last_ref, (own_ref, *send_refs) = refs[:blocks], refs[blocks], refs[blocks + 1:]
    height = own_ref.shape[0]
    start = (blocks - 1) * height
    part = part_ref[...] + part_of(
        mine_refs, [last_ref], mine_ids_ref, other_ids_ref[:, start:]
    )
    own_ref[...] = part[:height]
    for k, ref in enumerate(send_refs):
        ref[...] = part[(k + 1) * height:(k + 2) * height].astype(bf16)


def grad_kernel(raw_ref, own_ref, *refs):
    *got_refs, keep_ref, send_ref = refs
    rows = keep_ref.shape[0]
    total = own_ref[...]
    for ref in got_refs:
        total = total + ref[...].astype(f32)
    grad = back_norm(*normalize(raw_ref[...]), total)
    even = is_even()
    keep_ref[...] = jnp.where(even, grad[:rows], grad[rows:])
    send_ref[...] = jnp.where(even, grad[rows:], grad[:rows])


def out_kernel(keep_ref, got_ref, img_ref, txt_ref):
    even = is_even()
    keep, got = keep_ref[...], got_ref[...]
    img_ref[...] = jnp.where(even, got, keep)
    txt_ref[...] = jnp.where(even, keep, got)


def local(image_embeds, text_embeds, pair_ids):
    rows, width = image_embeds.shape
    blocks = max(lax.axis_size("img") // 2, lax.axis_size("txt"))
    pair = jax.ShapeDtypeStruct((2 * rows, width), bf16)
    total = jax.ShapeDtypeStruct((2 * rows, width), f32)
    single = jax.ShapeDtypeStruct((rows, width), f32)
    ids = pair_ids.reshape(1, -1)
    far_txt = core_swap(text_embeds)
    far_img = core_swap(image_embeds)
    far_ids = core_swap(ids)
    near = jnp.concatenate([text_embeds, image_embeds])
    mine, other, raw = call(sides_kernel, [pair] * 3, [near, far_txt, far_img])
    mine = [mine] + [chip_swap(mine, k) for k in range(1, blocks)]
    count = blocks * 2 * rows
    mine_ids, other_ids, first = call(
        ids_kernel,
        [
            jax.ShapeDtypeStruct((count, 1), jnp.int32),
            jax.ShapeDtypeStruct((1, count), jnp.int32),
            pair,
        ],
        [ids, far_ids, mine[1]],
    )
    other = [other] + [core_swap(block) for block in [first] + mine[2:]]
    part = jax.ShapeDtypeStruct((count, width), f32)
    (part,) = call(
        functools.partial(most_kernel, blocks),
        [part],
        [mine_ids, other_ids, *mine, *other[:-1]],
        cost=LONG,
    )
    own, *send = call(
        functools.partial(rest_kernel, blocks),
        [total] + [pair] * (blocks - 1),
        [mine_ids, other_ids, part, *mine, other[-1]],
    )
    got = [chip_swap(block, k + 1) for k, block in enumerate(send)]
    keep, send = call(grad_kernel, [single] * 2, [raw, own, *got])
    return tuple(call(out_kernel, [single] * 2, [keep, core_swap(send)]))


def solution(mesh):
    return jax.shard_map(
        local,
        mesh=mesh,
        in_specs=(P(("img", "txt"), None), P(("txt", "img"), None), P("img")),
        out_specs=(P(("img", "txt"), None), P(("txt", "img"), None)),
        check_vma=False,
    )
```

```python
import functools

import jax
import jax.numpy as jnp
from jax import lax
from jax.experimental import pallas as pl
from jax.experimental.pallas import tpu as pltpu
from jax.sharding import PartitionSpec as P

scale_logit = 8.0
shift_logit = -4.0
epsilon = 1e-06
f32 = jnp.float32
bf16 = jnp.bfloat16
VMEM = pl.BlockSpec(memory_space=pltpu.VMEM)
LONG = pl.CostEstimate(flops=10**10, bytes_accessed=10**7, transcendentals=0)


def normalize(raw):
    values = raw.astype(f32)
    inverse = lax.rsqrt(jnp.sum(values * values, axis=-1, keepdims=True) + epsilon)
    return (values * inverse, inverse)


def back_norm(unit, inverse, grad):
    inner = jnp.sum(unit * grad, axis=-1, keepdims=True)
    return inverse * (grad - unit * inner)


def pair_coeff(logit, same):
    label = jnp.where(same, 1.0, -1.0).astype(f32)
    return (-scale_logit * label * jax.nn.sigmoid(-label * logit)).astype(bf16)


def core_swap(block):
    size = lax.axis_size("img")
    return lax.ppermute(block, "img", [(i, i ^ 1) for i in range(size)])


def chip_swap(block, distance):
    n_img, n_txt = lax.axis_size("img"), lax.axis_size("txt")
    pairs = []
    for img in range(n_img):
        for txt in range(n_txt):
            if img % 2 == 0 and distance < n_img // 2:
                pairs.append((img * n_txt + txt, (img ^ (2 * distance)) * n_txt + txt))
            if img % 2 == 1 and distance < n_txt:
                pairs.append((img * n_txt + txt, img * n_txt + (txt ^ distance)))
    return lax.ppermute(block, ("img", "txt"), pairs)


def is_even():
    return lax.axis_index("img") % 2 == 0


def call(kernel, outs, args, cost=None):
    sizes = [a.size * a.dtype.itemsize for a in list(args) + list(outs)]
    return pl.pallas_call(
        kernel,
        out_shape=outs,
        in_specs=[VMEM] * len(args),
        out_specs=[VMEM] * len(outs),
        cost_estimate=cost,
        compiler_params=pltpu.CompilerParams(
            vmem_limit_bytes=min(48 * 2**20, 8 * 2**20 + 6 * sum(sizes))
        ),
    )(*args)


def sides_kernel(own_ref, txt_ref, img_ref, mine_ref, other_ref, raw_ref):
    rows = txt_ref.shape[0]
    even = is_even()
    own = normalize(own_ref[...])[0].astype(bf16)
    own_txt, own_img = own[:rows], own[rows:]
    far_txt = normalize(txt_ref[...])[0].astype(bf16)
    far_img = normalize(img_ref[...])[0].astype(bf16)
    mine_ref[:rows, :] = jnp.where(even, own_txt, far_img)
    mine_ref[rows:, :] = jnp.where(even, far_txt, own_img)
    other_ref[:rows, :] = jnp.where(even, own_img, far_txt)
    other_ref[rows:, :] = jnp.where(even, far_img, own_txt)
    raw_ref[:rows, :] = jnp.where(even, own_ref[:rows, :], img_ref[...])
    raw_ref[rows:, :] = jnp.where(even, txt_ref[...], own_ref[rows:, :])


def row_ids(rows, ids, far_ids, count):
    me_img = lax.axis_index("img")
    me_txt = lax.axis_index("txt")
    n_img = lax.axis_size("img")
    row = lax.broadcasted_iota(jnp.int32, (count, 1), 0)
    block, core, j = row // (2 * rows), row // rows % 2, row % rows
    chip = jnp.where(block == 0, 0, count // (2 * rows) - block)
    txt_ids = (me_txt * n_img + (((me_img // 2) ^ chip) * 2 + core)) * rows + j
    source = (me_txt ^ chip) * rows + j
    here = lax.broadcasted_iota(jnp.int32, (count, ids.shape[1]), 1) == source
    per_core = jnp.where(core == me_img % 2, ids, far_ids)
    img_ids = jnp.sum(jnp.where(here, per_core, 0), axis=1, keepdims=True)
    return txt_ids, img_ids


def ids_kernel(ids_ref, far_ids_ref, piece_ref, mine_ids_ref, other_ids_ref, out_ref):
    height = piece_ref.shape[0]
    count = mine_ids_ref.shape[0]
    even = is_even()
    txt_ids, img_ids = row_ids(height // 2, ids_ref[...], far_ids_ref[...], count)
    mine_ids_ref[...] = jnp.where(even, txt_ids, img_ids)
    other_ids = jnp.where(even, img_ids, txt_ids)
    diagonal = lax.broadcasted_iota(jnp.int32, (count, count), 0) == lax.broadcasted_iota(
        jnp.int32, (count, count), 1
    )
    other_ids_ref[...] = jnp.sum(jnp.where(diagonal, other_ids, 0), axis=0, keepdims=True)
    out_ref[...] = piece_ref[...]


def part_of(mine_refs, other_refs, mine_ids_ref, other_ids):
    mine = jnp.concatenate([ref[...] for ref in mine_refs], axis=0)
    other = jnp.concatenate([ref[...] for ref in other_refs], axis=0)
    scores = lax.dot_general(
        mine, other, (((1,), (1,)), ((), ())), preferred_element_type=f32
    )
    same = mine_ids_ref[...] == other_ids
    coeff = pair_coeff(scale_logit * scores + shift_logit, same)
    return jnp.dot(coeff, other, preferred_element_type=f32)


def most_kernel(blocks, mine_ids_ref, other_ids_ref, *refs):
    mine_refs, other_refs, part_ref = refs[:blocks], refs[blocks:-1], refs[-1]
    width = (blocks - 1) * mine_refs[0].shape[0]
    part_ref[...] = part_of(mine_refs, other_refs, mine_ids_ref, other_ids_ref[:, :width])


def rest_kernel(blocks, mine_ids_ref, other_ids_ref, part_ref, *refs):
    mine_refs, last_ref, (own_ref, *send_refs) = refs[:blocks], refs[blocks], refs[blocks + 1:]
    height = own_ref.shape[0]
    start = (blocks - 1) * height
    part = part_ref[...] + part_of(
        mine_refs, [last_ref], mine_ids_ref, other_ids_ref[:, start:]
    )
    own_ref[...] = part[:height]
    for k, ref in enumerate(send_refs):
        ref[...] = part[(k + 1) * height:(k + 2) * height].astype(bf16)


def grad_kernel(raw_ref, own_ref, *refs):
    *got_refs, keep_ref, send_ref = refs
    rows = keep_ref.shape[0]
    total = own_ref[...]
    for ref in got_refs:
        total = total + ref[...].astype(f32)
    grad = back_norm(*normalize(raw_ref[...]), total)
    even = is_even()
    keep_ref[...] = jnp.where(even, grad[:rows], grad[rows:])
    send_ref[...] = jnp.where(even, grad[rows:], grad[:rows])


def out_kernel(keep_ref, got_ref, img_ref, txt_ref):
    even = is_even()
    keep, got = keep_ref[...], got_ref[...]
    img_ref[...] = jnp.where(even, got, keep)
    txt_ref[...] = jnp.where(even, keep, got)


def local(image_embeds, text_embeds, pair_ids):
    rows, width = image_embeds.shape
    blocks = max(lax.axis_size("img") // 2, lax.axis_size("txt"))
    pair = jax.ShapeDtypeStruct((2 * rows, width), bf16)
    total = jax.ShapeDtypeStruct((2 * rows, width), f32)
    single = jax.ShapeDtypeStruct((rows, width), f32)
    ids = pair_ids.reshape(1, -1)
    far_txt = core_swap(text_embeds)
    far_img = core_swap(image_embeds)
    far_ids = core_swap(ids)
    near = jnp.concatenate([text_embeds, image_embeds])
    mine, other, raw = call(sides_kernel, [pair] * 3, [near, far_txt, far_img])
    order = list(range(blocks - 1, 0, -1))
    mine = [mine] + [chip_swap(mine, k) for k in order]
    count = blocks * 2 * rows
    mine_ids, other_ids, first = call(
        ids_kernel,
        [
            jax.ShapeDtypeStruct((count, 1), jnp.int32),
            jax.ShapeDtypeStruct((1, count), jnp.int32),
            pair,
        ],
        [ids, far_ids, mine[1]],
    )
    other = [other] + [core_swap(block) for block in [first] + mine[2:]]
    part = jax.ShapeDtypeStruct((count, width), f32)
    (part,) = call(
        functools.partial(most_kernel, blocks),
        [part],
        [mine_ids, other_ids, *mine, *other[:-1]],
        cost=LONG,
    )
    own, *send = call(
        functools.partial(rest_kernel, blocks),
        [total] + [pair] * (blocks - 1),
        [mine_ids, other_ids, part, *mine, other[-1]],
    )
    got = [chip_swap(block, k) for k, block in zip(order, send)]
    keep, send = call(grad_kernel, [single] * 2, [raw, own, *got])
    return tuple(call(out_kernel, [single] * 2, [keep, core_swap(send)]))


def solution(mesh):
    return jax.shard_map(
        local,
        mesh=mesh,
        in_specs=(P(("img", "txt"), None), P(("txt", "img"), None), P("img")),
        out_specs=(P(("img", "txt"), None), P(("txt", "img"), None)),
        check_vma=False,
    )
```

```python
import functools

import jax
import jax.numpy as jnp
from jax import lax
from jax.experimental import pallas as pl
from jax.experimental.pallas import tpu as pltpu
from jax.sharding import PartitionSpec as P

scale_logit = 8.0
shift_logit = -4.0
epsilon = 1e-06
f32 = jnp.float32
bf16 = jnp.bfloat16
VMEM = pl.BlockSpec(memory_space=pltpu.VMEM)
LONG = pl.CostEstimate(flops=10**10, bytes_accessed=10**7, transcendentals=0)


def normalize(raw):
    values = raw.astype(f32)
    inverse = lax.rsqrt(jnp.sum(values * values, axis=-1, keepdims=True) + epsilon)
    return (values * inverse, inverse)


def back_norm(unit, inverse, grad):
    inner = jnp.sum(unit * grad, axis=-1, keepdims=True)
    return inverse * (grad - unit * inner)


def pair_coeff(logit, same):
    label = jnp.where(same, 1.0, -1.0).astype(f32)
    return (-scale_logit * label * jax.nn.sigmoid(-label * logit)).astype(bf16)


def core_swap(block):
    size = lax.axis_size("img")
    return lax.ppermute(block, "img", [(i, i ^ 1) for i in range(size)])


def chip_swap(block, distance, cross=0):
    n_img, n_txt = lax.axis_size("img"), lax.axis_size("txt")
    pairs = []
    for img in range(n_img):
        for txt in range(n_txt):
            if img % 2 == 0 and distance < n_img // 2:
                pairs.append((img * n_txt + txt, (img ^ (2 * distance) ^ cross) * n_txt + txt))
            if img % 2 == 1 and distance < n_txt:
                pairs.append((img * n_txt + txt, (img ^ cross) * n_txt + (txt ^ distance)))
    return lax.ppermute(block, ("img", "txt"), pairs)


def is_even():
    return lax.axis_index("img") % 2 == 0


def call(kernel, outs, args, cost=None):
    sizes = [a.size * a.dtype.itemsize for a in list(args) + list(outs)]
    return pl.pallas_call(
        kernel,
        out_shape=outs,
        in_specs=[VMEM] * len(args),
        out_specs=[VMEM] * len(outs),
        cost_estimate=cost,
        compiler_params=pltpu.CompilerParams(
            vmem_limit_bytes=min(48 * 2**20, 8 * 2**20 + 6 * sum(sizes))
        ),
    )(*args)


def sides_kernel(own_ref, txt_ref, img_ref, mine_ref, other_ref):
    rows = txt_ref.shape[0]
    even = is_even()
    own = normalize(own_ref[...])[0].astype(bf16)
    own_txt, own_img = own[:rows], own[rows:]
    far_txt = normalize(txt_ref[...])[0].astype(bf16)
    far_img = normalize(img_ref[...])[0].astype(bf16)
    mine_ref[:rows, :] = jnp.where(even, own_txt, far_img)
    mine_ref[rows:, :] = jnp.where(even, far_txt, own_img)
    other_ref[:rows, :] = jnp.where(even, own_img, far_txt)
    other_ref[rows:, :] = jnp.where(even, far_img, own_txt)


def row_ids(rows, ids, far_ids, count):
    me_img = lax.axis_index("img")
    me_txt = lax.axis_index("txt")
    n_img = lax.axis_size("img")
    row = lax.broadcasted_iota(jnp.int32, (count, 1), 0)
    block, core, j = row // (2 * rows), row // rows % 2, row % rows
    chip = jnp.where(block == 0, 0, count // (2 * rows) - block)
    txt_ids = (me_txt * n_img + (((me_img // 2) ^ chip) * 2 + core)) * rows + j
    source = (me_txt ^ chip) * rows + j
    here = lax.broadcasted_iota(jnp.int32, (count, ids.shape[1]), 1) == source
    per_core = jnp.where(core == me_img % 2, ids, far_ids)
    img_ids = jnp.sum(jnp.where(here, per_core, 0), axis=1, keepdims=True)
    return txt_ids, img_ids


def ids_kernel(ids_ref, far_ids_ref, piece_ref, mine_ids_ref, other_ids_ref, out_ref):
    height = piece_ref.shape[0]
    count = mine_ids_ref.shape[0]
    even = is_even()
    txt_ids, img_ids = row_ids(height // 2, ids_ref[...], far_ids_ref[...], count)
    mine_ids_ref[...] = jnp.where(even, txt_ids, img_ids)
    other_ids = jnp.where(even, img_ids, txt_ids)
    diagonal = lax.broadcasted_iota(jnp.int32, (count, count), 0) == lax.broadcasted_iota(
        jnp.int32, (count, count), 1
    )
    other_ids_ref[...] = jnp.sum(jnp.where(diagonal, other_ids, 0), axis=0, keepdims=True)
    out_ref[...] = piece_ref[...]


def part_of(mine_refs, other_refs, mine_ids_ref, other_ids):
    mine = jnp.concatenate([ref[...] for ref in mine_refs], axis=0)
    other = jnp.concatenate([ref[...] for ref in other_refs], axis=0)
    scores = lax.dot_general(
        mine, other, (((1,), (1,)), ((), ())), preferred_element_type=f32
    )
    same = mine_ids_ref[...] == other_ids
    coeff = pair_coeff(scale_logit * scores + shift_logit, same)
    return jnp.dot(coeff, other, preferred_element_type=f32)


def most_kernel(blocks, mine_ids_ref, other_ids_ref, *refs):
    mine_refs, other_refs, part_ref = refs[:blocks], refs[blocks:-1], refs[-1]
    width = (blocks - 1) * mine_refs[0].shape[0]
    part_ref[...] = part_of(mine_refs, other_refs, mine_ids_ref, other_ids_ref[:, :width])


def rest_kernel(blocks, split, mine_ids_ref, other_ids_ref, part_ref, *refs):
    mine_refs, last_ref = refs[:blocks], refs[blocks]
    own_ref, same_ref, cross_ref, *send_refs = refs[blocks + 1:]
    height = own_ref.shape[0]
    rows = height // 2
    start = (blocks - 1) * height
    part = part_ref[...] + part_of(
        mine_refs, [last_ref], mine_ids_ref, other_ids_ref[:, start:]
    )
    own_ref[...] = part[:height]
    whole = [k for k in range(1, blocks) if k != split]
    for k, ref in zip(whole, send_refs):
        ref[...] = part[k * height:(k + 1) * height].astype(bf16)
    block = part[split * height:(split + 1) * height].astype(bf16)
    even = is_even()
    same_ref[...] = jnp.where(even, block[:rows], block[rows:])
    cross_ref[...] = jnp.where(even, block[rows:], block[:rows])


def sum_kernel(own_ref, *refs):
    *got_refs, keep_ref, send_ref = refs
    rows = keep_ref.shape[0]
    total = own_ref[...]
    for ref in got_refs:
        total = total + ref[...].astype(f32)
    even = is_even()
    keep_ref[...] = jnp.where(even, total[:rows], total[rows:])
    send_ref[...] = jnp.where(even, total[rows:], total[:rows])


def keep_kernel(raw_ref, keep_ref, same_ref, cross_ref, grad_ref, rest_ref):
    rows = keep_ref.shape[0]
    raw = jnp.where(is_even(), raw_ref[:rows, :], raw_ref[rows:, :])
    grad_ref[...] = back_norm(*normalize(raw), keep_ref[...] + same_ref[...].astype(f32))
    rest_ref[...] = cross_ref[...].astype(f32)


def out_kernel(raw_ref, grad_ref, rest_ref, got_ref, img_ref, txt_ref):
    rows = grad_ref.shape[0]
    even = is_even()
    raw = jnp.where(even, raw_ref[rows:, :], raw_ref[:rows, :])
    keep = grad_ref[...]
    got = back_norm(*normalize(raw), got_ref[...] + rest_ref[...])
    txt_ref[...] = jnp.where(even, keep, got)
    img_ref[...] = jnp.where(even, got, keep)


def local(image_embeds, text_embeds, pair_ids):
    rows, width = image_embeds.shape
    blocks = max(lax.axis_size("img") // 2, lax.axis_size("txt"))
    pair = jax.ShapeDtypeStruct((2 * rows, width), bf16)
    total = jax.ShapeDtypeStruct((2 * rows, width), f32)
    piece = jax.ShapeDtypeStruct((rows, width), bf16)
    single = jax.ShapeDtypeStruct((rows, width), f32)
    ids = pair_ids.reshape(1, -1)
    far_txt = core_swap(text_embeds)
    far_img = core_swap(image_embeds)
    far_ids = core_swap(ids)
    near = jnp.concatenate([text_embeds, image_embeds])
    mine, other = call(sides_kernel, [pair] * 2, [near, far_txt, far_img])
    order = list(range(blocks - 1, 0, -1))
    mine = [mine] + [chip_swap(mine, k) for k in order]
    count = blocks * 2 * rows
    mine_ids, other_ids, first = call(
        ids_kernel,
        [
            jax.ShapeDtypeStruct((count, 1), jnp.int32),
            jax.ShapeDtypeStruct((1, count), jnp.int32),
            pair,
        ],
        [ids, far_ids, mine[1]],
    )
    other = [other] + [core_swap(block) for block in [first] + mine[2:]]
    part = jax.ShapeDtypeStruct((count, width), f32)
    (part,) = call(
        functools.partial(most_kernel, blocks),
        [part],
        [mine_ids, other_ids, *mine, *other[:-1]],
        cost=LONG,
    )
    split = min(2, blocks - 1)
    own, same, cross, *send = call(
        functools.partial(rest_kernel, blocks, split),
        [total] + [piece] * 2 + [pair] * (blocks - 2),
        [mine_ids, other_ids, part, *mine, other[-1]],
    )
    far = order.pop(split - 1)
    got = [chip_swap(block, k) for k, block in zip(order, send)]
    same = chip_swap(same, far)
    cross = chip_swap(cross, far, cross=1)
    keep, send = call(sum_kernel, [single] * 2, [own, *got])
    got = core_swap(send)
    grad, rest = call(keep_kernel, [single] * 2, [near, keep, same, cross], cost=LONG)
    return tuple(call(out_kernel, [single] * 2, [near, grad, rest, got]))


def solution(mesh):
    return jax.shard_map(
        local,
        mesh=mesh,
        in_specs=(P(("img", "txt"), None), P(("txt", "img"), None), P("img")),
        out_specs=(P(("img", "txt"), None), P(("txt", "img"), None)),
        check_vma=False,
    )
```

```python
import functools

import jax
import jax.numpy as jnp
from jax import lax
from jax.experimental import pallas as pl
from jax.experimental.pallas import tpu as pltpu
from jax.sharding import PartitionSpec as P

scale_logit = 8.0
shift_logit = -4.0
epsilon = 1e-06
f32 = jnp.float32
bf16 = jnp.bfloat16
VMEM = pl.BlockSpec(memory_space=pltpu.VMEM)
LONG = pl.CostEstimate(flops=10**10, bytes_accessed=10**7, transcendentals=0)


def normalize(raw):
    values = raw.astype(f32)
    inverse = lax.rsqrt(jnp.sum(values * values, axis=-1, keepdims=True) + epsilon)
    return (values * inverse, inverse)


def back_norm(unit, inverse, grad):
    inner = jnp.sum(unit * grad, axis=-1, keepdims=True)
    return inverse * (grad - unit * inner)


def pair_coeff(logit, same):
    label = jnp.where(same, 1.0, -1.0).astype(f32)
    return (-scale_logit * label * jax.nn.sigmoid(-label * logit)).astype(bf16)


def core_swap(block):
    size = lax.axis_size("img")
    return lax.ppermute(block, "img", [(i, i ^ 1) for i in range(size)])


def chip_swap(block, distance, cross=0):
    n_img, n_txt = lax.axis_size("img"), lax.axis_size("txt")
    pairs = []
    for img in range(n_img):
        for txt in range(n_txt):
            if img % 2 == 0 and distance < n_img // 2:
                pairs.append((img * n_txt + txt, (img ^ (2 * distance) ^ cross) * n_txt + txt))
            if img % 2 == 1 and distance < n_txt:
                pairs.append((img * n_txt + txt, (img ^ cross) * n_txt + (txt ^ distance)))
    return lax.ppermute(block, ("img", "txt"), pairs)


def is_even():
    return lax.axis_index("img") % 2 == 0


def call(kernel, outs, args, cost=None):
    sizes = [a.size * a.dtype.itemsize for a in list(args) + list(outs)]
    return pl.pallas_call(
        kernel,
        out_shape=outs,
        in_specs=[VMEM] * len(args),
        out_specs=[VMEM] * len(outs),
        cost_estimate=cost,
        compiler_params=pltpu.CompilerParams(
            vmem_limit_bytes=min(48 * 2**20, 8 * 2**20 + 6 * sum(sizes))
        ),
    )(*args)


def sides_kernel(own_ref, txt_ref, img_ref, mine_ref, other_ref):
    rows = txt_ref.shape[0]
    even = is_even()
    own = normalize(own_ref[...])[0].astype(bf16)
    own_txt, own_img = own[:rows], own[rows:]
    far_txt = normalize(txt_ref[...])[0].astype(bf16)
    far_img = normalize(img_ref[...])[0].astype(bf16)
    mine_ref[:rows, :] = jnp.where(even, own_txt, far_img)
    mine_ref[rows:, :] = jnp.where(even, far_txt, own_img)
    other_ref[:rows, :] = jnp.where(even, own_img, far_txt)
    other_ref[rows:, :] = jnp.where(even, far_img, own_txt)


def row_ids(rows, ids, far_ids, count):
    me_img = lax.axis_index("img")
    me_txt = lax.axis_index("txt")
    n_img = lax.axis_size("img")
    row = lax.broadcasted_iota(jnp.int32, (count, 1), 0)
    block, core, j = row // (2 * rows), row // rows % 2, row % rows
    chip = jnp.where(block == 0, 0, count // (2 * rows) - block)
    txt_ids = (me_txt * n_img + (((me_img // 2) ^ chip) * 2 + core)) * rows + j
    source = (me_txt ^ chip) * rows + j
    here = lax.broadcasted_iota(jnp.int32, (count, ids.shape[1]), 1) == source
    per_core = jnp.where(core == me_img % 2, ids, far_ids)
    img_ids = jnp.sum(jnp.where(here, per_core, 0), axis=1, keepdims=True)
    return txt_ids, img_ids


def side_ids(rows, ids, far_ids, count):
    even = is_even()
    txt_ids, img_ids = row_ids(rows, ids, far_ids, count)
    other_ids = jnp.where(even, img_ids, txt_ids)
    diagonal = lax.broadcasted_iota(jnp.int32, (count, count), 0) == lax.broadcasted_iota(
        jnp.int32, (count, count), 1
    )
    other_ids = jnp.sum(jnp.where(diagonal, other_ids, 0), axis=0, keepdims=True)
    return jnp.where(even, txt_ids, img_ids), other_ids


def part_of(mine_refs, other_refs, mine_ids, other_ids):
    mine = jnp.concatenate([ref[...] for ref in mine_refs], axis=0)
    other = jnp.concatenate([ref[...] for ref in other_refs], axis=0)
    scores = lax.dot_general(
        mine, other, (((1,), (1,)), ((), ())), preferred_element_type=f32
    )
    same = mine_ids == other_ids
    coeff = pair_coeff(scale_logit * scores + shift_logit, same)
    return jnp.dot(coeff, other, preferred_element_type=f32)


def most_kernel(blocks, ids_ref, far_ids_ref, *refs):
    mine_refs, other_refs = refs[:blocks], refs[blocks:-3]
    part_ref, mine_ids_ref, other_ids_ref = refs[-3:]
    height = mine_refs[0].shape[0]
    mine_ids, other_ids = side_ids(
        height // 2, ids_ref[...], far_ids_ref[...], blocks * height
    )
    mine_ids_ref[...] = mine_ids
    other_ids_ref[...] = other_ids
    width = (blocks - 1) * height
    part_ref[...] = part_of(mine_refs, other_refs, mine_ids, other_ids[:, :width])


def rest_kernel(blocks, split, mine_ids_ref, other_ids_ref, part_ref, *refs):
    mine_refs, last_ref = refs[:blocks], refs[blocks]
    own_ref, same_ref, cross_ref, *send_refs = refs[blocks + 1:]
    height = own_ref.shape[0]
    rows = height // 2
    start = (blocks - 1) * height
    part = part_ref[...] + part_of(
        mine_refs, [last_ref], mine_ids_ref[...], other_ids_ref[:, start:]
    )
    own_ref[...] = part[:height]
    whole = [k for k in range(1, blocks) if k != split]
    for k, ref in zip(whole, send_refs):
        ref[...] = part[k * height:(k + 1) * height].astype(bf16)
    block = part[split * height:(split + 1) * height].astype(bf16)
    even = is_even()
    same_ref[...] = jnp.where(even, block[:rows], block[rows:])
    cross_ref[...] = jnp.where(even, block[rows:], block[:rows])


def sum_kernel(own_ref, *refs):
    *got_refs, keep_ref, send_ref = refs
    rows = keep_ref.shape[0]
    total = own_ref[...]
    for ref in got_refs:
        total = total + ref[...].astype(f32)
    even = is_even()
    keep_ref[...] = jnp.where(even, total[:rows], total[rows:])
    send_ref[...] = jnp.where(even, total[rows:], total[:rows])


def keep_kernel(raw_ref, keep_ref, same_ref, cross_ref, grad_ref, rest_ref):
    rows = keep_ref.shape[0]
    raw = jnp.where(is_even(), raw_ref[:rows, :], raw_ref[rows:2 * rows, :])
    grad_ref[...] = back_norm(*normalize(raw), keep_ref[...] + same_ref[...].astype(f32))
    rest_ref[...] = cross_ref[...].astype(f32)


def out_kernel(raw_ref, grad_ref, rest_ref, got_ref, img_ref, txt_ref):
    rows = grad_ref.shape[0]
    even = is_even()
    raw = jnp.where(even, raw_ref[rows:2 * rows, :], raw_ref[:rows, :])
    keep = grad_ref[...]
    got = back_norm(*normalize(raw), got_ref[...] + rest_ref[...])
    txt_ref[...] = jnp.where(even, keep, got)
    img_ref[...] = jnp.where(even, got, keep)


def local(image_embeds, text_embeds, pair_ids):
    rows, width = image_embeds.shape
    blocks = max(lax.axis_size("img") // 2, lax.axis_size("txt"))
    pair = jax.ShapeDtypeStruct((2 * rows, width), bf16)
    total = jax.ShapeDtypeStruct((2 * rows, width), f32)
    piece = jax.ShapeDtypeStruct((rows, width), bf16)
    single = jax.ShapeDtypeStruct((rows, width), f32)
    ids = pair_ids.reshape(1, -1)
    far_txt = core_swap(text_embeds)
    far_img = core_swap(image_embeds)
    far_ids = core_swap(ids)
    near = jnp.concatenate([text_embeds, image_embeds])
    mine, other = call(sides_kernel, [pair] * 2, [near, far_txt, far_img])
    order = list(range(blocks - 1, 0, -1))
    mine = [mine] + [chip_swap(mine, k) for k in order]
    other = [other] + [core_swap(block) for block in mine[1:]]
    count = blocks * 2 * rows
    part, mine_ids, other_ids = call(
        functools.partial(most_kernel, blocks),
        [
            jax.ShapeDtypeStruct((count, width), f32),
            jax.ShapeDtypeStruct((count, 1), jnp.int32),
            jax.ShapeDtypeStruct((1, count), jnp.int32),
        ],
        [ids, far_ids, *mine, *other[:-1]],
        cost=LONG,
    )
    split = min(2, blocks - 1)
    own, same, cross, *send = call(
        functools.partial(rest_kernel, blocks, split),
        [total] + [piece] * 2 + [pair] * (blocks - 2),
        [mine_ids, other_ids, part, *mine, other[-1]],
    )
    far = order.pop(split - 1)
    got = [chip_swap(block, k) for k, block in zip(order, send)]
    same = chip_swap(same, far)
    cross = chip_swap(cross, far, cross=1)
    keep, send = call(sum_kernel, [single] * 2, [own, *got])
    got = core_swap(send)
    grad, rest = call(keep_kernel, [single] * 2, [near, keep, same, cross], cost=LONG)
    return tuple(call(out_kernel, [single] * 2, [near, grad, rest, got]))


def solution(mesh):
    return jax.shard_map(
        local,
        mesh=mesh,
        in_specs=(P(("img", "txt"), None), P(("txt", "img"), None), P("img")),
        out_specs=(P(("img", "txt"), None), P(("txt", "img"), None)),
        check_vma=False,
    )
```

```python
import functools

import jax
import jax.numpy as jnp
from jax import lax
from jax.experimental import pallas as pl
from jax.experimental.pallas import tpu as pltpu
from jax.sharding import PartitionSpec as P

scale_logit = 8.0
shift_logit = -4.0
epsilon = 1e-06
f32 = jnp.float32
bf16 = jnp.bfloat16
VMEM = pl.BlockSpec(memory_space=pltpu.VMEM)
LONG = pl.CostEstimate(flops=10**10, bytes_accessed=10**7, transcendentals=0)
SHORT = pl.CostEstimate(flops=2 * 10**8, bytes_accessed=10**5, transcendentals=0)


def normalize(raw):
    values = raw.astype(f32)
    inverse = lax.rsqrt(jnp.sum(values * values, axis=-1, keepdims=True) + epsilon)
    return (values * inverse, inverse)


def back_norm(unit, inverse, grad):
    inner = jnp.sum(unit * grad, axis=-1, keepdims=True)
    return inverse * (grad - unit * inner)


def pair_coeff(logit, same):
    label = jnp.where(same, 1.0, -1.0).astype(f32)
    return (-scale_logit * label * jax.nn.sigmoid(-label * logit)).astype(bf16)


def core_swap(block):
    size = lax.axis_size("img")
    return lax.ppermute(block, "img", [(i, i ^ 1) for i in range(size)])


def chip_swap(block, distance, cross=0):
    n_img, n_txt = lax.axis_size("img"), lax.axis_size("txt")
    pairs = []
    for img in range(n_img):
        for txt in range(n_txt):
            if img % 2 == 0 and distance < n_img // 2:
                pairs.append((img * n_txt + txt, (img ^ (2 * distance) ^ cross) * n_txt + txt))
            if img % 2 == 1 and distance < n_txt:
                pairs.append((img * n_txt + txt, (img ^ cross) * n_txt + (txt ^ distance)))
    return lax.ppermute(block, ("img", "txt"), pairs)


def is_even():
    return lax.axis_index("img") % 2 == 0


def call(kernel, outs, args, cost=None):
    sizes = [a.size * a.dtype.itemsize for a in list(args) + list(outs)]
    return pl.pallas_call(
        kernel,
        out_shape=outs,
        in_specs=[VMEM] * len(args),
        out_specs=[VMEM] * len(outs),
        cost_estimate=cost,
        compiler_params=pltpu.CompilerParams(
            vmem_limit_bytes=min(48 * 2**20, 8 * 2**20 + 6 * sum(sizes))
        ),
    )(*args)


def sides_kernel(own_ref, txt_ref, img_ref, mine_ref, other_ref):
    rows = txt_ref.shape[0]
    even = is_even()
    own = normalize(own_ref[...])[0].astype(bf16)
    own_txt, own_img = own[:rows], own[rows:]
    far_txt = normalize(txt_ref[...])[0].astype(bf16)
    far_img = normalize(img_ref[...])[0].astype(bf16)
    mine_ref[:rows, :] = jnp.where(even, own_txt, far_img)
    mine_ref[rows:, :] = jnp.where(even, far_txt, own_img)
    other_ref[:rows, :] = jnp.where(even, own_img, far_txt)
    other_ref[rows:, :] = jnp.where(even, far_img, own_txt)


def row_ids(rows, ids, far_ids, count):
    me_img = lax.axis_index("img")
    me_txt = lax.axis_index("txt")
    n_img = lax.axis_size("img")
    row = lax.broadcasted_iota(jnp.int32, (count, 1), 0)
    block, core, j = row // (2 * rows), row // rows % 2, row % rows
    chip = jnp.where(block == 0, 0, count // (2 * rows) - block)
    txt_ids = (me_txt * n_img + (((me_img // 2) ^ chip) * 2 + core)) * rows + j
    source = (me_txt ^ chip) * rows + j
    here = lax.broadcasted_iota(jnp.int32, (count, ids.shape[1]), 1) == source
    per_core = jnp.where(core == me_img % 2, ids, far_ids)
    img_ids = jnp.sum(jnp.where(here, per_core, 0), axis=1, keepdims=True)
    return txt_ids, img_ids


def side_ids(rows, ids, far_ids, count):
    even = is_even()
    txt_ids, img_ids = row_ids(rows, ids, far_ids, count)
    other_ids = jnp.where(even, img_ids, txt_ids)
    diagonal = lax.broadcasted_iota(jnp.int32, (count, count), 0) == lax.broadcasted_iota(
        jnp.int32, (count, count), 1
    )
    other_ids = jnp.sum(jnp.where(diagonal, other_ids, 0), axis=0, keepdims=True)
    return jnp.where(even, txt_ids, img_ids), other_ids


def scores_of(mine_refs, other_refs):
    mine = jnp.concatenate([ref[...] for ref in mine_refs], axis=0)
    other = jnp.concatenate([ref[...] for ref in other_refs], axis=0)
    return lax.dot_general(mine, other, (((1,), (1,)), ((), ())), preferred_element_type=f32)


def most_kernel(blocks, *refs):
    refs[-1][...] = scores_of(refs[:blocks], refs[blocks:-1])


def rest_kernel(blocks, split, ids_ref, far_ids_ref, most_ref, *refs):
    mine_refs, other_refs = refs[:blocks], refs[blocks:2 * blocks]
    own_ref, same_ref, cross_ref, *send_refs = refs[2 * blocks:]
    height = own_ref.shape[0]
    rows = height // 2
    mine_ids, other_ids = side_ids(rows, ids_ref[...], far_ids_ref[...], blocks * height)
    scores = jnp.concatenate([most_ref[...], scores_of(mine_refs, other_refs[-1:])], axis=1)
    coeff = pair_coeff(scale_logit * scores + shift_logit, mine_ids == other_ids)
    other = jnp.concatenate([ref[...] for ref in other_refs], axis=0)
    part = jnp.dot(coeff, other, preferred_element_type=f32)
    own_ref[...] = part[:height]
    whole = [k for k in range(1, blocks) if k != split]
    for k, ref in zip(whole, send_refs):
        ref[...] = part[k * height:(k + 1) * height].astype(bf16)
    block = part[split * height:(split + 1) * height].astype(bf16)
    even = is_even()
    same_ref[...] = jnp.where(even, block[:rows], block[rows:])
    cross_ref[...] = jnp.where(even, block[rows:], block[:rows])


def sum_kernel(own_ref, *refs):
    *got_refs, keep_ref, send_ref = refs
    rows = keep_ref.shape[0]
    total = own_ref[...]
    for ref in got_refs:
        total = total + ref[...].astype(f32)
    even = is_even()
    keep_ref[...] = jnp.where(even, total[:rows], total[rows:])
    send_ref[...] = jnp.where(even, total[rows:], total[:rows])


def keep_kernel(raw_ref, keep_ref, same_ref, grad_ref, unit_ref, inverse_ref):
    rows = keep_ref.shape[0]
    even = is_even()
    unit, inverse = normalize(raw_ref[...])
    grad_ref[...] = back_norm(
        jnp.where(even, unit[:rows], unit[rows:]),
        jnp.where(even, inverse[:rows], inverse[rows:]),
        keep_ref[...] + same_ref[...].astype(f32),
    )
    unit_ref[...] = jnp.where(even, unit[rows:], unit[:rows])
    inverse_ref[...] = jnp.where(even, inverse[rows:], inverse[:rows])


def out_kernel(grad_ref, unit_ref, inverse_ref, cross_ref, got_ref, img_ref, txt_ref):
    even = is_even()
    total = got_ref[...] + cross_ref[...].astype(f32)
    keep = grad_ref[...]
    got = back_norm(unit_ref[...], inverse_ref[...], total)
    txt_ref[...] = jnp.where(even, keep, got)
    img_ref[...] = jnp.where(even, got, keep)


def local(image_embeds, text_embeds, pair_ids):
    rows, width = image_embeds.shape
    blocks = max(lax.axis_size("img") // 2, lax.axis_size("txt"))
    pair = jax.ShapeDtypeStruct((2 * rows, width), bf16)
    total = jax.ShapeDtypeStruct((2 * rows, width), f32)
    piece = jax.ShapeDtypeStruct((rows, width), bf16)
    single = jax.ShapeDtypeStruct((rows, width), f32)
    ids = pair_ids.reshape(1, -1)
    far_txt = core_swap(text_embeds)
    far_img = core_swap(image_embeds)
    near = jnp.concatenate([text_embeds, image_embeds])
    mine, other = call(sides_kernel, [pair] * 2, [near, far_txt, far_img])
    order = list(range(blocks - 1, 0, -1))
    mine = [mine] + [chip_swap(mine, k) for k in order]
    other = [other] + [core_swap(block) for block in mine[1:]]
    count = blocks * 2 * rows
    (most,) = call(
        functools.partial(most_kernel, blocks),
        [jax.ShapeDtypeStruct((count, count - 2 * rows), f32)],
        [*mine, *other[:-1]],
        cost=SHORT,
    )
    split = min(2, blocks - 1)
    own, same, cross, *send = call(
        functools.partial(rest_kernel, blocks, split),
        [total] + [piece] * 2 + [pair] * (blocks - 2),
        [ids, core_swap(ids), most, *mine, *other],
    )
    far = order.pop(split - 1)
    got = [chip_swap(block, k) for k, block in zip(order, send)]
    same = chip_swap(same, far)
    cross = chip_swap(cross, far, cross=1)
    keep, send = call(sum_kernel, [single] * 2, [own, *got])
    got = core_swap(send)
    column = jax.ShapeDtypeStruct((rows, 1), f32)
    kept = call(keep_kernel, [single, single, column], [near, keep, same], cost=LONG)
    return tuple(call(out_kernel, [single] * 2, [*kept, cross, got]))


def solution(mesh):
    return jax.shard_map(
        local,
        mesh=mesh,
        in_specs=(P(("img", "txt"), None), P(("txt", "img"), None), P("img")),
        out_specs=(P(("img", "txt"), None), P(("txt", "img"), None)),
        check_vma=False,
    )
```

```python
import functools

import jax
import jax.numpy as jnp
from jax import lax
from jax.experimental import pallas as pl
from jax.experimental.pallas import tpu as pltpu
from jax.sharding import PartitionSpec as P

scale_logit = 8.0
shift_logit = -4.0
epsilon = 1e-06
f32 = jnp.float32
bf16 = jnp.bfloat16
VMEM = pl.BlockSpec(memory_space=pltpu.VMEM)
LONG = pl.CostEstimate(flops=10**10, bytes_accessed=10**7, transcendentals=0)


def normalize(raw):
    values = raw.astype(f32)
    inverse = lax.rsqrt(jnp.sum(values * values, axis=-1, keepdims=True) + epsilon)
    return (values * inverse, inverse)


def back_norm(unit, inverse, grad):
    inner = jnp.sum(unit * grad, axis=-1, keepdims=True)
    return inverse * (grad - unit * inner)


def pair_coeff(logit, same):
    label = jnp.where(same, 1.0, -1.0).astype(f32)
    return (-scale_logit * label * jax.nn.sigmoid(-label * logit)).astype(bf16)


def core_swap(block):
    size = lax.axis_size("img")
    return lax.ppermute(block, "img", [(i, i ^ 1) for i in range(size)])


def chip_swap(block, distance, cross=0):
    n_img, n_txt = lax.axis_size("img"), lax.axis_size("txt")
    pairs = []
    for img in range(n_img):
        for txt in range(n_txt):
            if img % 2 == 0 and distance < n_img // 2:
                pairs.append((img * n_txt + txt, (img ^ (2 * distance) ^ cross) * n_txt + txt))
            if img % 2 == 1 and distance < n_txt:
                pairs.append((img * n_txt + txt, (img ^ cross) * n_txt + (txt ^ distance)))
    return lax.ppermute(block, ("img", "txt"), pairs)


def is_even():
    return lax.axis_index("img") % 2 == 0


def call(kernel, outs, args, cost=None):
    sizes = [a.size * a.dtype.itemsize for a in list(args) + list(outs)]
    return pl.pallas_call(
        kernel,
        out_shape=outs,
        in_specs=[VMEM] * len(args),
        out_specs=[VMEM] * len(outs),
        cost_estimate=cost,
        compiler_params=pltpu.CompilerParams(
            vmem_limit_bytes=min(48 * 2**20, 8 * 2**20 + 6 * sum(sizes))
        ),
    )(*args)


def sides_kernel(own_ref, txt_ref, img_ref, mine_ref, other_ref):
    rows = txt_ref.shape[0]
    even = is_even()
    own = normalize(own_ref[...])[0].astype(bf16)
    own_txt, own_img = own[:rows], own[rows:]
    far_txt = normalize(txt_ref[...])[0].astype(bf16)
    far_img = normalize(img_ref[...])[0].astype(bf16)
    mine_ref[:rows, :] = jnp.where(even, own_txt, far_img)
    mine_ref[rows:, :] = jnp.where(even, far_txt, own_img)
    other_ref[:rows, :] = jnp.where(even, own_img, far_txt)
    other_ref[rows:, :] = jnp.where(even, far_img, own_txt)


def pack_kernel(ids_ref, piece_ref, out_ref):
    height = piece_ref.shape[0]
    tile = out_ref.shape[0] - height
    count = ids_ref.shape[1]
    out_ref[:height, :] = piece_ref[...]
    ids = ids_ref[...]
    high = lax.broadcasted_iota(jnp.int32, (tile, count), 0) == 0
    out_ref[height:, :] = jnp.zeros((tile, out_ref.shape[1]), bf16)
    out_ref[height:, :count] = jnp.where(high, ids // 256, ids % 256).astype(f32).astype(bf16)


def row_ids(rows, ids, far_ids, count):
    me_img = lax.axis_index("img")
    me_txt = lax.axis_index("txt")
    n_img = lax.axis_size("img")
    row = lax.broadcasted_iota(jnp.int32, (count, 1), 0)
    block, core, j = row // (2 * rows), row // rows % 2, row % rows
    chip = jnp.where(block == 0, 0, count // (2 * rows) - block)
    txt_ids = (me_txt * n_img + (((me_img // 2) ^ chip) * 2 + core)) * rows + j
    source = (me_txt ^ chip) * rows + j
    here = lax.broadcasted_iota(jnp.int32, (count, ids.shape[1]), 1) == source
    per_core = jnp.where(core == me_img % 2, ids, far_ids)
    img_ids = jnp.sum(jnp.where(here, per_core, 0), axis=1, keepdims=True)
    return txt_ids, img_ids


def side_ids(rows, ids, far_ids, count):
    even = is_even()
    txt_ids, img_ids = row_ids(rows, ids, far_ids, count)
    other_ids = jnp.where(even, img_ids, txt_ids)
    diagonal = lax.broadcasted_iota(jnp.int32, (count, count), 0) == lax.broadcasted_iota(
        jnp.int32, (count, count), 1
    )
    other_ids = jnp.sum(jnp.where(diagonal, other_ids, 0), axis=0, keepdims=True)
    return jnp.where(even, txt_ids, img_ids), other_ids


def scores_of(mine_refs, other_refs):
    mine = jnp.concatenate([ref[...] for ref in mine_refs], axis=0)
    other = jnp.concatenate([ref[...] for ref in other_refs], axis=0)
    return lax.dot_general(mine, other, (((1,), (1,)), ((), ())), preferred_element_type=f32)


def most_kernel(blocks, *refs):
    refs[-1][...] = scores_of(refs[:blocks], refs[blocks:-1])


def rest_kernel(blocks, split, ids_ref, most_ref, *refs):
    mine_refs, (*other_refs, last_ref) = refs[:blocks], refs[blocks:2 * blocks]
    own_ref, same_ref, cross_ref, *send_refs = refs[2 * blocks:]
    height = own_ref.shape[0]
    rows = height // 2
    code = last_ref[height:, :ids_ref.shape[1]].astype(f32)
    far_ids = (code[0:1] * 256.0 + code[1:2]).astype(jnp.int32)
    mine_ids, other_ids = side_ids(rows, ids_ref[...], far_ids, blocks * height)
    other_refs = [*other_refs, last_ref.at[:height, :]]
    scores = jnp.concatenate([most_ref[...], scores_of(mine_refs, other_refs[-1:])], axis=1)
    coeff = pair_coeff(scale_logit * scores + shift_logit, mine_ids == other_ids)
    other = jnp.concatenate([ref[...] for ref in other_refs], axis=0)
    part = jnp.dot(coeff, other, preferred_element_type=f32)
    own_ref[...] = part[:height]
    whole = [k for k in range(1, blocks) if k != split]
    for k, ref in zip(whole, send_refs):
        ref[...] = part[k * height:(k + 1) * height].astype(bf16)
    block = part[split * height:(split + 1) * height].astype(bf16)
    even = is_even()
    same_ref[...] = jnp.where(even, block[:rows], block[rows:])
    cross_ref[...] = jnp.where(even, block[rows:], block[:rows])


def sum_kernel(own_ref, *refs):
    *got_refs, keep_ref, send_ref = refs
    rows = keep_ref.shape[0]
    total = own_ref[...]
    for ref in got_refs:
        total = total + ref[...].astype(f32)
    even = is_even()
    keep_ref[...] = jnp.where(even, total[:rows], total[rows:])
    send_ref[...] = jnp.where(even, total[rows:], total[:rows])


def keep_kernel(raw_ref, keep_ref, same_ref, grad_ref, unit_ref, inverse_ref):
    rows = keep_ref.shape[0]
    even = is_even()
    unit, inverse = normalize(raw_ref[...])
    grad_ref[...] = back_norm(
        jnp.where(even, unit[:rows], unit[rows:]),
        jnp.where(even, inverse[:rows], inverse[rows:]),
        keep_ref[...] + same_ref[...].astype(f32),
    )
    unit_ref[...] = jnp.where(even, unit[rows:], unit[:rows])
    inverse_ref[...] = jnp.where(even, inverse[rows:], inverse[:rows])


def out_kernel(grad_ref, unit_ref, inverse_ref, cross_ref, got_ref, img_ref, txt_ref):
    even = is_even()
    total = got_ref[...] + cross_ref[...].astype(f32)
    keep = grad_ref[...]
    got = back_norm(unit_ref[...], inverse_ref[...], total)
    txt_ref[...] = jnp.where(even, keep, got)
    img_ref[...] = jnp.where(even, got, keep)


def local(image_embeds, text_embeds, pair_ids):
    rows, width = image_embeds.shape
    blocks = max(lax.axis_size("img") // 2, lax.axis_size("txt"))
    pair = jax.ShapeDtypeStruct((2 * rows, width), bf16)
    total = jax.ShapeDtypeStruct((2 * rows, width), f32)
    piece = jax.ShapeDtypeStruct((rows, width), bf16)
    single = jax.ShapeDtypeStruct((rows, width), f32)
    ids = pair_ids.reshape(1, -1)
    far_txt = core_swap(text_embeds)
    far_img = core_swap(image_embeds)
    near = jnp.concatenate([text_embeds, image_embeds])
    mine, other = call(sides_kernel, [pair] * 2, [near, far_txt, far_img])
    order = list(range(blocks - 1, 0, -1))
    mine = [mine] + [chip_swap(mine, k) for k in order]
    packed = jax.ShapeDtypeStruct((3 * rows, width), bf16)
    (packed,) = call(pack_kernel, [packed], [ids, mine[-1]])
    other = [other] + [core_swap(block) for block in [*mine[1:-1], packed]]
    count = blocks * 2 * rows
    (most,) = call(
        functools.partial(most_kernel, blocks),
        [jax.ShapeDtypeStruct((count, count - 2 * rows), f32)],
        [*mine, *other[:-1]],
        cost=LONG,
    )
    split = min(2, blocks - 1)
    own, same, cross, *send = call(
        functools.partial(rest_kernel, blocks, split),
        [total] + [piece] * 2 + [pair] * (blocks - 2),
        [ids, most, *mine, *other],
    )
    far = order.pop(split - 1)
    got = [chip_swap(block, k) for k, block in zip(order, send)]
    same = chip_swap(same, far)
    cross = chip_swap(cross, far, cross=1)
    keep, send = call(sum_kernel, [single] * 2, [own, *got])
    got = core_swap(send)
    column = jax.ShapeDtypeStruct((rows, 1), f32)
    kept = call(keep_kernel, [single, single, column], [near, keep, same], cost=LONG)
    return tuple(call(out_kernel, [single] * 2, [*kept, cross, got]))


def solution(mesh):
    return jax.shard_map(
        local,
        mesh=mesh,
        in_specs=(P(("img", "txt"), None), P(("txt", "img"), None), P("img")),
        out_specs=(P(("img", "txt"), None), P(("txt", "img"), None)),
        check_vma=False,
    )
```

```python
import functools

import jax
import jax.numpy as jnp
from jax import lax
from jax.experimental import pallas as pl
from jax.experimental.pallas import tpu as pltpu
from jax.sharding import PartitionSpec as P

scale_logit = 8.0
shift_logit = -4.0
epsilon = 1e-06
LANES = 128
f32 = jnp.float32
bf16 = jnp.bfloat16
VMEM = pl.BlockSpec(memory_space=pltpu.VMEM)
LONG = pl.CostEstimate(flops=10**10, bytes_accessed=10**7, transcendentals=0)


def normalize(raw):
    values = raw.astype(f32)
    inverse = lax.rsqrt(jnp.sum(values * values, axis=-1, keepdims=True) + epsilon)
    return (values * inverse, inverse)


def back_norm(unit, inverse, grad):
    inner = jnp.sum(unit * grad, axis=-1, keepdims=True)
    return inverse * (grad - unit * inner)


def pair_coeff(logit, same):
    label = jnp.where(same, 1.0, -1.0).astype(f32)
    return (-scale_logit * label * jax.nn.sigmoid(-label * logit)).astype(bf16)


def core_swap(block):
    size = lax.axis_size("img")
    return lax.ppermute(block, "img", [(i, i ^ 1) for i in range(size)])


def chip_swap(block, distance, cross=0):
    n_img, n_txt = lax.axis_size("img"), lax.axis_size("txt")
    pairs = []
    for img in range(n_img):
        for txt in range(n_txt):
            if img % 2 == 0 and distance < n_img // 2:
                pairs.append((img * n_txt + txt, (img ^ (2 * distance) ^ cross) * n_txt + txt))
            if img % 2 == 1 and distance < n_txt:
                pairs.append((img * n_txt + txt, (img ^ cross) * n_txt + (txt ^ distance)))
    return lax.ppermute(block, ("img", "txt"), pairs)


def is_even():
    return lax.axis_index("img") % 2 == 0


def call(kernel, outs, args, cost=None):
    sizes = [a.size * a.dtype.itemsize for a in list(args) + list(outs)]
    return pl.pallas_call(
        kernel,
        out_shape=outs,
        in_specs=[VMEM] * len(args),
        out_specs=[VMEM] * len(outs),
        cost_estimate=cost,
        compiler_params=pltpu.CompilerParams(
            vmem_limit_bytes=min(48 * 2**20, 8 * 2**20 + 6 * sum(sizes))
        ),
    )(*args)


def sides_kernel(own_ref, txt_ref, img_ref, mine_ref, other_ref):
    rows = txt_ref.shape[0]
    even = is_even()
    own = normalize(own_ref[...])[0].astype(bf16)
    own_txt, own_img = own[:rows], own[rows:]
    far_txt = normalize(txt_ref[...])[0].astype(bf16)
    far_img = normalize(img_ref[...])[0].astype(bf16)
    mine_ref[:rows, :] = jnp.where(even, own_txt, far_img)
    mine_ref[rows:, :] = jnp.where(even, far_txt, own_img)
    other_ref[:rows, :] = jnp.where(even, own_img, far_txt)
    other_ref[rows:, :] = jnp.where(even, far_img, own_txt)


def pack_kernel(ids_ref, piece_ref, out_ref):
    height, width = piece_ref.shape
    tiles = width // LANES
    count = ids_ref.shape[1]
    for k in range(tiles):
        out_ref[k * height:(k + 1) * height, :] = piece_ref[:, k * LANES:(k + 1) * LANES]
    rest = out_ref.shape[0] - tiles * height
    row = lax.broadcasted_iota(jnp.int32, (rest, LANES), 0)
    code = jnp.zeros((rest, LANES), f32)
    for k in range(0, count, LANES):
        ids = ids_ref[:, k:k + LANES]
        if ids.shape[1] < LANES:
            ids = jnp.concatenate([ids, jnp.zeros((1, LANES - ids.shape[1]), ids.dtype)], axis=1)
        code = jnp.where(row == 2 * k // LANES, (ids // 256).astype(f32), code)
        code = jnp.where(row == 2 * k // LANES + 1, (ids % 256).astype(f32), code)
    out_ref[tiles * height:, :] = code.astype(bf16)


def unpack(ref, height, width, count):
    tiles = width // LANES
    piece = jnp.concatenate(
        [ref[k * height:(k + 1) * height, :] for k in range(tiles)], axis=1
    )
    code = ref[tiles * height:, :].astype(f32)
    ids = [code[k:k + 1] * 256.0 + code[k + 1:k + 2] for k in range(0, 2 * count // LANES or 2, 2)]
    ids = jnp.concatenate(ids, axis=1)[:, :count].astype(jnp.int32)
    return piece, ids


def row_ids(rows, ids, far_ids, count):
    me_img = lax.axis_index("img")
    me_txt = lax.axis_index("txt")
    n_img = lax.axis_size("img")
    row = lax.broadcasted_iota(jnp.int32, (count, 1), 0)
    block, core, j = row // (2 * rows), row // rows % 2, row % rows
    chip = jnp.where(block == 0, 0, count // (2 * rows) - block)
    txt_ids = (me_txt * n_img + (((me_img // 2) ^ chip) * 2 + core)) * rows + j
    source = (me_txt ^ chip) * rows + j
    here = lax.broadcasted_iota(jnp.int32, (count, ids.shape[1]), 1) == source
    per_core = jnp.where(core == me_img % 2, ids, far_ids)
    img_ids = jnp.sum(jnp.where(here, per_core, 0), axis=1, keepdims=True)
    return txt_ids, img_ids


def side_ids(rows, ids, far_ids, count):
    even = is_even()
    txt_ids, img_ids = row_ids(rows, ids, far_ids, count)
    other_ids = jnp.where(even, img_ids, txt_ids)
    diagonal = lax.broadcasted_iota(jnp.int32, (count, count), 0) == lax.broadcasted_iota(
        jnp.int32, (count, count), 1
    )
    other_ids = jnp.sum(jnp.where(diagonal, other_ids, 0), axis=0, keepdims=True)
    return jnp.where(even, txt_ids, img_ids), other_ids


def scores_of(mine_refs, other):
    mine = jnp.concatenate([ref[...] for ref in mine_refs], axis=0)
    return lax.dot_general(mine, other, (((1,), (1,)), ((), ())), preferred_element_type=f32)


def most_kernel(blocks, *refs):
    other = jnp.concatenate([ref[...] for ref in refs[blocks:-1]], axis=0)
    refs[-1][...] = scores_of(refs[:blocks], other)


def rest_kernel(blocks, split, ids_ref, most_ref, *refs):
    mine_refs, (*other_refs, last_ref) = refs[:blocks], refs[blocks:2 * blocks]
    own_ref, same_ref, cross_ref, *send_refs = refs[2 * blocks:]
    height, width = own_ref.shape
    rows = height // 2
    last, far_ids = unpack(last_ref, height, width, ids_ref.shape[1])
    mine_ids, other_ids = side_ids(rows, ids_ref[...], far_ids, blocks * height)
    scores = jnp.concatenate([most_ref[...], scores_of(mine_refs, last)], axis=1)
    coeff = pair_coeff(scale_logit * scores + shift_logit, mine_ids == other_ids)
    other = jnp.concatenate([*[ref[...] for ref in other_refs], last], axis=0)
    part = jnp.dot(coeff, other, preferred_element_type=f32)
    own_ref[...] = part[:height]
    whole = [k for k in range(1, blocks) if k != split]
    for k, ref in zip(whole, send_refs):
        ref[...] = part[k * height:(k + 1) * height].astype(bf16)
    block = part[split * height:(split + 1) * height].astype(bf16)
    even = is_even()
    same_ref[...] = jnp.where(even, block[:rows], block[rows:])
    cross_ref[...] = jnp.where(even, block[rows:], block[:rows])


def sum_kernel(own_ref, *refs):
    *got_refs, keep_ref, send_ref = refs
    rows = keep_ref.shape[0]
    total = own_ref[...]
    for ref in got_refs:
        total = total + ref[...].astype(f32)
    even = is_even()
    keep_ref[...] = jnp.where(even, total[:rows], total[rows:])
    send_ref[...] = jnp.where(even, total[rows:], total[:rows]).astype(bf16)


def keep_kernel(raw_ref, keep_ref, same_ref, grad_ref, unit_ref, inverse_ref):
    rows = keep_ref.shape[0]
    even = is_even()
    unit, inverse = normalize(raw_ref[...])
    grad_ref[...] = back_norm(
        jnp.where(even, unit[:rows], unit[rows:]),
        jnp.where(even, inverse[:rows], inverse[rows:]),
        keep_ref[...] + same_ref[...].astype(f32),
    )
    unit_ref[...] = jnp.where(even, unit[rows:], unit[:rows])
    inverse_ref[...] = jnp.where(even, inverse[rows:], inverse[:rows])


def out_kernel(grad_ref, unit_ref, inverse_ref, cross_ref, got_ref, img_ref, txt_ref):
    even = is_even()
    total = got_ref[...].astype(f32) + cross_ref[...].astype(f32)
    keep = grad_ref[...]
    got = back_norm(unit_ref[...], inverse_ref[...], total)
    txt_ref[...] = jnp.where(even, keep, got)
    img_ref[...] = jnp.where(even, got, keep)


def local(image_embeds, text_embeds, pair_ids):
    rows, width = image_embeds.shape
    blocks = max(lax.axis_size("img") // 2, lax.axis_size("txt"))
    pair = jax.ShapeDtypeStruct((2 * rows, width), bf16)
    total = jax.ShapeDtypeStruct((2 * rows, width), f32)
    piece = jax.ShapeDtypeStruct((rows, width), bf16)
    single = jax.ShapeDtypeStruct((rows, width), f32)
    ids = pair_ids.reshape(1, -1)
    far_txt = core_swap(text_embeds)
    far_img = core_swap(image_embeds)
    near = jnp.concatenate([text_embeds, image_embeds])
    mine, other = call(sides_kernel, [pair] * 2, [near, far_txt, far_img])
    order = list(range(blocks - 1, 0, -1))
    mine = [mine] + [chip_swap(mine, k) for k in order]
    packed = jax.ShapeDtypeStruct((2 * rows * (width // LANES) + 16, LANES), bf16)
    (packed,) = call(pack_kernel, [packed], [ids, mine[-1]])
    other = [other] + [core_swap(block) for block in [*mine[1:-1], packed]]
    count = blocks * 2 * rows
    (most,) = call(
        functools.partial(most_kernel, blocks),
        [jax.ShapeDtypeStruct((count, count - 2 * rows), f32)],
        [*mine, *other[:-1]],
        cost=LONG,
    )
    split = min(2, blocks - 1)
    own, same, cross, *send = call(
        functools.partial(rest_kernel, blocks, split),
        [total] + [piece] * 2 + [pair] * (blocks - 2),
        [ids, most, *mine, *other],
    )
    far = order.pop(split - 1)
    got = [chip_swap(block, k) for k, block in zip(order, send)]
    same = chip_swap(same, far)
    cross = chip_swap(cross, far, cross=1)
    keep, send = call(sum_kernel, [single, piece], [own, *got])
    got = core_swap(send)
    column = jax.ShapeDtypeStruct((rows, 1), f32)
    kept = call(keep_kernel, [single, single, column], [near, keep, same], cost=LONG)
    return tuple(call(out_kernel, [single] * 2, [*kept, cross, got]))


def solution(mesh):
    return jax.shard_map(
        local,
        mesh=mesh,
        in_specs=(P(("img", "txt"), None), P(("txt", "img"), None), P("img")),
        out_specs=(P(("img", "txt"), None), P(("txt", "img"), None)),
        check_vma=False,
    )
```

```python
import functools

import jax
import jax.numpy as jnp
from jax import lax
from jax.experimental import pallas as pl
from jax.experimental.pallas import tpu as pltpu
from jax.sharding import PartitionSpec as P

scale_logit = 8.0
shift_logit = -4.0
epsilon = 1e-06
LANES = 128
f32 = jnp.float32
bf16 = jnp.bfloat16
VMEM = pl.BlockSpec(memory_space=pltpu.VMEM)
LONG = pl.CostEstimate(flops=10**10, bytes_accessed=10**7, transcendentals=0)


def normalize(raw):
    values = raw.astype(f32)
    inverse = lax.rsqrt(jnp.sum(values * values, axis=-1, keepdims=True) + epsilon)
    return (values * inverse, inverse)


def back_norm(unit, inverse, grad):
    inner = jnp.sum(unit * grad, axis=-1, keepdims=True)
    return inverse * (grad - unit * inner)


def pair_coeff(logit, same):
    label = jnp.where(same, 1.0, -1.0).astype(f32)
    return (-scale_logit * label * jax.nn.sigmoid(-label * logit)).astype(bf16)


def core_swap(block):
    size = lax.axis_size("img")
    return lax.ppermute(block, "img", [(i, i ^ 1) for i in range(size)])


def chip_swap(block, distance, cross=0):
    n_img, n_txt = lax.axis_size("img"), lax.axis_size("txt")
    pairs = []
    for img in range(n_img):
        for txt in range(n_txt):
            if img % 2 == 0 and distance < n_img // 2:
                pairs.append((img * n_txt + txt, (img ^ (2 * distance) ^ cross) * n_txt + txt))
            if img % 2 == 1 and distance < n_txt:
                pairs.append((img * n_txt + txt, (img ^ cross) * n_txt + (txt ^ distance)))
    return lax.ppermute(block, ("img", "txt"), pairs)


def is_even():
    return lax.axis_index("img") % 2 == 0


def call(kernel, outs, args, cost=None):
    sizes = [a.size * a.dtype.itemsize for a in list(args) + list(outs)]
    return pl.pallas_call(
        kernel,
        out_shape=outs,
        in_specs=[VMEM] * len(args),
        out_specs=[VMEM] * len(outs),
        cost_estimate=cost,
        compiler_params=pltpu.CompilerParams(
            vmem_limit_bytes=min(48 * 2**20, 8 * 2**20 + 6 * sum(sizes))
        ),
    )(*args)


def sides_kernel(own_ref, txt_ref, img_ref, mine_ref, other_ref):
    rows = txt_ref.shape[0]
    even = is_even()
    own = normalize(own_ref[...])[0].astype(bf16)
    own_txt, own_img = own[:rows], own[rows:]
    far_txt = normalize(txt_ref[...])[0].astype(bf16)
    far_img = normalize(img_ref[...])[0].astype(bf16)
    mine_ref[:rows, :] = jnp.where(even, own_txt, far_img)
    mine_ref[rows:, :] = jnp.where(even, far_txt, own_img)
    other_ref[:rows, :] = jnp.where(even, own_img, far_txt)
    other_ref[rows:, :] = jnp.where(even, far_img, own_txt)


def pack_kernel(ids_ref, piece_ref, out_ref):
    height, width = piece_ref.shape
    tiles = width // LANES
    count = ids_ref.shape[1]
    for k in range(tiles):
        out_ref[k * height:(k + 1) * height, :] = piece_ref[:, k * LANES:(k + 1) * LANES]
    rest = out_ref.shape[0] - tiles * height
    row = lax.broadcasted_iota(jnp.int32, (rest, LANES), 0)
    code = jnp.zeros((rest, LANES), f32)
    for k in range(0, count, LANES):
        ids = ids_ref[:, k:k + LANES]
        if ids.shape[1] < LANES:
            ids = jnp.concatenate([ids, jnp.zeros((1, LANES - ids.shape[1]), ids.dtype)], axis=1)
        code = jnp.where(row == 2 * k // LANES, (ids // 256).astype(f32), code)
        code = jnp.where(row == 2 * k // LANES + 1, (ids % 256).astype(f32), code)
    out_ref[tiles * height:, :] = code.astype(bf16)


def unpack(ref, height, width, count):
    tiles = width // LANES
    piece = jnp.concatenate(
        [ref[k * height:(k + 1) * height, :] for k in range(tiles)], axis=1
    )
    code = ref[tiles * height:, :].astype(f32)
    ids = [code[k:k + 1] * 256.0 + code[k + 1:k + 2] for k in range(0, 2 * count // LANES or 2, 2)]
    ids = jnp.concatenate(ids, axis=1)[:, :count].astype(jnp.int32)
    return piece, ids


def row_ids(rows, ids, far_ids, count):
    me_img = lax.axis_index("img")
    me_txt = lax.axis_index("txt")
    n_img = lax.axis_size("img")
    row = lax.broadcasted_iota(jnp.int32, (count, 1), 0)
    block, core, j = row // (2 * rows), row // rows % 2, row % rows
    chip = jnp.where(block == 0, 0, count // (2 * rows) - block)
    txt_ids = (me_txt * n_img + (((me_img // 2) ^ chip) * 2 + core)) * rows + j
    source = (me_txt ^ chip) * rows + j
    here = lax.broadcasted_iota(jnp.int32, (count, ids.shape[1]), 1) == source
    per_core = jnp.where(core == me_img % 2, ids, far_ids)
    img_ids = jnp.sum(jnp.where(here, per_core, 0), axis=1, keepdims=True)
    return txt_ids, img_ids


def side_ids(rows, ids, far_ids, count):
    even = is_even()
    txt_ids, img_ids = row_ids(rows, ids, far_ids, count)
    other_ids = jnp.where(even, img_ids, txt_ids)
    diagonal = lax.broadcasted_iota(jnp.int32, (count, count), 0) == lax.broadcasted_iota(
        jnp.int32, (count, count), 1
    )
    other_ids = jnp.sum(jnp.where(diagonal, other_ids, 0), axis=0, keepdims=True)
    return jnp.where(even, txt_ids, img_ids), other_ids


def scores_of(mine_refs, other):
    mine = jnp.concatenate([ref[...] for ref in mine_refs], axis=0)
    return lax.dot_general(mine, other, (((1,), (1,)), ((), ())), preferred_element_type=f32)


def most_kernel(blocks, *refs):
    other = jnp.concatenate([ref[...] for ref in refs[blocks:-1]], axis=0)
    refs[-1][...] = scores_of(refs[:blocks], other)


def rest_kernel(blocks, split, ids_ref, most_ref, *refs):
    mine_refs, (*other_refs, last_ref) = refs[:blocks], refs[blocks:2 * blocks]
    own_ref, same_ref, cross_ref, *send_refs = refs[2 * blocks:]
    height, width = own_ref.shape
    rows = height // 2
    last, far_ids = unpack(last_ref, height, width, ids_ref.shape[1])
    mine_ids, other_ids = side_ids(rows, ids_ref[...], far_ids, blocks * height)
    scores = jnp.concatenate([most_ref[...], scores_of(mine_refs, last)], axis=1)
    coeff = pair_coeff(scale_logit * scores + shift_logit, mine_ids == other_ids)
    other = jnp.concatenate([*[ref[...] for ref in other_refs], last], axis=0)
    part = jnp.dot(coeff, other, preferred_element_type=f32)
    own_ref[...] = part[:height]
    whole = [k for k in range(1, blocks) if k != split]
    for k, ref in zip(whole, send_refs):
        ref[...] = part[k * height:(k + 1) * height].astype(bf16)
    block = part[split * height:(split + 1) * height].astype(bf16)
    even = is_even()
    same_ref[...] = jnp.where(even, block[:rows], block[rows:])
    cross_ref[...] = jnp.where(even, block[rows:], block[:rows])


def sum_kernel(own_ref, *refs):
    *got_refs, keep_ref, send_ref = refs
    rows = keep_ref.shape[0]
    total = own_ref[...]
    for ref in got_refs:
        total = total + ref[...].astype(f32)
    even = is_even()
    keep_ref[...] = jnp.where(even, total[:rows], total[rows:])
    send_ref[...] = jnp.where(even, total[rows:], total[:rows]).astype(bf16)


def keep_kernel(raw_ref, keep_ref, same_ref, grad_ref, unit_ref, inverse_ref):
    rows = keep_ref.shape[0]
    even = is_even()
    unit, inverse = normalize(raw_ref[...])
    grad_ref[...] = back_norm(
        jnp.where(even, unit[:rows], unit[rows:]),
        jnp.where(even, inverse[:rows], inverse[rows:]),
        keep_ref[...] + same_ref[...].astype(f32),
    )
    unit_ref[...] = jnp.where(even, unit[rows:], unit[:rows])
    inverse_ref[...] = jnp.where(even, inverse[rows:], inverse[:rows])


def out_kernel(grad_ref, unit_ref, inverse_ref, cross_ref, got_ref, img_ref, txt_ref):
    even = is_even()
    total = got_ref[...].astype(f32) + cross_ref[...].astype(f32)
    keep = grad_ref[...]
    got = back_norm(unit_ref[...], inverse_ref[...], total)
    txt_ref[...] = jnp.where(even, keep, got)
    img_ref[...] = jnp.where(even, got, keep)


def local(image_embeds, text_embeds, pair_ids):
    rows, width = image_embeds.shape
    blocks = max(lax.axis_size("img") // 2, lax.axis_size("txt"))
    pair = jax.ShapeDtypeStruct((2 * rows, width), bf16)
    total = jax.ShapeDtypeStruct((2 * rows, width), f32)
    piece = jax.ShapeDtypeStruct((rows, width), bf16)
    single = jax.ShapeDtypeStruct((rows, width), f32)
    ids = pair_ids.reshape(1, -1)
    far_txt = core_swap(text_embeds)
    far_img = core_swap(image_embeds)
    near = jnp.concatenate([text_embeds, image_embeds])
    mine, other = call(sides_kernel, [pair] * 2, [near, far_txt, far_img])
    order = list(range(blocks - 1, 0, -1))
    mine = [mine] + [chip_swap(mine, k) for k in order]
    packed = jax.ShapeDtypeStruct((2 * rows * (width // LANES) + 16, LANES), bf16)
    (packed,) = call(pack_kernel, [packed], [ids, mine[-1]])
    other = [other] + [core_swap(block) for block in [*mine[1:-1], packed]]
    count = blocks * 2 * rows
    (most,) = call(
        functools.partial(most_kernel, blocks),
        [jax.ShapeDtypeStruct((count, count - 2 * rows), f32)],
        [*mine, *other[:-1]],
        cost=LONG,
    )
    split = blocks - 1
    own, same, cross, *send = call(
        functools.partial(rest_kernel, blocks, split),
        [total] + [piece] * 2 + [pair] * (blocks - 2),
        [ids, most, *mine, *other],
    )
    far = order.pop(split - 1)
    got = [chip_swap(block, k) for k, block in zip(order, send)]
    same = chip_swap(same, far)
    cross = chip_swap(cross, far, cross=1)
    keep, send = call(sum_kernel, [single, piece], [own, *got])
    got = core_swap(send)
    column = jax.ShapeDtypeStruct((rows, 1), f32)
    kept = call(keep_kernel, [single, single, column], [near, keep, same], cost=LONG)
    return tuple(call(out_kernel, [single] * 2, [*kept, cross, got]))


def solution(mesh):
    return jax.shard_map(
        local,
        mesh=mesh,
        in_specs=(P(("img", "txt"), None), P(("txt", "img"), None), P("img")),
        out_specs=(P(("img", "txt"), None), P(("txt", "img"), None)),
        check_vma=False,
    )
```

```python
import functools

import jax
import jax.numpy as jnp
from jax import lax
from jax.experimental import pallas as pl
from jax.experimental.pallas import tpu as pltpu
from jax.sharding import PartitionSpec as P

scale_logit = 8.0
shift_logit = -4.0
epsilon = 1e-06
LANES = 128
f32 = jnp.float32
bf16 = jnp.bfloat16
VMEM = pl.BlockSpec(memory_space=pltpu.VMEM)
LONG = pl.CostEstimate(flops=10**10, bytes_accessed=10**7, transcendentals=0)


def normalize(raw):
    values = raw.astype(f32)
    inverse = lax.rsqrt(jnp.sum(values * values, axis=-1, keepdims=True) + epsilon)
    return (values * inverse, inverse)


def back_norm(unit, inverse, grad):
    inner = jnp.sum(unit * grad, axis=-1, keepdims=True)
    return inverse * (grad - unit * inner)


def pair_coeff(logit, same):
    label = jnp.where(same, 1.0, -1.0).astype(f32)
    return (-scale_logit * label * jax.nn.sigmoid(-label * logit)).astype(bf16)


def core_swap(block):
    size = lax.axis_size("img")
    return lax.ppermute(block, "img", [(i, i ^ 1) for i in range(size)])


def chip_swap(block, distance, cross=0):
    n_img, n_txt = lax.axis_size("img"), lax.axis_size("txt")
    pairs = []
    for img in range(n_img):
        for txt in range(n_txt):
            if img % 2 == 0 and distance < n_img // 2:
                pairs.append((img * n_txt + txt, (img ^ (2 * distance) ^ cross) * n_txt + txt))
            if img % 2 == 1 and distance < n_txt:
                pairs.append((img * n_txt + txt, (img ^ cross) * n_txt + (txt ^ distance)))
    return lax.ppermute(block, ("img", "txt"), pairs)


def is_even():
    return lax.axis_index("img") % 2 == 0


def call(kernel, outs, args, cost=None):
    sizes = [a.size * a.dtype.itemsize for a in list(args) + list(outs)]
    return pl.pallas_call(
        kernel,
        out_shape=outs,
        in_specs=[VMEM] * len(args),
        out_specs=[VMEM] * len(outs),
        cost_estimate=cost,
        compiler_params=pltpu.CompilerParams(
            vmem_limit_bytes=min(48 * 2**20, 8 * 2**20 + 6 * sum(sizes))
        ),
    )(*args)


def sides_kernel(own_ref, txt_ref, img_ref, mine_ref, other_ref):
    rows = txt_ref.shape[0]
    even = is_even()
    own = normalize(own_ref[...])[0].astype(bf16)
    own_txt, own_img = own[:rows], own[rows:]
    far_txt = normalize(txt_ref[...])[0].astype(bf16)
    far_img = normalize(img_ref[...])[0].astype(bf16)
    mine_ref[:rows, :] = jnp.where(even, own_txt, far_img)
    mine_ref[rows:, :] = jnp.where(even, far_txt, own_img)
    other_ref[:rows, :] = jnp.where(even, own_img, far_txt)
    other_ref[rows:, :] = jnp.where(even, far_img, own_txt)


def pack_kernel(ids_ref, piece_ref, out_ref):
    height, width = piece_ref.shape
    tiles = width // LANES
    count = ids_ref.shape[1]
    for k in range(tiles):
        out_ref[k * height:(k + 1) * height, :] = piece_ref[:, k * LANES:(k + 1) * LANES]
    rest = out_ref.shape[0] - tiles * height
    row = lax.broadcasted_iota(jnp.int32, (rest, LANES), 0)
    code = jnp.zeros((rest, LANES), f32)
    for k in range(0, count, LANES):
        ids = ids_ref[:, k:k + LANES]
        if ids.shape[1] < LANES:
            ids = jnp.concatenate([ids, jnp.zeros((1, LANES - ids.shape[1]), ids.dtype)], axis=1)
        code = jnp.where(row == 2 * k // LANES, (ids // 256).astype(f32), code)
        code = jnp.where(row == 2 * k // LANES + 1, (ids % 256).astype(f32), code)
    out_ref[tiles * height:, :] = code.astype(bf16)


def unpack(ref, height, width, count):
    tiles = width // LANES
    piece = jnp.concatenate(
        [ref[k * height:(k + 1) * height, :] for k in range(tiles)], axis=1
    )
    code = ref[tiles * height:, :].astype(f32)
    ids = [code[k:k + 1] * 256.0 + code[k + 1:k + 2] for k in range(0, 2 * count // LANES or 2, 2)]
    ids = jnp.concatenate(ids, axis=1)[:, :count].astype(jnp.int32)
    return piece, ids


def row_ids(rows, ids, far_ids, count):
    me_img = lax.axis_index("img")
    me_txt = lax.axis_index("txt")
    n_img = lax.axis_size("img")
    row = lax.broadcasted_iota(jnp.int32, (count, 1), 0)
    block, core, j = row // (2 * rows), row // rows % 2, row % rows
    chip = jnp.where(block == 0, 0, count // (2 * rows) - block)
    txt_ids = (me_txt * n_img + (((me_img // 2) ^ chip) * 2 + core)) * rows + j
    source = (me_txt ^ chip) * rows + j
    here = lax.broadcasted_iota(jnp.int32, (count, ids.shape[1]), 1) == source
    per_core = jnp.where(core == me_img % 2, ids, far_ids)
    img_ids = jnp.sum(jnp.where(here, per_core, 0), axis=1, keepdims=True)
    return txt_ids, img_ids


def side_ids(rows, ids, far_ids, count):
    even = is_even()
    txt_ids, img_ids = row_ids(rows, ids, far_ids, count)
    other_ids = jnp.where(even, img_ids, txt_ids)
    diagonal = lax.broadcasted_iota(jnp.int32, (count, count), 0) == lax.broadcasted_iota(
        jnp.int32, (count, count), 1
    )
    other_ids = jnp.sum(jnp.where(diagonal, other_ids, 0), axis=0, keepdims=True)
    return jnp.where(even, txt_ids, img_ids), other_ids


def scores_of(mine_refs, other):
    mine = jnp.concatenate([ref[...] for ref in mine_refs], axis=0)
    return lax.dot_general(mine, other, (((1,), (1,)), ((), ())), preferred_element_type=f32)


def most_kernel(blocks, *refs):
    other = jnp.concatenate([ref[...] for ref in refs[blocks:-1]], axis=0)
    refs[-1][...] = scores_of(refs[:blocks], other)


def rest_kernel(blocks, split, ids_ref, most_ref, *refs):
    mine_refs, (*other_refs, last_ref) = refs[:blocks], refs[blocks:2 * blocks]
    own_ref, same_ref, cross_ref, *send_refs = refs[2 * blocks:]
    height, width = own_ref.shape
    rows = height // 2
    last, far_ids = unpack(last_ref, height, width, ids_ref.shape[1])
    mine_ids, other_ids = side_ids(rows, ids_ref[...], far_ids, blocks * height)
    scores = jnp.concatenate([most_ref[...], scores_of(mine_refs, last)], axis=1)
    coeff = pair_coeff(scale_logit * scores + shift_logit, mine_ids == other_ids)
    other = jnp.concatenate([*[ref[...] for ref in other_refs], last], axis=0)
    part = jnp.dot(coeff, other, preferred_element_type=f32)
    own_ref[...] = part[:height]
    whole = [k for k in range(1, blocks) if k != split]
    for k, ref in zip(whole, send_refs):
        ref[...] = part[k * height:(k + 1) * height].astype(bf16)
    block = part[split * height:(split + 1) * height].astype(bf16)
    even = is_even()
    same_ref[...] = jnp.where(even, block[:rows], block[rows:])
    cross_ref[...] = jnp.where(even, block[rows:], block[:rows])


def sum_kernel(own_ref, *refs):
    *got_refs, keep_ref, send_ref = refs
    rows = keep_ref.shape[0]
    total = own_ref[...]
    for ref in got_refs:
        total = total + ref[...].astype(f32)
    even = is_even()
    keep_ref[...] = jnp.where(even, total[:rows], total[rows:])
    send_ref[...] = jnp.where(even, total[rows:], total[:rows]).astype(bf16)


def keep_kernel(raw_ref, keep_ref, same_ref, grad_ref, unit_ref, inverse_ref):
    rows = keep_ref.shape[0]
    even = is_even()
    unit, inverse = normalize(raw_ref[...])
    grad_ref[...] = back_norm(
        jnp.where(even, unit[:rows], unit[rows:]),
        jnp.where(even, inverse[:rows], inverse[rows:]),
        keep_ref[...] + same_ref[...].astype(f32),
    )
    unit_ref[...] = jnp.where(even, unit[rows:], unit[:rows])
    inverse_ref[...] = jnp.where(even, inverse[rows:], inverse[:rows])


def out_kernel(grad_ref, unit_ref, inverse_ref, cross_ref, got_ref, img_ref, txt_ref):
    even = is_even()
    total = got_ref[...].astype(f32) + cross_ref[...].astype(f32)
    keep = grad_ref[...]
    got = back_norm(unit_ref[...], inverse_ref[...], total)
    txt_ref[...] = jnp.where(even, keep, got)
    img_ref[...] = jnp.where(even, got, keep)


def local(image_embeds, text_embeds, pair_ids):
    rows, width = image_embeds.shape
    blocks = max(lax.axis_size("img") // 2, lax.axis_size("txt"))
    pair = jax.ShapeDtypeStruct((2 * rows, width), bf16)
    total = jax.ShapeDtypeStruct((2 * rows, width), f32)
    piece = jax.ShapeDtypeStruct((rows, width), bf16)
    single = jax.ShapeDtypeStruct((rows, width), f32)
    ids = pair_ids.reshape(1, -1)
    far_txt = core_swap(text_embeds)
    far_img = core_swap(image_embeds)
    near = jnp.concatenate([text_embeds, image_embeds])
    mine, other = call(sides_kernel, [pair] * 2, [near, far_txt, far_img])
    order = list(range(blocks - 1, 0, -1))
    mine = [mine] + [chip_swap(mine, k) for k in order]
    packed = jax.ShapeDtypeStruct((2 * rows * (width // LANES) + 16, LANES), bf16)
    (packed,) = call(pack_kernel, [packed], [ids, mine[-1]])
    other = [other] + [core_swap(block) for block in [*mine[1:-1], packed]]
    count = blocks * 2 * rows
    (most,) = call(
        functools.partial(most_kernel, blocks),
        [jax.ShapeDtypeStruct((count, count - 2 * rows), f32)],
        [*mine, *other[:-1]],
        cost=LONG,
    )
    split = min(2, blocks - 1)
    own, same, cross, *send = call(
        functools.partial(rest_kernel, blocks, split),
        [total] + [piece] * 2 + [pair] * (blocks - 2),
        [ids, most, *mine, *other],
    )
    far = order.pop(split - 1)
    got = [chip_swap(block, k) for k, block in zip(order, send)][::-1]
    same = chip_swap(same, far)
    cross = chip_swap(cross, far, cross=1)
    keep, send = call(sum_kernel, [single, piece], [own, *got])
    got = core_swap(send)
    column = jax.ShapeDtypeStruct((rows, 1), f32)
    kept = call(keep_kernel, [single, single, column], [near, keep, same], cost=LONG)
    return tuple(call(out_kernel, [single] * 2, [*kept, cross, got]))


def solution(mesh):
    return jax.shard_map(
        local,
        mesh=mesh,
        in_specs=(P(("img", "txt"), None), P(("txt", "img"), None), P("img")),
        out_specs=(P(("img", "txt"), None), P(("txt", "img"), None)),
        check_vma=False,
    )
```

```python
import functools

import jax
import jax.numpy as jnp
from jax import lax
from jax.experimental import pallas as pl
from jax.experimental.pallas import tpu as pltpu
from jax.sharding import PartitionSpec as P

scale_logit = 8.0
shift_logit = -4.0
epsilon = 1e-06
LANES = 128
f32 = jnp.float32
bf16 = jnp.bfloat16
VMEM = pl.BlockSpec(memory_space=pltpu.VMEM)
LONG = pl.CostEstimate(flops=10**10, bytes_accessed=10**7, transcendentals=0)


def normalize(raw):
    values = raw.astype(f32)
    inverse = lax.rsqrt(jnp.sum(values * values, axis=-1, keepdims=True) + epsilon)
    return (values * inverse, inverse)


def back_norm(unit, inverse, grad):
    inner = jnp.sum(unit * grad, axis=-1, keepdims=True)
    return inverse * (grad - unit * inner)


def pair_coeff(logit, same):
    label = jnp.where(same, 1.0, -1.0).astype(f32)
    return (-scale_logit * label * jax.nn.sigmoid(-label * logit)).astype(bf16)


def core_swap(block):
    size = lax.axis_size("img")
    return lax.ppermute(block, "img", [(i, i ^ 1) for i in range(size)])


def chip_swap(block, distance, cross=0):
    n_img, n_txt = lax.axis_size("img"), lax.axis_size("txt")
    pairs = []
    for img in range(n_img):
        for txt in range(n_txt):
            if img % 2 == 0 and distance < n_img // 2:
                pairs.append((img * n_txt + txt, (img ^ (2 * distance) ^ cross) * n_txt + txt))
            if img % 2 == 1 and distance < n_txt:
                pairs.append((img * n_txt + txt, (img ^ cross) * n_txt + (txt ^ distance)))
    return lax.ppermute(block, ("img", "txt"), pairs)


def is_even():
    return lax.axis_index("img") % 2 == 0


def call(kernel, outs, args, cost=None):
    sizes = [a.size * a.dtype.itemsize for a in list(args) + list(outs)]
    return pl.pallas_call(
        kernel,
        out_shape=outs,
        in_specs=[VMEM] * len(args),
        out_specs=[VMEM] * len(outs),
        cost_estimate=cost,
        compiler_params=pltpu.CompilerParams(
            vmem_limit_bytes=min(48 * 2**20, 8 * 2**20 + 6 * sum(sizes))
        ),
    )(*args)


def sides_kernel(own_ref, txt_ref, img_ref, mine_ref, other_ref):
    rows = txt_ref.shape[0]
    even = is_even()
    own = normalize(own_ref[...])[0].astype(bf16)
    own_txt, own_img = own[:rows], own[rows:]
    far_txt = normalize(txt_ref[...])[0].astype(bf16)
    far_img = normalize(img_ref[...])[0].astype(bf16)
    mine_ref[:rows, :] = jnp.where(even, own_txt, far_img)
    mine_ref[rows:, :] = jnp.where(even, far_txt, own_img)
    other_ref[:rows, :] = jnp.where(even, own_img, far_txt)
    other_ref[rows:, :] = jnp.where(even, far_img, own_txt)


def pack_kernel(ids_ref, piece_ref, out_ref):
    height, width = piece_ref.shape
    tiles = width // LANES
    count = ids_ref.shape[1]
    for k in range(tiles):
        out_ref[k * height:(k + 1) * height, :] = piece_ref[:, k * LANES:(k + 1) * LANES]
    rest = out_ref.shape[0] - tiles * height
    row = lax.broadcasted_iota(jnp.int32, (rest, LANES), 0)
    code = jnp.zeros((rest, LANES), f32)
    for k in range(0, count, LANES):
        ids = ids_ref[:, k:k + LANES]
        if ids.shape[1] < LANES:
            ids = jnp.concatenate([ids, jnp.zeros((1, LANES - ids.shape[1]), ids.dtype)], axis=1)
        code = jnp.where(row == 2 * k // LANES, (ids // 256).astype(f32), code)
        code = jnp.where(row == 2 * k // LANES + 1, (ids % 256).astype(f32), code)
    out_ref[tiles * height:, :] = code.astype(bf16)


def unpack(ref, height, width, count):
    tiles = width // LANES
    piece = jnp.concatenate(
        [ref[k * height:(k + 1) * height, :] for k in range(tiles)], axis=1
    )
    code = ref[tiles * height:, :].astype(f32)
    ids = [code[k:k + 1] * 256.0 + code[k + 1:k + 2] for k in range(0, 2 * count // LANES or 2, 2)]
    ids = jnp.concatenate(ids, axis=1)[:, :count].astype(jnp.int32)
    return piece, ids


def row_ids(rows, ids, far_ids, count):
    me_img = lax.axis_index("img")
    me_txt = lax.axis_index("txt")
    n_img = lax.axis_size("img")
    row = lax.broadcasted_iota(jnp.int32, (count, 1), 0)
    block, core, j = row // (2 * rows), row // rows % 2, row % rows
    blocks = count // (2 * rows)
    chip = jnp.where(block == 0, 0, blocks - block)
    if blocks > 2:
        chip = jnp.where(block == 1, blocks - 2, jnp.where(block == 2, blocks - 1, chip))
    txt_ids = (me_txt * n_img + (((me_img // 2) ^ chip) * 2 + core)) * rows + j
    source = (me_txt ^ chip) * rows + j
    here = lax.broadcasted_iota(jnp.int32, (count, ids.shape[1]), 1) == source
    per_core = jnp.where(core == me_img % 2, ids, far_ids)
    img_ids = jnp.sum(jnp.where(here, per_core, 0), axis=1, keepdims=True)
    return txt_ids, img_ids


def side_ids(rows, ids, far_ids, count):
    even = is_even()
    txt_ids, img_ids = row_ids(rows, ids, far_ids, count)
    other_ids = jnp.where(even, img_ids, txt_ids)
    diagonal = lax.broadcasted_iota(jnp.int32, (count, count), 0) == lax.broadcasted_iota(
        jnp.int32, (count, count), 1
    )
    other_ids = jnp.sum(jnp.where(diagonal, other_ids, 0), axis=0, keepdims=True)
    return jnp.where(even, txt_ids, img_ids), other_ids


def scores_of(mine_refs, other):
    mine = jnp.concatenate([ref[...] for ref in mine_refs], axis=0)
    return lax.dot_general(mine, other, (((1,), (1,)), ((), ())), preferred_element_type=f32)


def most_kernel(blocks, *refs):
    other = jnp.concatenate([ref[...] for ref in refs[blocks:-1]], axis=0)
    refs[-1][...] = scores_of(refs[:blocks], other)


def rest_kernel(blocks, split, ids_ref, most_ref, *refs):
    mine_refs, (*other_refs, last_ref) = refs[:blocks], refs[blocks:2 * blocks]
    own_ref, same_ref, cross_ref, *send_refs = refs[2 * blocks:]
    height, width = own_ref.shape
    rows = height // 2
    last, far_ids = unpack(last_ref, height, width, ids_ref.shape[1])
    mine_ids, other_ids = side_ids(rows, ids_ref[...], far_ids, blocks * height)
    scores = jnp.concatenate([most_ref[...], scores_of(mine_refs, last)], axis=1)
    coeff = pair_coeff(scale_logit * scores + shift_logit, mine_ids == other_ids)
    other = jnp.concatenate([*[ref[...] for ref in other_refs], last], axis=0)
    part = jnp.dot(coeff, other, preferred_element_type=f32)
    own_ref[...] = part[:height]
    whole = [k for k in range(1, blocks) if k != split]
    for k, ref in zip(whole, send_refs):
        ref[...] = part[k * height:(k + 1) * height].astype(bf16)
    block = part[split * height:(split + 1) * height].astype(bf16)
    even = is_even()
    same_ref[...] = jnp.where(even, block[:rows], block[rows:])
    cross_ref[...] = jnp.where(even, block[rows:], block[:rows])


def sum_kernel(own_ref, *refs):
    *got_refs, keep_ref, send_ref = refs
    rows = keep_ref.shape[0]
    total = own_ref[...]
    for ref in got_refs:
        total = total + ref[...].astype(f32)
    even = is_even()
    keep_ref[...] = jnp.where(even, total[:rows], total[rows:])
    send_ref[...] = jnp.where(even, total[rows:], total[:rows]).astype(bf16)


def keep_kernel(raw_ref, keep_ref, same_ref, grad_ref, unit_ref, inverse_ref):
    rows = keep_ref.shape[0]
    even = is_even()
    unit, inverse = normalize(raw_ref[...])
    grad_ref[...] = back_norm(
        jnp.where(even, unit[:rows], unit[rows:]),
        jnp.where(even, inverse[:rows], inverse[rows:]),
        keep_ref[...] + same_ref[...].astype(f32),
    )
    unit_ref[...] = jnp.where(even, unit[rows:], unit[:rows])
    inverse_ref[...] = jnp.where(even, inverse[rows:], inverse[:rows])


def out_kernel(grad_ref, unit_ref, inverse_ref, cross_ref, got_ref, img_ref, txt_ref):
    even = is_even()
    total = got_ref[...].astype(f32) + cross_ref[...].astype(f32)
    keep = grad_ref[...]
    got = back_norm(unit_ref[...], inverse_ref[...], total)
    txt_ref[...] = jnp.where(even, keep, got)
    img_ref[...] = jnp.where(even, got, keep)


def local(image_embeds, text_embeds, pair_ids):
    rows, width = image_embeds.shape
    blocks = max(lax.axis_size("img") // 2, lax.axis_size("txt"))
    pair = jax.ShapeDtypeStruct((2 * rows, width), bf16)
    total = jax.ShapeDtypeStruct((2 * rows, width), f32)
    piece = jax.ShapeDtypeStruct((rows, width), bf16)
    single = jax.ShapeDtypeStruct((rows, width), f32)
    ids = pair_ids.reshape(1, -1)
    far_txt = core_swap(text_embeds)
    far_img = core_swap(image_embeds)
    near = jnp.concatenate([text_embeds, image_embeds])
    mine, other = call(sides_kernel, [pair] * 2, [near, far_txt, far_img])
    order = list(range(blocks - 1, 0, -1))
    order[:2] = order[1::-1]
    mine = [mine] + [chip_swap(mine, k) for k in order]
    packed = jax.ShapeDtypeStruct((2 * rows * (width // LANES) + 16, LANES), bf16)
    (packed,) = call(pack_kernel, [packed], [ids, mine[-1]])
    other = [other] + [core_swap(block) for block in [*mine[1:-1], packed]]
    count = blocks * 2 * rows
    (most,) = call(
        functools.partial(most_kernel, blocks),
        [jax.ShapeDtypeStruct((count, count - 2 * rows), f32)],
        [*mine, *other[:-1]],
        cost=LONG,
    )
    split = 1
    own, same, cross, *send = call(
        functools.partial(rest_kernel, blocks, split),
        [total] + [piece] * 2 + [pair] * (blocks - 2),
        [ids, most, *mine, *other],
    )
    far = order.pop(split - 1)
    got = [chip_swap(block, k) for k, block in zip(order, send)]
    same = chip_swap(same, far)
    cross = chip_swap(cross, far, cross=1)
    keep, send = call(sum_kernel, [single, piece], [own, *got])
    got = core_swap(send)
    column = jax.ShapeDtypeStruct((rows, 1), f32)
    kept = call(keep_kernel, [single, single, column], [near, keep, same], cost=LONG)
    return tuple(call(out_kernel, [single] * 2, [*kept, cross, got]))


def solution(mesh):
    return jax.shard_map(
        local,
        mesh=mesh,
        in_specs=(P(("img", "txt"), None), P(("txt", "img"), None), P("img")),
        out_specs=(P(("img", "txt"), None), P(("txt", "img"), None)),
        check_vma=False,
    )
```

```python
import functools

import jax
import jax.numpy as jnp
from jax import lax
from jax.experimental import pallas as pl
from jax.experimental.pallas import tpu as pltpu
from jax.sharding import PartitionSpec as P

scale_logit = 8.0
shift_logit = -4.0
epsilon = 1e-06
LANES = 128
TXT_CORE = 1
f32 = jnp.float32
bf16 = jnp.bfloat16
VMEM = pl.BlockSpec(memory_space=pltpu.VMEM)
LONG = pl.CostEstimate(flops=10**10, bytes_accessed=10**7, transcendentals=0)


def normalize(raw):
    values = raw.astype(f32)
    inverse = lax.rsqrt(jnp.sum(values * values, axis=-1, keepdims=True) + epsilon)
    return (values * inverse, inverse)


def back_norm(unit, inverse, grad):
    inner = jnp.sum(unit * grad, axis=-1, keepdims=True)
    return inverse * (grad - unit * inner)


def pair_coeff(logit, same):
    label = jnp.where(same, 1.0, -1.0).astype(f32)
    return (-scale_logit * label * jax.nn.sigmoid(-label * logit)).astype(bf16)


def core_swap(block):
    size = lax.axis_size("img")
    return lax.ppermute(block, "img", [(i, i ^ 1) for i in range(size)])


def chip_swap(block, distance, cross=0):
    n_img, n_txt = lax.axis_size("img"), lax.axis_size("txt")
    pairs = []
    for img in range(n_img):
        for txt in range(n_txt):
            if img % 2 == TXT_CORE and distance < n_img // 2:
                pairs.append((img * n_txt + txt, (img ^ (2 * distance) ^ cross) * n_txt + txt))
            if img % 2 != TXT_CORE and distance < n_txt:
                pairs.append((img * n_txt + txt, (img ^ cross) * n_txt + (txt ^ distance)))
    return lax.ppermute(block, ("img", "txt"), pairs)


def is_txt():
    return lax.axis_index("img") % 2 == TXT_CORE


def is_even():
    return lax.axis_index("img") % 2 == 0


def call(kernel, outs, args, cost=None):
    sizes = [a.size * a.dtype.itemsize for a in list(args) + list(outs)]
    return pl.pallas_call(
        kernel,
        out_shape=outs,
        in_specs=[VMEM] * len(args),
        out_specs=[VMEM] * len(outs),
        cost_estimate=cost,
        compiler_params=pltpu.CompilerParams(
            vmem_limit_bytes=min(48 * 2**20, 8 * 2**20 + 6 * sum(sizes))
        ),
    )(*args)


def sides_kernel(own_ref, txt_ref, img_ref, mine_ref, other_ref):
    rows = txt_ref.shape[0]
    even, txt = is_even(), is_txt()
    own = normalize(own_ref[...])[0].astype(bf16)
    far_txt = normalize(txt_ref[...])[0].astype(bf16)
    far_img = normalize(img_ref[...])[0].astype(bf16)
    mine_own = jnp.where(txt, own[:rows], own[rows:])
    mine_far = jnp.where(txt, far_txt, far_img)
    other_own = jnp.where(txt, own[rows:], own[:rows])
    other_far = jnp.where(txt, far_img, far_txt)
    mine_ref[:rows, :] = jnp.where(even, mine_own, mine_far)
    mine_ref[rows:, :] = jnp.where(even, mine_far, mine_own)
    other_ref[:rows, :] = jnp.where(even, other_own, other_far)
    other_ref[rows:, :] = jnp.where(even, other_far, other_own)


def pack_kernel(ids_ref, piece_ref, out_ref):
    height, width = piece_ref.shape
    tiles = width // LANES
    count = ids_ref.shape[1]
    for k in range(tiles):
        out_ref[k * height:(k + 1) * height, :] = piece_ref[:, k * LANES:(k + 1) * LANES]
    rest = out_ref.shape[0] - tiles * height
    row = lax.broadcasted_iota(jnp.int32, (rest, LANES), 0)
    code = jnp.zeros((rest, LANES), f32)
    for k in range(0, count, LANES):
        ids = ids_ref[:, k:k + LANES]
        if ids.shape[1] < LANES:
            ids = jnp.concatenate([ids, jnp.zeros((1, LANES - ids.shape[1]), ids.dtype)], axis=1)
        code = jnp.where(row == 2 * k // LANES, (ids // 256).astype(f32), code)
        code = jnp.where(row == 2 * k // LANES + 1, (ids % 256).astype(f32), code)
    out_ref[tiles * height:, :] = code.astype(bf16)


def unpack(ref, height, width, count):
    tiles = width // LANES
    piece = jnp.concatenate(
        [ref[k * height:(k + 1) * height, :] for k in range(tiles)], axis=1
    )
    code = ref[tiles * height:, :].astype(f32)
    ids = [code[k:k + 1] * 256.0 + code[k + 1:k + 2] for k in range(0, 2 * count // LANES or 2, 2)]
    ids = jnp.concatenate(ids, axis=1)[:, :count].astype(jnp.int32)
    return piece, ids


def row_ids(rows, ids, far_ids, count):
    me_img = lax.axis_index("img")
    me_txt = lax.axis_index("txt")
    n_img = lax.axis_size("img")
    row = lax.broadcasted_iota(jnp.int32, (count, 1), 0)
    block, core, j = row // (2 * rows), row // rows % 2, row % rows
    chip = jnp.where(block == 0, 0, count // (2 * rows) - block)
    txt_ids = (me_txt * n_img + (((me_img // 2) ^ chip) * 2 + core)) * rows + j
    source = (me_txt ^ chip) * rows + j
    here = lax.broadcasted_iota(jnp.int32, (count, ids.shape[1]), 1) == source
    per_core = jnp.where(core == me_img % 2, ids, far_ids)
    img_ids = jnp.sum(jnp.where(here, per_core, 0), axis=1, keepdims=True)
    return txt_ids, img_ids


def side_ids(rows, ids, far_ids, count):
    txt = is_txt()
    txt_ids, img_ids = row_ids(rows, ids, far_ids, count)
    other_ids = jnp.where(txt, img_ids, txt_ids)
    diagonal = lax.broadcasted_iota(jnp.int32, (count, count), 0) == lax.broadcasted_iota(
        jnp.int32, (count, count), 1
    )
    other_ids = jnp.sum(jnp.where(diagonal, other_ids, 0), axis=0, keepdims=True)
    return jnp.where(txt, txt_ids, img_ids), other_ids


def scores_of(mine_refs, other):
    mine = jnp.concatenate([ref[...] for ref in mine_refs], axis=0)
    return lax.dot_general(mine, other, (((1,), (1,)), ((), ())), preferred_element_type=f32)


def most_kernel(blocks, *refs):
    other = jnp.concatenate([ref[...] for ref in refs[blocks:-1]], axis=0)
    refs[-1][...] = scores_of(refs[:blocks], other)


def rest_kernel(blocks, split, ids_ref, most_ref, *refs):
    mine_refs, (*other_refs, last_ref) = refs[:blocks], refs[blocks:2 * blocks]
    own_ref, same_ref, cross_ref, *send_refs = refs[2 * blocks:]
    height, width = own_ref.shape
    rows = height // 2
    last, far_ids = unpack(last_ref, height, width, ids_ref.shape[1])
    mine_ids, other_ids = side_ids(rows, ids_ref[...], far_ids, blocks * height)
    scores = jnp.concatenate([most_ref[...], scores_of(mine_refs, last)], axis=1)
    coeff = pair_coeff(scale_logit * scores + shift_logit, mine_ids == other_ids)
    other = jnp.concatenate([*[ref[...] for ref in other_refs], last], axis=0)
    part = jnp.dot(coeff, other, preferred_element_type=f32)
    own_ref[...] = part[:height]
    whole = [k for k in range(1, blocks) if k != split]
    for k, ref in zip(whole, send_refs):
        ref[...] = part[k * height:(k + 1) * height].astype(bf16)
    block = part[split * height:(split + 1) * height].astype(bf16)
    even = is_even()
    same_ref[...] = jnp.where(even, block[:rows], block[rows:])
    cross_ref[...] = jnp.where(even, block[rows:], block[:rows])


def sum_kernel(own_ref, *refs):
    *got_refs, keep_ref, send_ref = refs
    rows = keep_ref.shape[0]
    total = own_ref[...]
    for ref in got_refs:
        total = total + ref[...].astype(f32)
    even = is_even()
    keep_ref[...] = jnp.where(even, total[:rows], total[rows:])
    send_ref[...] = jnp.where(even, total[rows:], total[:rows]).astype(bf16)


def keep_kernel(raw_ref, keep_ref, same_ref, grad_ref, unit_ref, inverse_ref):
    rows = keep_ref.shape[0]
    txt = is_txt()
    unit, inverse = normalize(raw_ref[...])
    grad_ref[...] = back_norm(
        jnp.where(txt, unit[:rows], unit[rows:]),
        jnp.where(txt, inverse[:rows], inverse[rows:]),
        keep_ref[...] + same_ref[...].astype(f32),
    )
    unit_ref[...] = jnp.where(txt, unit[rows:], unit[:rows])
    inverse_ref[...] = jnp.where(txt, inverse[rows:], inverse[:rows])


def out_kernel(grad_ref, unit_ref, inverse_ref, cross_ref, got_ref, img_ref, txt_ref):
    txt = is_txt()
    total = got_ref[...].astype(f32) + cross_ref[...].astype(f32)
    keep = grad_ref[...]
    got = back_norm(unit_ref[...], inverse_ref[...], total)
    txt_ref[...] = jnp.where(txt, keep, got)
    img_ref[...] = jnp.where(txt, got, keep)


def local(image_embeds, text_embeds, pair_ids):
    rows, width = image_embeds.shape
    blocks = max(lax.axis_size("img") // 2, lax.axis_size("txt"))
    pair = jax.ShapeDtypeStruct((2 * rows, width), bf16)
    total = jax.ShapeDtypeStruct((2 * rows, width), f32)
    piece = jax.ShapeDtypeStruct((rows, width), bf16)
    single = jax.ShapeDtypeStruct((rows, width), f32)
    ids = pair_ids.reshape(1, -1)
    far_txt = core_swap(text_embeds)
    far_img = core_swap(image_embeds)
    near = jnp.concatenate([text_embeds, image_embeds])
    mine, other = call(sides_kernel, [pair] * 2, [near, far_txt, far_img])
    order = list(range(blocks - 1, 0, -1))
    mine = [mine] + [chip_swap(mine, k) for k in order]
    packed = jax.ShapeDtypeStruct((2 * rows * (width // LANES) + 16, LANES), bf16)
    (packed,) = call(pack_kernel, [packed], [ids, mine[-1]])
    other = [other] + [core_swap(block) for block in [*mine[1:-1], packed]]
    count = blocks * 2 * rows
    (most,) = call(
        functools.partial(most_kernel, blocks),
        [jax.ShapeDtypeStruct((count, count - 2 * rows), f32)],
        [*mine, *other[:-1]],
        cost=LONG,
    )
    split = min(2, blocks - 1)
    own, same, cross, *send = call(
        functools.partial(rest_kernel, blocks, split),
        [total] + [piece] * 2 + [pair] * (blocks - 2),
        [ids, most, *mine, *other],
    )
    far = order.pop(split - 1)
    got = [chip_swap(block, k) for k, block in zip(order, send)]
    same = chip_swap(same, far)
    cross = chip_swap(cross, far, cross=1)
    keep, send = call(sum_kernel, [single, piece], [own, *got])
    got = core_swap(send)
    column = jax.ShapeDtypeStruct((rows, 1), f32)
    kept = call(keep_kernel, [single, single, column], [near, keep, same], cost=LONG)
    return tuple(call(out_kernel, [single] * 2, [*kept, cross, got]))


def solution(mesh):
    return jax.shard_map(
        local,
        mesh=mesh,
        in_specs=(P(("img", "txt"), None), P(("txt", "img"), None), P("img")),
        out_specs=(P(("img", "txt"), None), P(("txt", "img"), None)),
        check_vma=False,
    )
```

```python
import functools

import jax
import jax.numpy as jnp
from jax import lax
from jax.experimental import pallas as pl
from jax.experimental.pallas import tpu as pltpu
from jax.sharding import PartitionSpec as P

scale_logit = 8.0
shift_logit = -4.0
epsilon = 1e-06
f32 = jnp.float32
bf16 = jnp.bfloat16
VMEM = pl.BlockSpec(memory_space=pltpu.VMEM)
LONG = pl.CostEstimate(flops=10**10, bytes_accessed=10**7, transcendentals=0)


def normalize(raw):
    values = raw.astype(f32)
    inverse = lax.rsqrt(jnp.sum(values * values, axis=-1, keepdims=True) + epsilon)
    return (values * inverse, inverse)


def back_norm(unit, inverse, grad):
    inner = jnp.sum(unit * grad, axis=-1, keepdims=True)
    return inverse * (grad - unit * inner)


def pair_coeff(logit, same):
    label = jnp.where(same, 1.0, -1.0).astype(f32)
    return (-scale_logit * label * jax.nn.sigmoid(-label * logit)).astype(bf16)


def core_swap(block):
    size = lax.axis_size("img")
    return lax.ppermute(block, "img", [(i, i ^ 1) for i in range(size)])


def chip_swap(block, distance, cross=0):
    n_img, n_txt = lax.axis_size("img"), lax.axis_size("txt")
    pairs = []
    for img in range(n_img):
        for txt in range(n_txt):
            if img % 2 == 0 and distance < n_img // 2:
                pairs.append((img * n_txt + txt, (img ^ (2 * distance) ^ cross) * n_txt + txt))
            if img % 2 == 1 and distance < n_txt:
                pairs.append((img * n_txt + txt, (img ^ cross) * n_txt + (txt ^ distance)))
    return lax.ppermute(block, ("img", "txt"), pairs)


def is_even():
    return lax.axis_index("img") % 2 == 0


def call(kernel, outs, args, cost=None):
    sizes = [a.size * a.dtype.itemsize for a in list(args) + list(outs)]
    return pl.pallas_call(
        kernel,
        out_shape=outs,
        in_specs=[VMEM] * len(args),
        out_specs=[VMEM] * len(outs),
        cost_estimate=cost,
        compiler_params=pltpu.CompilerParams(
            vmem_limit_bytes=min(48 * 2**20, 8 * 2**20 + 6 * sum(sizes))
        ),
    )(*args)


def sides_kernel(own_ref, txt_ref, img_ref, mine_ref, other_ref):
    rows = txt_ref.shape[0]
    even = is_even()
    own = normalize(own_ref[...])[0].astype(bf16)
    own_txt, own_img = own[:rows], own[rows:]
    far_txt = normalize(txt_ref[...])[0].astype(bf16)
    far_img = normalize(img_ref[...])[0].astype(bf16)
    mine_ref[:rows, :] = jnp.where(even, own_txt, far_img)
    mine_ref[rows:, :] = jnp.where(even, far_txt, own_img)
    other_ref[:rows, :] = jnp.where(even, own_img, far_txt)
    other_ref[rows:, :] = jnp.where(even, far_img, own_txt)


def row_ids(rows, ids, far_ids, count):
    me_img = lax.axis_index("img")
    me_txt = lax.axis_index("txt")
    n_img = lax.axis_size("img")
    row = lax.broadcasted_iota(jnp.int32, (count, 1), 0)
    block, core, j = row // (2 * rows), row // rows % 2, row % rows
    chip = jnp.where(block == 0, 0, count // (2 * rows) - block)
    txt_ids = (me_txt * n_img + (((me_img // 2) ^ chip) * 2 + core)) * rows + j
    source = (me_txt ^ chip) * rows + j
    here = lax.broadcasted_iota(jnp.int32, (count, ids.shape[1]), 1) == source
    per_core = jnp.where(core == me_img % 2, ids, far_ids)
    img_ids = jnp.sum(jnp.where(here, per_core, 0), axis=1, keepdims=True)
    return txt_ids, img_ids


def side_ids(rows, ids, far_ids, count):
    even = is_even()
    txt_ids, img_ids = row_ids(rows, ids, far_ids, count)
    other_ids = jnp.where(even, img_ids, txt_ids)
    diagonal = lax.broadcasted_iota(jnp.int32, (count, count), 0) == lax.broadcasted_iota(
        jnp.int32, (count, count), 1
    )
    other_ids = jnp.sum(jnp.where(diagonal, other_ids, 0), axis=0, keepdims=True)
    return jnp.where(even, txt_ids, img_ids), other_ids


def scores_of(mine_refs, other_refs):
    mine = jnp.concatenate([ref[...] for ref in mine_refs], axis=0)
    other = jnp.concatenate([ref[...] for ref in other_refs], axis=0)
    return lax.dot_general(mine, other, (((1,), (1,)), ((), ())), preferred_element_type=f32)


def pair_kernel(blocks, split, ids_ref, far_ids_ref, *refs):
    mine_refs, other_refs = refs[:blocks], refs[blocks:2 * blocks]
    own_ref, same_ref, cross_ref, *send_refs = refs[2 * blocks:]
    height = own_ref.shape[0]
    rows = height // 2
    mine_ids, other_ids = side_ids(rows, ids_ref[...], far_ids_ref[...], blocks * height)
    scores = scores_of(mine_refs, other_refs)
    coeff = pair_coeff(scale_logit * scores + shift_logit, mine_ids == other_ids)
    other = jnp.concatenate([ref[...] for ref in other_refs], axis=0)
    part = jnp.dot(coeff, other, preferred_element_type=f32)
    own_ref[...] = part[:height]
    whole = [k for k in range(1, blocks) if k != split]
    for k, ref in zip(whole, send_refs):
        ref[...] = part[k * height:(k + 1) * height].astype(bf16)
    block = part[split * height:(split + 1) * height].astype(bf16)
    even = is_even()
    same_ref[...] = jnp.where(even, block[:rows], block[rows:])
    cross_ref[...] = jnp.where(even, block[rows:], block[:rows])


def sum_kernel(own_ref, *refs):
    *got_refs, keep_ref, send_ref = refs
    rows = keep_ref.shape[0]
    total = own_ref[...]
    for ref in got_refs:
        total = total + ref[...].astype(f32)
    even = is_even()
    keep_ref[...] = jnp.where(even, total[:rows], total[rows:])
    send_ref[...] = jnp.where(even, total[rows:], total[:rows]).astype(bf16)


def keep_kernel(raw_ref, keep_ref, same_ref, grad_ref, unit_ref, inverse_ref):
    rows = keep_ref.shape[0]
    even = is_even()
    unit, inverse = normalize(raw_ref[...])
    grad_ref[...] = back_norm(
        jnp.where(even, unit[:rows], unit[rows:]),
        jnp.where(even, inverse[:rows], inverse[rows:]),
        keep_ref[...] + same_ref[...].astype(f32),
    )
    unit_ref[...] = jnp.where(even, unit[rows:], unit[:rows])
    inverse_ref[...] = jnp.where(even, inverse[rows:], inverse[:rows])


def out_kernel(grad_ref, unit_ref, inverse_ref, cross_ref, got_ref, img_ref, txt_ref):
    even = is_even()
    total = got_ref[...].astype(f32) + cross_ref[...].astype(f32)
    keep = grad_ref[...]
    got = back_norm(unit_ref[...], inverse_ref[...], total)
    txt_ref[...] = jnp.where(even, keep, got)
    img_ref[...] = jnp.where(even, got, keep)


def local(image_embeds, text_embeds, pair_ids):
    rows, width = image_embeds.shape
    blocks = max(lax.axis_size("img") // 2, lax.axis_size("txt"))
    pair = jax.ShapeDtypeStruct((2 * rows, width), bf16)
    total = jax.ShapeDtypeStruct((2 * rows, width), f32)
    piece = jax.ShapeDtypeStruct((rows, width), bf16)
    single = jax.ShapeDtypeStruct((rows, width), f32)
    ids = pair_ids.reshape(1, -1)
    far_txt = core_swap(text_embeds)
    far_img = core_swap(image_embeds)
    near = jnp.concatenate([text_embeds, image_embeds])
    mine, other = call(sides_kernel, [pair] * 2, [near, far_txt, far_img])
    order = list(range(blocks - 1, 0, -1))
    mine = [mine] + [chip_swap(mine, k) for k in order]
    other = [other, *[core_swap(block) for block in mine[1:-1]], chip_swap(mine[0], 1, cross=1)]
    split = min(2, blocks - 1)
    own, same, cross, *send = call(
        functools.partial(pair_kernel, blocks, split),
        [total] + [piece] * 2 + [pair] * (blocks - 2),
        [ids, core_swap(ids), *mine, *other],
    )
    far = order.pop(split - 1)
    got = [chip_swap(block, k) for k, block in zip(order, send)]
    same = chip_swap(same, far)
    cross = chip_swap(cross, far, cross=1)
    keep, send = call(sum_kernel, [single, piece], [own, *got])
    got = core_swap(send)
    column = jax.ShapeDtypeStruct((rows, 1), f32)
    kept = call(keep_kernel, [single, single, column], [near, keep, same], cost=LONG)
    return tuple(call(out_kernel, [single] * 2, [*kept, cross, got]))


def solution(mesh):
    return jax.shard_map(
        local,
        mesh=mesh,
        in_specs=(P(("img", "txt"), None), P(("txt", "img"), None), P("img")),
        out_specs=(P(("img", "txt"), None), P(("txt", "img"), None)),
        check_vma=False,
    )
```

```python
import functools

import jax
import jax.numpy as jnp
from jax import lax
from jax.experimental import pallas as pl
from jax.experimental.pallas import tpu as pltpu
from jax.sharding import PartitionSpec as P

scale_logit = 8.0
shift_logit = -4.0
epsilon = 1e-06
f32 = jnp.float32
bf16 = jnp.bfloat16
VMEM = pl.BlockSpec(memory_space=pltpu.VMEM)
LONG = pl.CostEstimate(flops=10**10, bytes_accessed=10**7, transcendentals=0)


def normalize(raw):
    values = raw.astype(f32)
    inverse = lax.rsqrt(jnp.sum(values * values, axis=-1, keepdims=True) + epsilon)
    return (values * inverse, inverse)


def back_norm(unit, inverse, grad):
    inner = jnp.sum(unit * grad, axis=-1, keepdims=True)
    return inverse * (grad - unit * inner)


def pair_coeff(logit, same):
    label = jnp.where(same, 1.0, -1.0).astype(f32)
    return (-scale_logit * label * jax.nn.sigmoid(-label * logit)).astype(bf16)


def core_swap(block):
    size = lax.axis_size("img")
    return lax.ppermute(block, "img", [(i, i ^ 1) for i in range(size)])


def chip_swap(block, distance, cross=0):
    n_img, n_txt = lax.axis_size("img"), lax.axis_size("txt")
    pairs = []
    for img in range(n_img):
        for txt in range(n_txt):
            if img % 2 == 0 and distance < n_img // 2:
                pairs.append((img * n_txt + txt, (img ^ (2 * distance) ^ cross) * n_txt + txt))
            if img % 2 == 1 and distance < n_txt:
                pairs.append((img * n_txt + txt, (img ^ cross) * n_txt + (txt ^ distance)))
    return lax.ppermute(block, ("img", "txt"), pairs)


def is_even():
    return lax.axis_index("img") % 2 == 0


def call(kernel, outs, args, cost=None):
    sizes = [a.size * a.dtype.itemsize for a in list(args) + list(outs)]
    return pl.pallas_call(
        kernel,
        out_shape=outs,
        in_specs=[VMEM] * len(args),
        out_specs=[VMEM] * len(outs),
        cost_estimate=cost,
        compiler_params=pltpu.CompilerParams(
            vmem_limit_bytes=min(48 * 2**20, 8 * 2**20 + 6 * sum(sizes))
        ),
    )(*args)


def sides_kernel(own_ref, txt_ref, img_ref, mine_ref, other_ref):
    rows = txt_ref.shape[0]
    even = is_even()
    own = normalize(own_ref[...])[0].astype(bf16)
    own_txt, own_img = own[:rows], own[rows:]
    far_txt = normalize(txt_ref[...])[0].astype(bf16)
    far_img = normalize(img_ref[...])[0].astype(bf16)
    mine_ref[:rows, :] = jnp.where(even, own_txt, far_img)
    mine_ref[rows:, :] = jnp.where(even, far_txt, own_img)
    other_ref[:rows, :] = jnp.where(even, own_img, far_txt)
    other_ref[rows:, :] = jnp.where(even, far_img, own_txt)


def row_ids(rows, ids, far_ids, count):
    me_img = lax.axis_index("img")
    me_txt = lax.axis_index("txt")
    n_img = lax.axis_size("img")
    row = lax.broadcasted_iota(jnp.int32, (count, 1), 0)
    block, core, j = row // (2 * rows), row // rows % 2, row % rows
    chip = jnp.where(block == 0, 0, count // (2 * rows) - block)
    txt_ids = (me_txt * n_img + (((me_img // 2) ^ chip) * 2 + core)) * rows + j
    source = (me_txt ^ chip) * rows + j
    here = lax.broadcasted_iota(jnp.int32, (count, ids.shape[1]), 1) == source
    per_core = jnp.where(core == me_img % 2, ids, far_ids)
    img_ids = jnp.sum(jnp.where(here, per_core, 0), axis=1, keepdims=True)
    return txt_ids, img_ids


def side_ids(rows, ids, far_ids, count):
    even = is_even()
    txt_ids, img_ids = row_ids(rows, ids, far_ids, count)
    other_ids = jnp.where(even, img_ids, txt_ids)
    diagonal = lax.broadcasted_iota(jnp.int32, (count, count), 0) == lax.broadcasted_iota(
        jnp.int32, (count, count), 1
    )
    other_ids = jnp.sum(jnp.where(diagonal, other_ids, 0), axis=0, keepdims=True)
    return jnp.where(even, txt_ids, img_ids), other_ids


def scores_of(mine_refs, other_refs):
    mine = jnp.concatenate([ref[...] for ref in mine_refs], axis=0)
    other = jnp.concatenate([ref[...] for ref in other_refs], axis=0)
    return lax.dot_general(mine, other, (((1,), (1,)), ((), ())), preferred_element_type=f32)


def pair_kernel(blocks, split, ids_ref, far_ids_ref, *refs):
    mine_refs, other_refs = refs[:blocks], refs[blocks:2 * blocks]
    own_ref, same_ref, cross_ref, *send_refs = refs[2 * blocks:]
    height = own_ref.shape[0]
    rows = height // 2
    mine_ids, other_ids = side_ids(rows, ids_ref[...], far_ids_ref[...], blocks * height)
    scores = scores_of(mine_refs, other_refs)
    coeff = pair_coeff(scale_logit * scores + shift_logit, mine_ids == other_ids)
    other = jnp.concatenate([ref[...] for ref in other_refs], axis=0)
    part = jnp.dot(coeff, other, preferred_element_type=f32)
    own_ref[...] = part[:height]
    whole = [k for k in range(1, blocks) if k != split]
    for k, ref in zip(whole, send_refs):
        ref[...] = part[k * height:(k + 1) * height].astype(bf16)
    block = part[split * height:(split + 1) * height].astype(bf16)
    even = is_even()
    same_ref[...] = jnp.where(even, block[:rows], block[rows:])
    cross_ref[...] = jnp.where(even, block[rows:], block[:rows])


def sum_kernel(own_ref, *refs):
    *got_refs, keep_ref, send_ref = refs
    rows = keep_ref.shape[0]
    total = own_ref[...]
    for ref in got_refs:
        total = total + ref[...].astype(f32)
    even = is_even()
    keep_ref[...] = jnp.where(even, total[:rows], total[rows:])
    send_ref[...] = jnp.where(even, total[rows:], total[:rows]).astype(bf16)


def unit_kernel(raw_ref, cross_ref, unit_ref, inverse_ref, rest_ref):
    unit_ref[...], inverse_ref[...] = normalize(raw_ref[...])
    rest_ref[...] = cross_ref[...].astype(f32)


def out_kernel(unit_ref, inverse_ref, rest_ref, keep_ref, same_ref, got_ref, img_ref, txt_ref):
    rows = keep_ref.shape[0]
    even = is_even()
    keep = keep_ref[...] + same_ref[...].astype(f32)
    got = got_ref[...].astype(f32) + rest_ref[...]
    unit, inverse = unit_ref[...], inverse_ref[...]
    txt_ref[...] = back_norm(unit[:rows], inverse[:rows], jnp.where(even, keep, got))
    img_ref[...] = back_norm(unit[rows:], inverse[rows:], jnp.where(even, got, keep))


def local(image_embeds, text_embeds, pair_ids):
    rows, width = image_embeds.shape
    blocks = max(lax.axis_size("img") // 2, lax.axis_size("txt"))
    pair = jax.ShapeDtypeStruct((2 * rows, width), bf16)
    total = jax.ShapeDtypeStruct((2 * rows, width), f32)
    piece = jax.ShapeDtypeStruct((rows, width), bf16)
    single = jax.ShapeDtypeStruct((rows, width), f32)
    ids = pair_ids.reshape(1, -1)
    far_txt = core_swap(text_embeds)
    far_img = core_swap(image_embeds)
    near = jnp.concatenate([text_embeds, image_embeds])
    mine, other = call(sides_kernel, [pair] * 2, [near, far_txt, far_img])
    order = list(range(blocks - 1, 0, -1))
    mine = [mine] + [chip_swap(mine, k) for k in order]
    other = [other, *[core_swap(block) for block in mine[1:-1]], chip_swap(mine[0], 1, cross=1)]
    split = min(2, blocks - 1)
    own, same, cross, *send = call(
        functools.partial(pair_kernel, blocks, split),
        [total] + [piece] * 2 + [pair] * (blocks - 2),
        [ids, core_swap(ids), *mine, *other],
    )
    far = order.pop(split - 1)
    got = [chip_swap(block, k) for k, block in zip(order, send)]
    cross = chip_swap(cross, far, cross=1)
    same = chip_swap(same, far)
    keep, send = call(sum_kernel, [single, piece], [own, *got])
    got = core_swap(send)
    column = jax.ShapeDtypeStruct((2 * rows, 1), f32)
    ready = call(unit_kernel, [total, column, single], [near, cross], cost=LONG)
    return tuple(call(out_kernel, [single] * 2, [*ready, keep, same, got]))


def solution(mesh):
    return jax.shard_map(
        local,
        mesh=mesh,
        in_specs=(P(("img", "txt"), None), P(("txt", "img"), None), P("img")),
        out_specs=(P(("img", "txt"), None), P(("txt", "img"), None)),
        check_vma=False,
    )
```

```python
import functools

import jax
import jax.numpy as jnp
from jax import lax
from jax.experimental import pallas as pl
from jax.experimental.pallas import tpu as pltpu
from jax.sharding import PartitionSpec as P

scale_logit = 8.0
shift_logit = -4.0
epsilon = 1e-06
f32 = jnp.float32
bf16 = jnp.bfloat16
VMEM = pl.BlockSpec(memory_space=pltpu.VMEM)
LONG = pl.CostEstimate(flops=10**10, bytes_accessed=10**7, transcendentals=0)


def normalize(raw):
    values = raw.astype(f32)
    inverse = lax.rsqrt(jnp.sum(values * values, axis=-1, keepdims=True) + epsilon)
    return (values * inverse, inverse)


def back_norm(unit, inverse, grad):
    inner = jnp.sum(unit * grad, axis=-1, keepdims=True)
    return inverse * (grad - unit * inner)


def pair_coeff(logit, same):
    label = jnp.where(same, 1.0, -1.0).astype(f32)
    return (-scale_logit * label * jax.nn.sigmoid(-label * logit)).astype(bf16)


def core_swap(block):
    size = lax.axis_size("img")
    return lax.ppermute(block, "img", [(i, i ^ 1) for i in range(size)])


def chip_swap(block, txt_distance, img_distance, cross=0):
    n_img, n_txt = lax.axis_size("img"), lax.axis_size("txt")
    pairs = []
    for img in range(n_img):
        for txt in range(n_txt):
            if img % 2 == 0 and txt_distance < n_img // 2:
                target = (img ^ (2 * txt_distance) ^ cross) * n_txt + txt
                pairs.append((img * n_txt + txt, target))
            if img % 2 == 1 and img_distance < n_txt:
                target = (img ^ cross) * n_txt + (txt ^ img_distance)
                pairs.append((img * n_txt + txt, target))
    return lax.ppermute(block, ("img", "txt"), pairs)


def is_even():
    return lax.axis_index("img") % 2 == 0


def call(kernel, outs, args, cost=None):
    sizes = [a.size * a.dtype.itemsize for a in list(args) + list(outs)]
    return pl.pallas_call(
        kernel,
        out_shape=outs,
        in_specs=[VMEM] * len(args),
        out_specs=[VMEM] * len(outs),
        cost_estimate=cost,
        compiler_params=pltpu.CompilerParams(
            vmem_limit_bytes=min(48 * 2**20, 8 * 2**20 + 6 * sum(sizes))
        ),
    )(*args)


def sides_kernel(own_ref, txt_ref, img_ref, mine_ref, other_ref):
    rows = txt_ref.shape[0]
    even = is_even()
    own = normalize(own_ref[...])[0].astype(bf16)
    own_txt, own_img = own[:rows], own[rows:]
    far_txt = normalize(txt_ref[...])[0].astype(bf16)
    far_img = normalize(img_ref[...])[0].astype(bf16)
    mine_ref[:rows, :] = jnp.where(even, own_txt, far_img)
    mine_ref[rows:, :] = jnp.where(even, far_txt, own_img)
    other_ref[:rows, :] = jnp.where(even, own_img, far_txt)
    other_ref[rows:, :] = jnp.where(even, far_img, own_txt)


def row_ids(rows, ids, far_ids, count):
    me_img = lax.axis_index("img")
    me_txt = lax.axis_index("txt")
    n_img = lax.axis_size("img")
    row = lax.broadcasted_iota(jnp.int32, (count, 1), 0)
    block, core, j = row // (2 * rows), row // rows % 2, row % rows
    chip = jnp.where(block == 0, 0, count // (2 * rows) - block)
    txt_ids = (me_txt * n_img + (((me_img // 2) ^ chip) * 2 + core)) * rows + j
    source = (me_txt ^ chip) * rows + j
    here = lax.broadcasted_iota(jnp.int32, (count, ids.shape[1]), 1) == source
    per_core = jnp.where(core == me_img % 2, ids, far_ids)
    img_ids = jnp.sum(jnp.where(here, per_core, 0), axis=1, keepdims=True)
    return txt_ids, img_ids


def side_ids(rows, ids, far_ids, count):
    even = is_even()
    txt_ids, img_ids = row_ids(rows, ids, far_ids, count)
    other_ids = jnp.where(even, img_ids, txt_ids)
    diagonal = lax.broadcasted_iota(jnp.int32, (count, count), 0) == lax.broadcasted_iota(
        jnp.int32, (count, count), 1
    )
    other_ids = jnp.sum(jnp.where(diagonal, other_ids, 0), axis=0, keepdims=True)
    return jnp.where(even, txt_ids, img_ids), other_ids


def scores_of(mine_refs, other_refs):
    mine = jnp.concatenate([ref[...] for ref in mine_refs], axis=0)
    other = jnp.concatenate([ref[...] for ref in other_refs], axis=0)
    return lax.dot_general(mine, other, (((1,), (1,)), ((), ())), preferred_element_type=f32)


def pair_kernel(blocks, plan, ids_ref, far_ids_ref, *refs):
    mine_refs, other_refs = refs[:blocks], refs[blocks:2 * blocks]
    own_ref, same_ref, cross_ref, *send_refs = refs[2 * blocks:]
    height = own_ref.shape[0]
    rows = height // 2
    mine_ids, other_ids = side_ids(rows, ids_ref[...], far_ids_ref[...], blocks * height)
    scores = scores_of(mine_refs, other_refs)
    coeff = pair_coeff(scale_logit * scores + shift_logit, mine_ids == other_ids)
    other = jnp.concatenate([ref[...] for ref in other_refs], axis=0)
    part = jnp.dot(coeff, other, preferred_element_type=f32)
    own_ref[...] = part[:height]
    even = is_even()

    def block_of(txt_distance, img_distance):
        txt, img = [
            part[(blocks - k) * height:(blocks - k + 1) * height] for k in (txt_distance, img_distance)
        ]
        return jnp.where(even, txt, img).astype(bf16)

    *whole, split = plan
    for distances, ref in zip(whole, send_refs):
        ref[...] = block_of(*distances)
    block = block_of(*split)
    same_ref[...] = jnp.where(even, block[:rows], block[rows:])
    cross_ref[...] = jnp.where(even, block[rows:], block[:rows])


def sum_kernel(own_ref, *refs):
    *got_refs, keep_ref, send_ref = refs
    rows = keep_ref.shape[0]
    total = own_ref[...]
    for ref in got_refs:
        total = total + ref[...].astype(f32)
    even = is_even()
    keep_ref[...] = jnp.where(even, total[:rows], total[rows:])
    send_ref[...] = jnp.where(even, total[rows:], total[:rows]).astype(bf16)


def unit_kernel(raw_ref, cross_ref, unit_ref, inverse_ref, rest_ref):
    unit_ref[...], inverse_ref[...] = normalize(raw_ref[...])
    rest_ref[...] = cross_ref[...].astype(f32)


def out_kernel(unit_ref, inverse_ref, rest_ref, keep_ref, same_ref, got_ref, img_ref, txt_ref):
    rows = keep_ref.shape[0]
    even = is_even()
    keep = keep_ref[...] + same_ref[...].astype(f32)
    got = got_ref[...].astype(f32) + rest_ref[...]
    unit, inverse = unit_ref[...], inverse_ref[...]
    txt_ref[...] = back_norm(unit[:rows], inverse[:rows], jnp.where(even, keep, got))
    img_ref[...] = back_norm(unit[rows:], inverse[rows:], jnp.where(even, got, keep))


def local(image_embeds, text_embeds, pair_ids):
    rows, width = image_embeds.shape
    blocks = max(lax.axis_size("img") // 2, lax.axis_size("txt"))
    pair = jax.ShapeDtypeStruct((2 * rows, width), bf16)
    total = jax.ShapeDtypeStruct((2 * rows, width), f32)
    piece = jax.ShapeDtypeStruct((rows, width), bf16)
    single = jax.ShapeDtypeStruct((rows, width), f32)
    ids = pair_ids.reshape(1, -1)
    far_txt = core_swap(text_embeds)
    far_img = core_swap(image_embeds)
    near = jnp.concatenate([text_embeds, image_embeds])
    mine, other = call(sides_kernel, [pair] * 2, [near, far_txt, far_img])
    order = list(range(blocks - 1, 0, -1))
    mine = [mine] + [chip_swap(mine, k, k) for k in order]
    other = [other, *[core_swap(block) for block in mine[1:-1]], chip_swap(mine[0], 1, 1, cross=1)]
    txt_plan = order[::-1]
    img_plan = order[:1] + order[2:] + order[1:2]
    plan = list(zip(txt_plan, img_plan))
    own, same, cross, *send = call(
        functools.partial(pair_kernel, blocks, plan),
        [total] + [piece] * 2 + [pair] * (blocks - 2),
        [ids, core_swap(ids), *mine, *other],
    )
    got = [chip_swap(block, *distances) for distances, block in zip(plan, send)]
    cross = chip_swap(cross, *plan[-1], cross=1)
    same = chip_swap(same, *plan[-1])
    keep, send = call(sum_kernel, [single, piece], [own, *got])
    got = core_swap(send)
    column = jax.ShapeDtypeStruct((2 * rows, 1), f32)
    ready = call(unit_kernel, [total, column, single], [near, cross], cost=LONG)
    return tuple(call(out_kernel, [single] * 2, [*ready, keep, same, got]))


def solution(mesh):
    return jax.shard_map(
        local,
        mesh=mesh,
        in_specs=(P(("img", "txt"), None), P(("txt", "img"), None), P("img")),
        out_specs=(P(("img", "txt"), None), P(("txt", "img"), None)),
        check_vma=False,
    )
```

```python
import functools

import jax
import jax.numpy as jnp
from jax import lax
from jax.experimental import pallas as pl
from jax.experimental.pallas import tpu as pltpu
from jax.sharding import PartitionSpec as P

scale_logit = 8.0
shift_logit = -4.0
epsilon = 1e-06
f32 = jnp.float32
bf16 = jnp.bfloat16
VMEM = pl.BlockSpec(memory_space=pltpu.VMEM)
LONG = pl.CostEstimate(flops=10**10, bytes_accessed=10**7, transcendentals=0)


def normalize(raw):
    values = raw.astype(f32)
    inverse = lax.rsqrt(jnp.sum(values * values, axis=-1, keepdims=True) + epsilon)
    return (values * inverse, inverse)


def back_norm(unit, inverse, grad):
    inner = jnp.sum(unit * grad, axis=-1, keepdims=True)
    return inverse * (grad - unit * inner)


def pair_coeff(logit, same):
    label = jnp.where(same, 1.0, -1.0).astype(f32)
    return (-scale_logit * label * jax.nn.sigmoid(-label * logit)).astype(bf16)


def core_swap(block):
    size = lax.axis_size("img")
    return lax.ppermute(block, "img", [(i, i ^ 1) for i in range(size)])


def chip_swap(block, distance, cross=lambda txt: 0):
    n_img, n_txt = lax.axis_size("img"), lax.axis_size("txt")
    pairs = []
    for img in range(n_img):
        for txt in range(n_txt):
            other = cross(txt)
            if img % 2 == 0 and distance < n_img // 2:
                pairs.append((img * n_txt + txt, (img ^ (2 * distance) ^ other) * n_txt + txt))
            if img % 2 == 1 and distance < n_txt:
                pairs.append((img * n_txt + txt, (img ^ other) * n_txt + (txt ^ distance)))
    return lax.ppermute(block, ("img", "txt"), pairs)


def cross_first(distance):
    return (lax.axis_index("txt") % 2 == 0) | (distance % 2 == 1)


def is_even():
    return lax.axis_index("img") % 2 == 0


def call(kernel, outs, args, cost=None):
    sizes = [a.size * a.dtype.itemsize for a in list(args) + list(outs)]
    return pl.pallas_call(
        kernel,
        out_shape=outs,
        in_specs=[VMEM] * len(args),
        out_specs=[VMEM] * len(outs),
        cost_estimate=cost,
        compiler_params=pltpu.CompilerParams(
            vmem_limit_bytes=min(48 * 2**20, 8 * 2**20 + 6 * sum(sizes))
        ),
    )(*args)


def sides_kernel(own_ref, txt_ref, img_ref, mine_ref, other_ref):
    rows = txt_ref.shape[0]
    even = is_even()
    own = normalize(own_ref[...])[0].astype(bf16)
    own_txt, own_img = own[:rows], own[rows:]
    far_txt = normalize(txt_ref[...])[0].astype(bf16)
    far_img = normalize(img_ref[...])[0].astype(bf16)
    mine_ref[:rows, :] = jnp.where(even, own_txt, far_img)
    mine_ref[rows:, :] = jnp.where(even, far_txt, own_img)
    other_ref[:rows, :] = jnp.where(even, own_img, far_txt)
    other_ref[rows:, :] = jnp.where(even, far_img, own_txt)


def row_ids(rows, ids, far_ids, count):
    me_img = lax.axis_index("img")
    me_txt = lax.axis_index("txt")
    n_img = lax.axis_size("img")
    row = lax.broadcasted_iota(jnp.int32, (count, 1), 0)
    block, core, j = row // (2 * rows), row // rows % 2, row % rows
    chip = jnp.where(block == 0, 0, count // (2 * rows) - block)
    txt_ids = (me_txt * n_img + (((me_img // 2) ^ chip) * 2 + core)) * rows + j
    source = (me_txt ^ chip) * rows + j
    here = lax.broadcasted_iota(jnp.int32, (count, ids.shape[1]), 1) == source
    per_core = jnp.where(core == me_img % 2, ids, far_ids)
    img_ids = jnp.sum(jnp.where(here, per_core, 0), axis=1, keepdims=True)
    return txt_ids, img_ids


def side_ids(rows, ids, far_ids, count):
    even = is_even()
    txt_ids, img_ids = row_ids(rows, ids, far_ids, count)
    other_ids = jnp.where(even, img_ids, txt_ids)
    diagonal = lax.broadcasted_iota(jnp.int32, (count, count), 0) == lax.broadcasted_iota(
        jnp.int32, (count, count), 1
    )
    other_ids = jnp.sum(jnp.where(diagonal, other_ids, 0), axis=0, keepdims=True)
    return jnp.where(even, txt_ids, img_ids), other_ids


def scores_of(mine_refs, other_refs):
    mine = jnp.concatenate([ref[...] for ref in mine_refs], axis=0)
    other = jnp.concatenate([ref[...] for ref in other_refs], axis=0)
    return lax.dot_general(mine, other, (((1,), (1,)), ((), ())), preferred_element_type=f32)


def pair_kernel(blocks, split, ids_ref, far_ids_ref, *refs):
    mine_refs, other_refs = refs[:blocks], refs[blocks:2 * blocks]
    own_ref, first_ref, second_ref, *send_refs = refs[2 * blocks:]
    height = own_ref.shape[0]
    rows = height // 2
    mine_ids, other_ids = side_ids(rows, ids_ref[...], far_ids_ref[...], blocks * height)
    scores = scores_of(mine_refs, other_refs)
    coeff = pair_coeff(scale_logit * scores + shift_logit, mine_ids == other_ids)
    other = jnp.concatenate([ref[...] for ref in other_refs], axis=0)
    part = jnp.dot(coeff, other, preferred_element_type=f32)
    own_ref[...] = part[:height]
    whole = [k for k in range(1, blocks) if k != split]
    for k, ref in zip(whole, send_refs):
        ref[...] = part[k * height:(k + 1) * height].astype(bf16)
    block = part[split * height:(split + 1) * height].astype(bf16)
    even = is_even()
    first = jnp.logical_xor(even, cross_first(blocks - split))
    first_ref[...] = jnp.where(first, block[:rows], block[rows:])
    second_ref[...] = jnp.where(first, block[rows:], block[:rows])


def sum_kernel(own_ref, *refs):
    *got_refs, keep_ref, send_ref = refs
    rows = keep_ref.shape[0]
    total = own_ref[...]
    for ref in got_refs:
        total = total + ref[...].astype(f32)
    even = is_even()
    keep_ref[...] = jnp.where(even, total[:rows], total[rows:])
    send_ref[...] = jnp.where(even, total[rows:], total[:rows]).astype(bf16)


def unit_kernel(raw_ref, first_ref, unit_ref, inverse_ref, rest_ref):
    unit_ref[...], inverse_ref[...] = normalize(raw_ref[...])
    rest_ref[...] = first_ref[...].astype(f32)


def out_kernel(
    far, unit_ref, inverse_ref, first_ref, keep_ref, second_ref, got_ref, img_ref, txt_ref
):
    rows = keep_ref.shape[0]
    even = is_even()
    first, second = first_ref[...], second_ref[...].astype(f32)
    cross = cross_first(far)
    keep = keep_ref[...] + jnp.where(cross, second, first)
    got = got_ref[...].astype(f32) + jnp.where(cross, first, second)
    unit, inverse = unit_ref[...], inverse_ref[...]
    txt_ref[...] = back_norm(unit[:rows], inverse[:rows], jnp.where(even, keep, got))
    img_ref[...] = back_norm(unit[rows:], inverse[rows:], jnp.where(even, got, keep))


def local(image_embeds, text_embeds, pair_ids):
    rows, width = image_embeds.shape
    blocks = max(lax.axis_size("img") // 2, lax.axis_size("txt"))
    pair = jax.ShapeDtypeStruct((2 * rows, width), bf16)
    total = jax.ShapeDtypeStruct((2 * rows, width), f32)
    piece = jax.ShapeDtypeStruct((rows, width), bf16)
    single = jax.ShapeDtypeStruct((rows, width), f32)
    ids = pair_ids.reshape(1, -1)
    far_txt = core_swap(text_embeds)
    far_img = core_swap(image_embeds)
    near = jnp.concatenate([text_embeds, image_embeds])
    mine, other = call(sides_kernel, [pair] * 2, [near, far_txt, far_img])
    order = list(range(blocks - 1, 0, -1))
    mine = [mine] + [chip_swap(mine, k) for k in order]
    other = [other, *[core_swap(block) for block in mine[1:-1]], chip_swap(mine[0], 1, lambda txt: 1)]
    split = min(2, blocks - 1)
    own, first, second, *send = call(
        functools.partial(pair_kernel, blocks, split),
        [total] + [piece] * 2 + [pair] * (blocks - 2),
        [ids, core_swap(ids), *mine, *other],
    )
    far = order.pop(split - 1)
    got = [chip_swap(block, k) for k, block in zip(order, send)]
    first = chip_swap(first, far, lambda txt: int(txt % 2 == 0 or far % 2 == 1))
    second = chip_swap(second, far, lambda txt: int(txt % 2 == 1 and far % 2 == 0))
    keep, send = call(sum_kernel, [single, piece], [own, *got])
    got = core_swap(send)
    column = jax.ShapeDtypeStruct((2 * rows, 1), f32)
    ready = call(unit_kernel, [total, column, single], [near, first], cost=LONG)
    kernel = functools.partial(out_kernel, far)
    return tuple(call(kernel, [single] * 2, [*ready, keep, second, got]))


def solution(mesh):
    return jax.shard_map(
        local,
        mesh=mesh,
        in_specs=(P(("img", "txt"), None), P(("txt", "img"), None), P("img")),
        out_specs=(P(("img", "txt"), None), P(("txt", "img"), None)),
        check_vma=False,
    )
```

```python
import functools

import jax
import jax.numpy as jnp
from jax import lax
from jax.experimental import pallas as pl
from jax.experimental.pallas import tpu as pltpu
from jax.sharding import PartitionSpec as P

scale_logit = 8.0
shift_logit = -4.0
epsilon = 1e-06
f32 = jnp.float32
bf16 = jnp.bfloat16
VMEM = pl.BlockSpec(memory_space=pltpu.VMEM)
LONG = pl.CostEstimate(flops=10**10, bytes_accessed=10**7, transcendentals=0)


def normalize(raw):
    values = raw.astype(f32)
    inverse = lax.rsqrt(jnp.sum(values * values, axis=-1, keepdims=True) + epsilon)
    return (values * inverse, inverse)


def back_norm(unit, inverse, grad):
    inner = jnp.sum(unit * grad, axis=-1, keepdims=True)
    return inverse * (grad - unit * inner)


def pair_coeff(logit, same):
    label = jnp.where(same, 1.0, -1.0).astype(f32)
    return (-scale_logit * label * jax.nn.sigmoid(-label * logit)).astype(bf16)


def core_swap(block):
    size = lax.axis_size("img")
    return lax.ppermute(block, "img", [(i, i ^ 1) for i in range(size)])


def chip_swap(block, distance, cross=lambda txt: 0):
    n_img, n_txt = lax.axis_size("img"), lax.axis_size("txt")
    pairs = []
    for img in range(n_img):
        for txt in range(n_txt):
            other = cross(txt)
            if img % 2 == 0 and distance < n_img // 2:
                pairs.append((img * n_txt + txt, (img ^ (2 * distance) ^ other) * n_txt + txt))
            if img % 2 == 1 and distance < n_txt:
                pairs.append((img * n_txt + txt, (img ^ other) * n_txt + (txt ^ distance)))
    return lax.ppermute(block, ("img", "txt"), pairs)


def cross_first(distance):
    return (lax.axis_index("txt") % 2 == 0) | (distance % 2 == 1)


def is_even():
    return lax.axis_index("img") % 2 == 0


def call(kernel, outs, args, cost=None):
    sizes = [a.size * a.dtype.itemsize for a in list(args) + list(outs)]
    return pl.pallas_call(
        kernel,
        out_shape=outs,
        in_specs=[VMEM] * len(args),
        out_specs=[VMEM] * len(outs),
        cost_estimate=cost,
        compiler_params=pltpu.CompilerParams(
            vmem_limit_bytes=min(48 * 2**20, 8 * 2**20 + 6 * sum(sizes))
        ),
    )(*args)


def sides_kernel(own_ref, txt_ref, img_ref, mine_ref, other_ref):
    rows = txt_ref.shape[0]
    even = is_even()
    own = normalize(own_ref[...])[0].astype(bf16)
    own_txt, own_img = own[:rows], own[rows:]
    far_txt = normalize(txt_ref[...])[0].astype(bf16)
    far_img = normalize(img_ref[...])[0].astype(bf16)
    mine_ref[:rows, :] = jnp.where(even, own_txt, far_img)
    mine_ref[rows:, :] = jnp.where(even, far_txt, own_img)
    other_ref[:rows, :] = jnp.where(even, own_img, far_txt)
    other_ref[rows:, :] = jnp.where(even, far_img, own_txt)


def row_ids(rows, ids, far_ids, count):
    me_img = lax.axis_index("img")
    me_txt = lax.axis_index("txt")
    n_img = lax.axis_size("img")
    row = lax.broadcasted_iota(jnp.int32, (count, 1), 0)
    block, core, j = row // (2 * rows), row // rows % 2, row % rows
    chip = jnp.where(block == 0, 0, count // (2 * rows) - block)
    txt_ids = (me_txt * n_img + (((me_img // 2) ^ chip) * 2 + core)) * rows + j
    source = (me_txt ^ chip) * rows + j
    here = lax.broadcasted_iota(jnp.int32, (count, ids.shape[1]), 1) == source
    per_core = jnp.where(core == me_img % 2, ids, far_ids)
    img_ids = jnp.sum(jnp.where(here, per_core, 0), axis=1, keepdims=True)
    return txt_ids, img_ids


def side_ids(rows, ids, far_ids, count):
    even = is_even()
    txt_ids, img_ids = row_ids(rows, ids, far_ids, count)
    other_ids = jnp.where(even, img_ids, txt_ids)
    diagonal = lax.broadcasted_iota(jnp.int32, (count, count), 0) == lax.broadcasted_iota(
        jnp.int32, (count, count), 1
    )
    other_ids = jnp.sum(jnp.where(diagonal, other_ids, 0), axis=0, keepdims=True)
    return jnp.where(even, txt_ids, img_ids), other_ids


def scores_of(mine_refs, other_refs):
    mine = jnp.concatenate([ref[...] for ref in mine_refs], axis=0)
    other = jnp.concatenate([ref[...] for ref in other_refs], axis=0)
    return lax.dot_general(mine, other, (((1,), (1,)), ((), ())), preferred_element_type=f32)


def pair_kernel(blocks, split, ids_ref, far_ids_ref, *refs):
    mine_refs, other_refs = refs[:blocks], refs[blocks:2 * blocks]
    own_ref, first_ref, second_ref, *send_refs = refs[2 * blocks:]
    height = own_ref.shape[0]
    rows = height // 2
    mine_ids, other_ids = side_ids(rows, ids_ref[...], far_ids_ref[...], blocks * height)
    scores = scores_of(mine_refs, other_refs)
    coeff = pair_coeff(scale_logit * scores + shift_logit, mine_ids == other_ids)
    other = jnp.concatenate([ref[...] for ref in other_refs], axis=0)
    part = jnp.dot(coeff, other, preferred_element_type=f32)
    own_ref[...] = part[:height]
    whole = [k for k in range(1, blocks) if k != split]
    for k, ref in zip(whole, send_refs):
        ref[...] = part[k * height:(k + 1) * height].astype(bf16)
    block = part[split * height:(split + 1) * height].astype(bf16)
    even = is_even()
    first = jnp.logical_xor(even, cross_first(blocks - split))
    first_ref[...] = jnp.where(first, block[:rows], block[rows:])
    second_ref[...] = jnp.where(first, block[rows:], block[:rows])


def sum_kernel(own_ref, *refs):
    *got_refs, keep_ref, send_ref = refs
    rows = keep_ref.shape[0]
    total = own_ref[...]
    for ref in got_refs:
        total = total + ref[...].astype(f32)
    even = is_even()
    keep_ref[...] = jnp.where(even, total[:rows], total[rows:])
    send_ref[...] = jnp.where(even, total[rows:], total[:rows]).astype(bf16)


def unit_kernel(raw_ref, first_ref, unit_ref, inverse_ref, rest_ref):
    unit_ref[...], inverse_ref[...] = normalize(raw_ref[...])
    rest_ref[...] = first_ref[...].astype(f32)


def out_kernel(
    far, unit_ref, inverse_ref, first_ref, keep_ref, second_ref, got_ref, img_ref, txt_ref
):
    rows = keep_ref.shape[0]
    even = is_even()
    first, second = first_ref[...], second_ref[...].astype(f32)
    cross = cross_first(far)
    keep = keep_ref[...] + jnp.where(cross, second, first)
    got = got_ref[...].astype(f32) + jnp.where(cross, first, second)
    unit, inverse = unit_ref[...], inverse_ref[...]
    txt_ref[...] = back_norm(unit[:rows], inverse[:rows], jnp.where(even, keep, got))
    img_ref[...] = back_norm(unit[rows:], inverse[rows:], jnp.where(even, got, keep))


def local(image_embeds, text_embeds, pair_ids):
    rows, width = image_embeds.shape
    blocks = max(lax.axis_size("img") // 2, lax.axis_size("txt"))
    pair = jax.ShapeDtypeStruct((2 * rows, width), bf16)
    total = jax.ShapeDtypeStruct((2 * rows, width), f32)
    piece = jax.ShapeDtypeStruct((rows, width), bf16)
    single = jax.ShapeDtypeStruct((rows, width), f32)
    ids = pair_ids.reshape(1, -1)
    far_txt = core_swap(text_embeds)
    far_img = core_swap(image_embeds)
    near = jnp.concatenate([text_embeds, image_embeds])
    mine, other = call(sides_kernel, [pair] * 2, [near, far_txt, far_img])
    order = list(range(blocks - 1, 0, -1))
    mine = [mine] + [chip_swap(mine, k) for k in order]
    other = [other, *[core_swap(block) for block in mine[1:-1]], chip_swap(mine[0], 1, lambda txt: 1)]
    split = blocks - 1
    own, first, second, *send = call(
        functools.partial(pair_kernel, blocks, split),
        [total] + [piece] * 2 + [pair] * (blocks - 2),
        [ids, core_swap(ids), *mine, *other],
    )
    far = order.pop(split - 1)
    got = [chip_swap(block, k) for k, block in zip(order, send)]
    first = chip_swap(first, far, lambda txt: int(txt % 2 == 0 or far % 2 == 1))
    second = chip_swap(second, far, lambda txt: int(txt % 2 == 1 and far % 2 == 0))
    keep, send = call(sum_kernel, [single, piece], [own, *got])
    got = core_swap(send)
    column = jax.ShapeDtypeStruct((2 * rows, 1), f32)
    ready = call(unit_kernel, [total, column, single], [near, first], cost=LONG)
    kernel = functools.partial(out_kernel, far)
    return tuple(call(kernel, [single] * 2, [*ready, keep, second, got]))


def solution(mesh):
    return jax.shard_map(
        local,
        mesh=mesh,
        in_specs=(P(("img", "txt"), None), P(("txt", "img"), None), P("img")),
        out_specs=(P(("img", "txt"), None), P(("txt", "img"), None)),
        check_vma=False,
    )
```

```python
import functools

import jax
import jax.numpy as jnp
from jax import lax
from jax.experimental import pallas as pl
from jax.experimental.pallas import tpu as pltpu
from jax.sharding import PartitionSpec as P

scale_logit = 8.0
shift_logit = -4.0
epsilon = 1e-06
f32 = jnp.float32
bf16 = jnp.bfloat16
VMEM = pl.BlockSpec(memory_space=pltpu.VMEM)
LONG = pl.CostEstimate(flops=10**10, bytes_accessed=10**7, transcendentals=0)


def normalize(raw):
    values = raw.astype(f32)
    inverse = lax.rsqrt(jnp.sum(values * values, axis=-1, keepdims=True) + epsilon)
    return (values * inverse, inverse)


def back_norm(unit, inverse, grad):
    inner = jnp.sum(unit * grad, axis=-1, keepdims=True)
    return inverse * (grad - unit * inner)


def pair_coeff(logit, same):
    label = jnp.where(same, 1.0, -1.0).astype(f32)
    return (-scale_logit * label * jax.nn.sigmoid(-label * logit)).astype(bf16)


def core_swap(block):
    size = lax.axis_size("img")
    return lax.ppermute(block, "img", [(i, i ^ 1) for i in range(size)])


def chip_swap(block, distance, cross=lambda txt: 0):
    n_img, n_txt = lax.axis_size("img"), lax.axis_size("txt")
    pairs = []
    for img in range(n_img):
        for txt in range(n_txt):
            other = cross(txt)
            if img % 2 == 0 and distance < n_img // 2:
                pairs.append((img * n_txt + txt, (img ^ (2 * distance) ^ other) * n_txt + txt))
            if img % 2 == 1 and distance < n_txt:
                pairs.append((img * n_txt + txt, (img ^ other) * n_txt + (txt ^ distance)))
    return lax.ppermute(block, ("img", "txt"), pairs)


def cross_first(distance):
    return (lax.axis_index("txt") % 2 == 0) | (distance % 2 == 1)


def is_even():
    return lax.axis_index("img") % 2 == 0


def call(kernel, outs, args, cost=None):
    sizes = [a.size * a.dtype.itemsize for a in list(args) + list(outs)]
    return pl.pallas_call(
        kernel,
        out_shape=outs,
        in_specs=[VMEM] * len(args),
        out_specs=[VMEM] * len(outs),
        cost_estimate=cost,
        compiler_params=pltpu.CompilerParams(
            vmem_limit_bytes=min(48 * 2**20, 8 * 2**20 + 6 * sum(sizes))
        ),
    )(*args)


def sides_kernel(own_ref, txt_ref, img_ref, mine_ref, other_ref):
    rows = txt_ref.shape[0]
    even = is_even()
    own = normalize(own_ref[...])[0].astype(bf16)
    own_txt, own_img = own[:rows], own[rows:]
    far_txt = normalize(txt_ref[...])[0].astype(bf16)
    far_img = normalize(img_ref[...])[0].astype(bf16)
    mine_ref[:rows, :] = jnp.where(even, own_txt, far_img)
    mine_ref[rows:, :] = jnp.where(even, far_txt, own_img)
    other_ref[:rows, :] = jnp.where(even, own_img, far_txt)
    other_ref[rows:, :] = jnp.where(even, far_img, own_txt)


def row_ids(rows, ids, far_ids, count):
    me_img = lax.axis_index("img")
    me_txt = lax.axis_index("txt")
    n_img = lax.axis_size("img")
    row = lax.broadcasted_iota(jnp.int32, (count, 1), 0)
    block, core, j = row // (2 * rows), row // rows % 2, row % rows
    chip = jnp.where(block == 0, 0, count // (2 * rows) - block)
    txt_ids = (me_txt * n_img + (((me_img // 2) ^ chip) * 2 + core)) * rows + j
    source = (me_txt ^ chip) * rows + j
    here = lax.broadcasted_iota(jnp.int32, (count, ids.shape[1]), 1) == source
    per_core = jnp.where(core == me_img % 2, ids, far_ids)
    img_ids = jnp.sum(jnp.where(here, per_core, 0), axis=1, keepdims=True)
    return txt_ids, img_ids


def side_ids(rows, ids, far_ids, count):
    even = is_even()
    txt_ids, img_ids = row_ids(rows, ids, far_ids, count)
    other_ids = jnp.where(even, img_ids, txt_ids)
    diagonal = lax.broadcasted_iota(jnp.int32, (count, count), 0) == lax.broadcasted_iota(
        jnp.int32, (count, count), 1
    )
    other_ids = jnp.sum(jnp.where(diagonal, other_ids, 0), axis=0, keepdims=True)
    return jnp.where(even, txt_ids, img_ids), other_ids


def scores_of(mine_refs, other_refs):
    mine = jnp.concatenate([ref[...] for ref in mine_refs], axis=0)
    other = jnp.concatenate([ref[...] for ref in other_refs], axis=0)
    return lax.dot_general(mine, other, (((1,), (1,)), ((), ())), preferred_element_type=f32)


def pair_kernel(blocks, split, ids_ref, far_ids_ref, *refs):
    mine_refs, other_refs = refs[:blocks], refs[blocks:2 * blocks]
    own_ref, first_ref, second_ref, *send_refs = refs[2 * blocks:]
    height = own_ref.shape[0]
    rows = height // 2
    mine_ids, other_ids = side_ids(rows, ids_ref[...], far_ids_ref[...], blocks * height)
    scores = scores_of(mine_refs, other_refs)
    coeff = pair_coeff(scale_logit * scores + shift_logit, mine_ids == other_ids)
    other = jnp.concatenate([ref[...] for ref in other_refs], axis=0)
    part = jnp.dot(coeff, other, preferred_element_type=f32)
    own_ref[...] = part[:height]
    whole = [k for k in range(1, blocks) if k != split]
    for k, ref in zip(whole, send_refs):
        ref[...] = part[k * height:(k + 1) * height].astype(bf16)
    block = part[split * height:(split + 1) * height].astype(bf16)
    even = is_even()
    first = jnp.logical_xor(even, cross_first(blocks - split))
    first_ref[...] = jnp.where(first, block[:rows], block[rows:])
    second_ref[...] = jnp.where(first, block[rows:], block[:rows])


def sum_kernel(own_ref, *refs):
    *got_refs, keep_ref, send_ref = refs
    rows = keep_ref.shape[0]
    total = own_ref[...]
    for ref in got_refs:
        total = total + ref[...].astype(f32)
    even = is_even()
    keep_ref[...] = jnp.where(even, total[:rows], total[rows:])
    send_ref[...] = jnp.where(even, total[rows:], total[:rows]).astype(bf16)


def unit_kernel(raw_ref, first_ref, unit_ref, inverse_ref, rest_ref):
    unit_ref[...], inverse_ref[...] = normalize(raw_ref[...])
    rest_ref[...] = first_ref[...].astype(f32)


def out_kernel(
    far, unit_ref, inverse_ref, first_ref, keep_ref, second_ref, got_ref, img_ref, txt_ref
):
    rows = keep_ref.shape[0]
    even = is_even()
    first, second = first_ref[...], second_ref[...].astype(f32)
    cross = cross_first(far)
    keep = keep_ref[...] + jnp.where(cross, second, first)
    got = got_ref[...].astype(f32) + jnp.where(cross, first, second)
    unit, inverse = unit_ref[...], inverse_ref[...]
    txt_ref[...] = back_norm(unit[:rows], inverse[:rows], jnp.where(even, keep, got))
    img_ref[...] = back_norm(unit[rows:], inverse[rows:], jnp.where(even, got, keep))


def local(image_embeds, text_embeds, pair_ids):
    rows, width = image_embeds.shape
    blocks = max(lax.axis_size("img") // 2, lax.axis_size("txt"))
    pair = jax.ShapeDtypeStruct((2 * rows, width), bf16)
    total = jax.ShapeDtypeStruct((2 * rows, width), f32)
    piece = jax.ShapeDtypeStruct((rows, width), bf16)
    single = jax.ShapeDtypeStruct((rows, width), f32)
    ids = pair_ids.reshape(1, -1)
    far_txt = core_swap(text_embeds)
    far_img = core_swap(image_embeds)
    near = jnp.concatenate([text_embeds, image_embeds])
    mine, other = call(sides_kernel, [pair] * 2, [near, far_txt, far_img])
    order = list(range(blocks - 1, 0, -1))
    mine = [mine] + [chip_swap(mine, k) for k in order]
    other = [other, *[core_swap(block) for block in mine[1:-1]], chip_swap(mine[0], 1, lambda txt: 1)]
    split = blocks - 1
    own, first, second, *send = call(
        functools.partial(pair_kernel, blocks, split),
        [total] + [piece] * 2 + [pair] * (blocks - 2),
        [ids, core_swap(ids), *mine, *other],
    )
    far = order.pop(split - 1)
    got = [chip_swap(block, k) for k, block in zip(order, send)][::-1]
    first = chip_swap(first, far, lambda txt: int(txt % 2 == 0 or far % 2 == 1))
    second = chip_swap(second, far, lambda txt: int(txt % 2 == 1 and far % 2 == 0))
    keep, send = call(sum_kernel, [single, piece], [own, *got])
    got = core_swap(send)
    column = jax.ShapeDtypeStruct((2 * rows, 1), f32)
    ready = call(unit_kernel, [total, column, single], [near, first], cost=LONG)
    kernel = functools.partial(out_kernel, far)
    return tuple(call(kernel, [single] * 2, [*ready, keep, second, got]))


def solution(mesh):
    return jax.shard_map(
        local,
        mesh=mesh,
        in_specs=(P(("img", "txt"), None), P(("txt", "img"), None), P("img")),
        out_specs=(P(("img", "txt"), None), P(("txt", "img"), None)),
        check_vma=False,
    )
```

```python
import functools

import jax
import jax.numpy as jnp
from jax import lax
from jax.experimental import pallas as pl
from jax.experimental.pallas import tpu as pltpu
from jax.sharding import PartitionSpec as P

scale_logit = 8.0
shift_logit = -4.0
epsilon = 1e-06
f32 = jnp.float32
bf16 = jnp.bfloat16
VMEM = pl.BlockSpec(memory_space=pltpu.VMEM)
LONG = pl.CostEstimate(flops=10**10, bytes_accessed=10**7, transcendentals=0)


def normalize(raw):
    values = raw.astype(f32)
    inverse = lax.rsqrt(jnp.sum(values * values, axis=-1, keepdims=True) + epsilon)
    return (values * inverse, inverse)


def back_norm(unit, inverse, grad):
    inner = jnp.sum(unit * grad, axis=-1, keepdims=True)
    return inverse * (grad - unit * inner)


def pair_coeff(logit, same):
    label = jnp.where(same, 1.0, -1.0).astype(f32)
    return (-scale_logit * label * jax.nn.sigmoid(-label * logit)).astype(bf16)


def core_swap(block):
    size = lax.axis_size("img")
    return lax.ppermute(block, "img", [(i, i ^ 1) for i in range(size)])


def chip_swap(block, distance, cross=lambda txt: 0):
    n_img, n_txt = lax.axis_size("img"), lax.axis_size("txt")
    pairs = []
    for img in range(n_img):
        for txt in range(n_txt):
            other = cross(txt)
            if img % 2 == 0 and distance < n_img // 2:
                pairs.append((img * n_txt + txt, (img ^ (2 * distance) ^ other) * n_txt + txt))
            if img % 2 == 1 and distance < n_txt:
                pairs.append((img * n_txt + txt, (img ^ other) * n_txt + (txt ^ distance)))
    return lax.ppermute(block, ("img", "txt"), pairs)


def cross_first(distance):
    return (lax.axis_index("txt") % 2 == 0) | (distance % 2 == 1)


def is_even():
    return lax.axis_index("img") % 2 == 0


def call(kernel, outs, args, cost=None):
    sizes = [a.size * a.dtype.itemsize for a in list(args) + list(outs)]
    return pl.pallas_call(
        kernel,
        out_shape=outs,
        in_specs=[VMEM] * len(args),
        out_specs=[VMEM] * len(outs),
        cost_estimate=cost,
        compiler_params=pltpu.CompilerParams(
            vmem_limit_bytes=min(48 * 2**20, 8 * 2**20 + 6 * sum(sizes))
        ),
    )(*args)


def sides_kernel(own_ref, txt_ref, img_ref, mine_ref, other_ref):
    rows = txt_ref.shape[0]
    even = is_even()
    own = normalize(own_ref[...])[0].astype(bf16)
    own_txt, own_img = own[:rows], own[rows:]
    far_txt = normalize(txt_ref[...])[0].astype(bf16)
    far_img = normalize(img_ref[...])[0].astype(bf16)
    mine_ref[:rows, :] = jnp.where(even, own_txt, far_img)
    mine_ref[rows:, :] = jnp.where(even, far_txt, own_img)
    other_ref[:rows, :] = jnp.where(even, own_img, far_txt)
    other_ref[rows:, :] = jnp.where(even, far_img, own_txt)


def row_ids(rows, ids, far_ids, count):
    me_img = lax.axis_index("img")
    me_txt = lax.axis_index("txt")
    n_img = lax.axis_size("img")
    row = lax.broadcasted_iota(jnp.int32, (count, 1), 0)
    block, core, j = row // (2 * rows), row // rows % 2, row % rows
    blocks = count // (2 * rows)
    chip = jnp.where(block == 0, 0, blocks - block)
    if blocks > 2:
        chip = jnp.where(block == 1, blocks - 2, jnp.where(block == 2, blocks - 1, chip))
    txt_ids = (me_txt * n_img + (((me_img // 2) ^ chip) * 2 + core)) * rows + j
    source = (me_txt ^ chip) * rows + j
    here = lax.broadcasted_iota(jnp.int32, (count, ids.shape[1]), 1) == source
    per_core = jnp.where(core == me_img % 2, ids, far_ids)
    img_ids = jnp.sum(jnp.where(here, per_core, 0), axis=1, keepdims=True)
    return txt_ids, img_ids


def side_ids(rows, ids, far_ids, count):
    even = is_even()
    txt_ids, img_ids = row_ids(rows, ids, far_ids, count)
    other_ids = jnp.where(even, img_ids, txt_ids)
    diagonal = lax.broadcasted_iota(jnp.int32, (count, count), 0) == lax.broadcasted_iota(
        jnp.int32, (count, count), 1
    )
    other_ids = jnp.sum(jnp.where(diagonal, other_ids, 0), axis=0, keepdims=True)
    return jnp.where(even, txt_ids, img_ids), other_ids


def scores_of(mine_refs, other_refs):
    mine = jnp.concatenate([ref[...] for ref in mine_refs], axis=0)
    other = jnp.concatenate([ref[...] for ref in other_refs], axis=0)
    return lax.dot_general(mine, other, (((1,), (1,)), ((), ())), preferred_element_type=f32)


def pair_kernel(blocks, split, ids_ref, far_ids_ref, *refs):
    mine_refs, other_refs = refs[:blocks], refs[blocks:2 * blocks]
    own_ref, first_ref, second_ref, *send_refs = refs[2 * blocks:]
    height = own_ref.shape[0]
    rows = height // 2
    mine_ids, other_ids = side_ids(rows, ids_ref[...], far_ids_ref[...], blocks * height)
    scores = scores_of(mine_refs, other_refs)
    coeff = pair_coeff(scale_logit * scores + shift_logit, mine_ids == other_ids)
    other = jnp.concatenate([ref[...] for ref in other_refs], axis=0)
    part = jnp.dot(coeff, other, preferred_element_type=f32)
    own_ref[...] = part[:height]
    whole = [k for k in range(1, blocks) if k != split]
    for k, ref in zip(whole, send_refs):
        ref[...] = part[k * height:(k + 1) * height].astype(bf16)
    block = part[split * height:(split + 1) * height].astype(bf16)
    even = is_even()
    first = jnp.logical_xor(even, cross_first(blocks - split))
    first_ref[...] = jnp.where(first, block[:rows], block[rows:])
    second_ref[...] = jnp.where(first, block[rows:], block[:rows])


def sum_kernel(own_ref, *refs):
    *got_refs, keep_ref, send_ref = refs
    rows = keep_ref.shape[0]
    total = own_ref[...]
    for ref in got_refs:
        total = total + ref[...].astype(f32)
    even = is_even()
    keep_ref[...] = jnp.where(even, total[:rows], total[rows:])
    send_ref[...] = jnp.where(even, total[rows:], total[:rows]).astype(bf16)


def unit_kernel(raw_ref, first_ref, unit_ref, inverse_ref, rest_ref):
    unit_ref[...], inverse_ref[...] = normalize(raw_ref[...])
    rest_ref[...] = first_ref[...].astype(f32)


def out_kernel(
    far, unit_ref, inverse_ref, first_ref, keep_ref, second_ref, got_ref, img_ref, txt_ref
):
    rows = keep_ref.shape[0]
    even = is_even()
    first, second = first_ref[...], second_ref[...].astype(f32)
    cross = cross_first(far)
    keep = keep_ref[...] + jnp.where(cross, second, first)
    got = got_ref[...].astype(f32) + jnp.where(cross, first, second)
    unit, inverse = unit_ref[...], inverse_ref[...]
    txt_ref[...] = back_norm(unit[:rows], inverse[:rows], jnp.where(even, keep, got))
    img_ref[...] = back_norm(unit[rows:], inverse[rows:], jnp.where(even, got, keep))


def local(image_embeds, text_embeds, pair_ids):
    rows, width = image_embeds.shape
    blocks = max(lax.axis_size("img") // 2, lax.axis_size("txt"))
    pair = jax.ShapeDtypeStruct((2 * rows, width), bf16)
    total = jax.ShapeDtypeStruct((2 * rows, width), f32)
    piece = jax.ShapeDtypeStruct((rows, width), bf16)
    single = jax.ShapeDtypeStruct((rows, width), f32)
    ids = pair_ids.reshape(1, -1)
    far_txt = core_swap(text_embeds)
    far_img = core_swap(image_embeds)
    near = jnp.concatenate([text_embeds, image_embeds])
    mine, other = call(sides_kernel, [pair] * 2, [near, far_txt, far_img])
    order = list(range(blocks - 1, 0, -1))
    order[:2] = order[1::-1]
    mine = [mine] + [chip_swap(mine, k) for k in order]
    other = [other, *[core_swap(block) for block in mine[1:-1]], chip_swap(mine[0], 1, lambda txt: 1)]
    split = blocks - 1
    own, first, second, *send = call(
        functools.partial(pair_kernel, blocks, split),
        [total] + [piece] * 2 + [pair] * (blocks - 2),
        [ids, core_swap(ids), *mine, *other],
    )
    far = order.pop(split - 1)
    got = [chip_swap(block, k) for k, block in zip(order, send)]
    got[:2] = got[1::-1]
    first = chip_swap(first, far, lambda txt: int(txt % 2 == 0 or far % 2 == 1))
    second = chip_swap(second, far, lambda txt: int(txt % 2 == 1 and far % 2 == 0))
    keep, send = call(sum_kernel, [single, piece], [own, *got])
    got = core_swap(send)
    column = jax.ShapeDtypeStruct((2 * rows, 1), f32)
    ready = call(unit_kernel, [total, column, single], [near, first], cost=LONG)
    kernel = functools.partial(out_kernel, far)
    return tuple(call(kernel, [single] * 2, [*ready, keep, second, got]))


def solution(mesh):
    return jax.shard_map(
        local,
        mesh=mesh,
        in_specs=(P(("img", "txt"), None), P(("txt", "img"), None), P("img")),
        out_specs=(P(("img", "txt"), None), P(("txt", "img"), None)),
        check_vma=False,
    )
```

```python
import functools

import jax
import jax.numpy as jnp
from jax import lax
from jax.experimental import pallas as pl
from jax.experimental.pallas import tpu as pltpu
from jax.sharding import PartitionSpec as P

scale_logit = 8.0
shift_logit = -4.0
epsilon = 1e-06
f32 = jnp.float32
bf16 = jnp.bfloat16
VMEM = pl.BlockSpec(memory_space=pltpu.VMEM)
LONG = pl.CostEstimate(flops=10**10, bytes_accessed=10**7, transcendentals=0)


def normalize(raw):
    values = raw.astype(f32)
    inverse = lax.rsqrt(jnp.sum(values * values, axis=-1, keepdims=True) + epsilon)
    return (values * inverse, inverse)


def back_norm(unit, inverse, grad):
    inner = jnp.sum(unit * grad, axis=-1, keepdims=True)
    return inverse * (grad - unit * inner)


def pair_coeff(logit, same):
    label = jnp.where(same, 1.0, -1.0).astype(f32)
    return (-scale_logit * label * jax.nn.sigmoid(-label * logit)).astype(bf16)


def core_swap(block):
    size = lax.axis_size("img")
    return lax.ppermute(block, "img", [(i, i ^ 1) for i in range(size)])


def chip_swap(block, distances, cross=lambda txt: 0):
    n_img, n_txt = lax.axis_size("img"), lax.axis_size("txt")
    along_img, along_txt = distances
    pairs = []
    for img in range(n_img):
        for txt in range(n_txt):
            other = cross(txt)
            if img % 2 == 0 and along_img < n_img // 2:
                pairs.append((img * n_txt + txt, (img ^ (2 * along_img) ^ other) * n_txt + txt))
            if img % 2 == 1 and along_txt < n_txt:
                pairs.append((img * n_txt + txt, (img ^ other) * n_txt + (txt ^ along_txt)))
    return lax.ppermute(block, ("img", "txt"), pairs)


def orders(blocks):
    falling = list(range(blocks - 1, 0, -1))
    return falling, falling[1::-1] + falling[2:]


def cross_first(distance):
    return (lax.axis_index("txt") % 2 == 0) | (distance % 2 == 1)


def is_even():
    return lax.axis_index("img") % 2 == 0


def call(kernel, outs, args, cost=None):
    sizes = [a.size * a.dtype.itemsize for a in list(args) + list(outs)]
    return pl.pallas_call(
        kernel,
        out_shape=outs,
        in_specs=[VMEM] * len(args),
        out_specs=[VMEM] * len(outs),
        cost_estimate=cost,
        compiler_params=pltpu.CompilerParams(
            vmem_limit_bytes=min(48 * 2**20, 8 * 2**20 + 6 * sum(sizes))
        ),
    )(*args)


def sides_kernel(own_ref, txt_ref, img_ref, mine_ref, other_ref):
    rows = txt_ref.shape[0]
    even = is_even()
    own = normalize(own_ref[...])[0].astype(bf16)
    own_txt, own_img = own[:rows], own[rows:]
    far_txt = normalize(txt_ref[...])[0].astype(bf16)
    far_img = normalize(img_ref[...])[0].astype(bf16)
    mine_ref[:rows, :] = jnp.where(even, own_txt, far_img)
    mine_ref[rows:, :] = jnp.where(even, far_txt, own_img)
    other_ref[:rows, :] = jnp.where(even, own_img, far_txt)
    other_ref[rows:, :] = jnp.where(even, far_img, own_txt)


def row_ids(rows, ids, far_ids, count):
    me_img = lax.axis_index("img")
    me_txt = lax.axis_index("txt")
    n_img = lax.axis_size("img")
    row = lax.broadcasted_iota(jnp.int32, (count, 1), 0)
    block, core, j = row // (2 * rows), row // rows % 2, row % rows
    chips = []
    for order in orders(count // (2 * rows)):
        chip = jnp.zeros_like(block)
        for k, distance in enumerate(order):
            chip = jnp.where(block == k + 1, distance, chip)
        chips.append(chip)
    txt_ids = (me_txt * n_img + (((me_img // 2) ^ chips[0]) * 2 + core)) * rows + j
    source = (me_txt ^ chips[1]) * rows + j
    here = lax.broadcasted_iota(jnp.int32, (count, ids.shape[1]), 1) == source
    per_core = jnp.where(core == me_img % 2, ids, far_ids)
    img_ids = jnp.sum(jnp.where(here, per_core, 0), axis=1, keepdims=True)
    return txt_ids, img_ids


def side_ids(rows, ids, far_ids, count):
    even = is_even()
    txt_ids, img_ids = row_ids(rows, ids, far_ids, count)
    other_ids = jnp.where(even, img_ids, txt_ids)
    diagonal = lax.broadcasted_iota(jnp.int32, (count, count), 0) == lax.broadcasted_iota(
        jnp.int32, (count, count), 1
    )
    other_ids = jnp.sum(jnp.where(diagonal, other_ids, 0), axis=0, keepdims=True)
    return jnp.where(even, txt_ids, img_ids), other_ids


def scores_of(mine_refs, other_refs):
    mine = jnp.concatenate([ref[...] for ref in mine_refs], axis=0)
    other = jnp.concatenate([ref[...] for ref in other_refs], axis=0)
    return lax.dot_general(mine, other, (((1,), (1,)), ((), ())), preferred_element_type=f32)


def pair_kernel(blocks, plan, ids_ref, far_ids_ref, *refs):
    mine_refs, other_refs = refs[:blocks], refs[blocks:2 * blocks]
    own_ref, first_ref, second_ref, *send_refs = refs[2 * blocks:]
    height = own_ref.shape[0]
    rows = height // 2
    mine_ids, other_ids = side_ids(rows, ids_ref[...], far_ids_ref[...], blocks * height)
    scores = scores_of(mine_refs, other_refs)
    coeff = pair_coeff(scale_logit * scores + shift_logit, mine_ids == other_ids)
    other = jnp.concatenate([ref[...] for ref in other_refs], axis=0)
    part = jnp.dot(coeff, other, preferred_element_type=f32)
    own_ref[...] = part[:height]
    even = is_even()
    txt_order, img_order = orders(blocks)

    def block_of(distance):
        txt, img = [
            part[(order.index(distance) + 1) * height:(order.index(distance) + 2) * height]
            for order in (txt_order, img_order)
        ]
        return jnp.where(even, txt, img).astype(bf16)

    *whole, split = plan
    for distance, ref in zip(whole, send_refs):
        ref[...] = block_of(distance)
    block = block_of(split)
    first = jnp.logical_xor(even, cross_first(split))
    first_ref[...] = jnp.where(first, block[:rows], block[rows:])
    second_ref[...] = jnp.where(first, block[rows:], block[:rows])


def sum_kernel(own_ref, *refs):
    *got_refs, keep_ref, send_ref = refs
    rows = keep_ref.shape[0]
    total = own_ref[...]
    for ref in got_refs:
        total = total + ref[...].astype(f32)
    even = is_even()
    keep_ref[...] = jnp.where(even, total[:rows], total[rows:])
    send_ref[...] = jnp.where(even, total[rows:], total[:rows]).astype(bf16)


def unit_kernel(raw_ref, first_ref, unit_ref, inverse_ref, rest_ref):
    unit_ref[...], inverse_ref[...] = normalize(raw_ref[...])
    rest_ref[...] = first_ref[...].astype(f32)


def out_kernel(
    far, unit_ref, inverse_ref, first_ref, keep_ref, second_ref, got_ref, img_ref, txt_ref
):
    rows = keep_ref.shape[0]
    even = is_even()
    first, second = first_ref[...], second_ref[...].astype(f32)
    cross = cross_first(far)
    keep = keep_ref[...] + jnp.where(cross, second, first)
    got = got_ref[...].astype(f32) + jnp.where(cross, first, second)
    unit, inverse = unit_ref[...], inverse_ref[...]
    txt_ref[...] = back_norm(unit[:rows], inverse[:rows], jnp.where(even, keep, got))
    img_ref[...] = back_norm(unit[rows:], inverse[rows:], jnp.where(even, got, keep))


def local(image_embeds, text_embeds, pair_ids):
    rows, width = image_embeds.shape
    blocks = max(lax.axis_size("img") // 2, lax.axis_size("txt"))
    pair = jax.ShapeDtypeStruct((2 * rows, width), bf16)
    total = jax.ShapeDtypeStruct((2 * rows, width), f32)
    piece = jax.ShapeDtypeStruct((rows, width), bf16)
    single = jax.ShapeDtypeStruct((rows, width), f32)
    ids = pair_ids.reshape(1, -1)
    far_txt = core_swap(text_embeds)
    far_img = core_swap(image_embeds)
    near = jnp.concatenate([text_embeds, image_embeds])
    mine, other = call(sides_kernel, [pair] * 2, [near, far_txt, far_img])
    mine = [mine] + [chip_swap(mine, distances) for distances in zip(*orders(blocks))]
    other = [other, *[core_swap(block) for block in mine[1:-1]], chip_swap(mine[0], (1, 1), lambda txt: 1)]
    plan = list(range(blocks - 1, 0, -1))
    far = plan[-1]
    own, first, second, *send = call(
        functools.partial(pair_kernel, blocks, plan),
        [total] + [piece] * 2 + [pair] * (blocks - 2),
        [ids, core_swap(ids), *mine, *other],
    )
    got = [chip_swap(block, (k, k)) for k, block in zip(plan, send)]
    first = chip_swap(first, (far, far), lambda txt: int(txt % 2 == 0 or far % 2 == 1))
    second = chip_swap(second, (far, far), lambda txt: int(txt % 2 == 1 and far % 2 == 0))
    keep, send = call(sum_kernel, [single, piece], [own, *got])
    got = core_swap(send)
    column = jax.ShapeDtypeStruct((2 * rows, 1), f32)
    ready = call(unit_kernel, [total, column, single], [near, first], cost=LONG)
    kernel = functools.partial(out_kernel, far)
    return tuple(call(kernel, [single] * 2, [*ready, keep, second, got]))


def solution(mesh):
    return jax.shard_map(
        local,
        mesh=mesh,
        in_specs=(P(("img", "txt"), None), P(("txt", "img"), None), P("img")),
        out_specs=(P(("img", "txt"), None), P(("txt", "img"), None)),
        check_vma=False,
    )
```

```python
import functools

import jax
import jax.numpy as jnp
from jax import lax
from jax.experimental import pallas as pl
from jax.experimental.pallas import tpu as pltpu
from jax.sharding import PartitionSpec as P

scale_logit = 8.0
shift_logit = -4.0
epsilon = 1e-06
f32 = jnp.float32
bf16 = jnp.bfloat16
VMEM = pl.BlockSpec(memory_space=pltpu.VMEM)
LONG = pl.CostEstimate(flops=10**10, bytes_accessed=10**7, transcendentals=0)


def normalize(raw):
    values = raw.astype(f32)
    inverse = lax.rsqrt(jnp.sum(values * values, axis=-1, keepdims=True) + epsilon)
    return (values * inverse, inverse)


def back_norm(unit, inverse, grad):
    inner = jnp.sum(unit * grad, axis=-1, keepdims=True)
    return inverse * (grad - unit * inner)


def pair_coeff(logit, same):
    label = jnp.where(same, 1.0, -1.0).astype(f32)
    return (-scale_logit * label * jax.nn.sigmoid(-label * logit)).astype(bf16)


def core_swap(block):
    size = lax.axis_size("img")
    return lax.ppermute(block, "img", [(i, i ^ 1) for i in range(size)])


def chip_swap(block, distances, cross=lambda txt: 0):
    n_img, n_txt = lax.axis_size("img"), lax.axis_size("txt")
    along_img, along_txt = distances
    pairs = []
    for img in range(n_img):
        for txt in range(n_txt):
            other = cross(txt)
            if img % 2 == 0 and along_img < n_img // 2:
                pairs.append((img * n_txt + txt, (img ^ (2 * along_img) ^ other) * n_txt + txt))
            if img % 2 == 1 and along_txt < n_txt:
                pairs.append((img * n_txt + txt, (img ^ other) * n_txt + (txt ^ along_txt)))
    return lax.ppermute(block, ("img", "txt"), pairs)


def orders(blocks):
    falling = list(range(blocks - 1, 0, -1))
    return falling[1::-1] + falling[2:], falling


def cross_first(distance):
    return (lax.axis_index("txt") % 2 == 0) | (distance % 2 == 1)


def is_even():
    return lax.axis_index("img") % 2 == 0


def call(kernel, outs, args, cost=None):
    sizes = [a.size * a.dtype.itemsize for a in list(args) + list(outs)]
    return pl.pallas_call(
        kernel,
        out_shape=outs,
        in_specs=[VMEM] * len(args),
        out_specs=[VMEM] * len(outs),
        cost_estimate=cost,
        compiler_params=pltpu.CompilerParams(
            vmem_limit_bytes=min(48 * 2**20, 8 * 2**20 + 6 * sum(sizes))
        ),
    )(*args)


def sides_kernel(own_ref, txt_ref, img_ref, mine_ref, other_ref):
    rows = txt_ref.shape[0]
    even = is_even()
    own = normalize(own_ref[...])[0].astype(bf16)
    own_txt, own_img = own[:rows], own[rows:]
    far_txt = normalize(txt_ref[...])[0].astype(bf16)
    far_img = normalize(img_ref[...])[0].astype(bf16)
    mine_ref[:rows, :] = jnp.where(even, own_txt, far_img)
    mine_ref[rows:, :] = jnp.where(even, far_txt, own_img)
    other_ref[:rows, :] = jnp.where(even, own_img, far_txt)
    other_ref[rows:, :] = jnp.where(even, far_img, own_txt)


def row_ids(rows, ids, far_ids, count):
    me_img = lax.axis_index("img")
    me_txt = lax.axis_index("txt")
    n_img = lax.axis_size("img")
    row = lax.broadcasted_iota(jnp.int32, (count, 1), 0)
    block, core, j = row // (2 * rows), row // rows % 2, row % rows
    chips = []
    for order in orders(count // (2 * rows)):
        chip = jnp.zeros_like(block)
        for k, distance in enumerate(order):
            chip = jnp.where(block == k + 1, distance, chip)
        chips.append(chip)
    txt_ids = (me_txt * n_img + (((me_img // 2) ^ chips[0]) * 2 + core)) * rows + j
    source = (me_txt ^ chips[1]) * rows + j
    here = lax.broadcasted_iota(jnp.int32, (count, ids.shape[1]), 1) == source
    per_core = jnp.where(core == me_img % 2, ids, far_ids)
    img_ids = jnp.sum(jnp.where(here, per_core, 0), axis=1, keepdims=True)
    return txt_ids, img_ids


def side_ids(rows, ids, far_ids, count):
    even = is_even()
    txt_ids, img_ids = row_ids(rows, ids, far_ids, count)
    other_ids = jnp.where(even, img_ids, txt_ids)
    diagonal = lax.broadcasted_iota(jnp.int32, (count, count), 0) == lax.broadcasted_iota(
        jnp.int32, (count, count), 1
    )
    other_ids = jnp.sum(jnp.where(diagonal, other_ids, 0), axis=0, keepdims=True)
    return jnp.where(even, txt_ids, img_ids), other_ids


def scores_of(mine_refs, other_refs):
    mine = jnp.concatenate([ref[...] for ref in mine_refs], axis=0)
    other = jnp.concatenate([ref[...] for ref in other_refs], axis=0)
    return lax.dot_general(mine, other, (((1,), (1,)), ((), ())), preferred_element_type=f32)


def pair_kernel(blocks, plan, ids_ref, far_ids_ref, *refs):
    mine_refs, other_refs = refs[:blocks], refs[blocks:2 * blocks]
    own_ref, first_ref, second_ref, *send_refs = refs[2 * blocks:]
    height = own_ref.shape[0]
    rows = height // 2
    mine_ids, other_ids = side_ids(rows, ids_ref[...], far_ids_ref[...], blocks * height)
    scores = scores_of(mine_refs, other_refs)
    coeff = pair_coeff(scale_logit * scores + shift_logit, mine_ids == other_ids)
    other = jnp.concatenate([ref[...] for ref in other_refs], axis=0)
    part = jnp.dot(coeff, other, preferred_element_type=f32)
    own_ref[...] = part[:height]
    even = is_even()
    txt_order, img_order = orders(blocks)

    def block_of(distance):
        txt, img = [
            part[(order.index(distance) + 1) * height:(order.index(distance) + 2) * height]
            for order in (txt_order, img_order)
        ]
        return jnp.where(even, txt, img).astype(bf16)

    *whole, split = plan
    for distance, ref in zip(whole, send_refs):
        ref[...] = block_of(distance)
    block = block_of(split)
    first = jnp.logical_xor(even, cross_first(split))
    first_ref[...] = jnp.where(first, block[:rows], block[rows:])
    second_ref[...] = jnp.where(first, block[rows:], block[:rows])


def sum_kernel(own_ref, *refs):
    *got_refs, keep_ref, send_ref = refs
    rows = keep_ref.shape[0]
    total = own_ref[...]
    for ref in got_refs:
        total = total + ref[...].astype(f32)
    even = is_even()
    keep_ref[...] = jnp.where(even, total[:rows], total[rows:])
    send_ref[...] = jnp.where(even, total[rows:], total[:rows]).astype(bf16)


def unit_kernel(raw_ref, first_ref, unit_ref, inverse_ref, rest_ref):
    unit_ref[...], inverse_ref[...] = normalize(raw_ref[...])
    rest_ref[...] = first_ref[...].astype(f32)


def out_kernel(
    far, unit_ref, inverse_ref, first_ref, keep_ref, second_ref, got_ref, img_ref, txt_ref
):
    rows = keep_ref.shape[0]
    even = is_even()
    first, second = first_ref[...], second_ref[...].astype(f32)
    cross = cross_first(far)
    keep = keep_ref[...] + jnp.where(cross, second, first)
    got = got_ref[...].astype(f32) + jnp.where(cross, first, second)
    unit, inverse = unit_ref[...], inverse_ref[...]
    txt_ref[...] = back_norm(unit[:rows], inverse[:rows], jnp.where(even, keep, got))
    img_ref[...] = back_norm(unit[rows:], inverse[rows:], jnp.where(even, got, keep))


def local(image_embeds, text_embeds, pair_ids):
    rows, width = image_embeds.shape
    blocks = max(lax.axis_size("img") // 2, lax.axis_size("txt"))
    pair = jax.ShapeDtypeStruct((2 * rows, width), bf16)
    total = jax.ShapeDtypeStruct((2 * rows, width), f32)
    piece = jax.ShapeDtypeStruct((rows, width), bf16)
    single = jax.ShapeDtypeStruct((rows, width), f32)
    ids = pair_ids.reshape(1, -1)
    far_txt = core_swap(text_embeds)
    far_img = core_swap(image_embeds)
    near = jnp.concatenate([text_embeds, image_embeds])
    mine, other = call(sides_kernel, [pair] * 2, [near, far_txt, far_img])
    mine = [mine] + [chip_swap(mine, distances) for distances in zip(*orders(blocks))]
    other = [other, *[core_swap(block) for block in mine[1:-1]], chip_swap(mine[0], (1, 1), lambda txt: 1)]
    plan = list(range(blocks - 1, 0, -1))
    far = plan[-1]
    own, first, second, *send = call(
        functools.partial(pair_kernel, blocks, plan),
        [total] + [piece] * 2 + [pair] * (blocks - 2),
        [ids, core_swap(ids), *mine, *other],
    )
    got = [chip_swap(block, (k, k)) for k, block in zip(plan, send)]
    first = chip_swap(first, (far, far), lambda txt: int(txt % 2 == 0 or far % 2 == 1))
    second = chip_swap(second, (far, far), lambda txt: int(txt % 2 == 1 and far % 2 == 0))
    keep, send = call(sum_kernel, [single, piece], [own, *got])
    got = core_swap(send)
    column = jax.ShapeDtypeStruct((2 * rows, 1), f32)
    ready = call(unit_kernel, [total, column, single], [near, first], cost=LONG)
    kernel = functools.partial(out_kernel, far)
    return tuple(call(kernel, [single] * 2, [*ready, keep, second, got]))


def solution(mesh):
    return jax.shard_map(
        local,
        mesh=mesh,
        in_specs=(P(("img", "txt"), None), P(("txt", "img"), None), P("img")),
        out_specs=(P(("img", "txt"), None), P(("txt", "img"), None)),
        check_vma=False,
    )
```

```python
import functools

import jax
import jax.numpy as jnp
from jax import lax
from jax.experimental import pallas as pl
from jax.experimental.pallas import tpu as pltpu
from jax.sharding import PartitionSpec as P

scale_logit = 8.0
shift_logit = -4.0
epsilon = 1e-06
f32 = jnp.float32
bf16 = jnp.bfloat16
VMEM = pl.BlockSpec(memory_space=pltpu.VMEM)
LANES = 128
LONG = pl.CostEstimate(flops=10**10, bytes_accessed=10**7, transcendentals=0)


def normalize(raw):
    values = raw.astype(f32)
    inverse = lax.rsqrt(jnp.sum(values * values, axis=-1, keepdims=True) + epsilon)
    return (values * inverse, inverse)


def back_norm(unit, inverse, grad):
    inner = jnp.sum(unit * grad, axis=-1, keepdims=True)
    return inverse * (grad - unit * inner)


def pair_coeff(logit, same):
    label = jnp.where(same, 1.0, -1.0).astype(f32)
    return (-scale_logit * label * jax.nn.sigmoid(-label * logit)).astype(bf16)


def core_swap(block):
    size = lax.axis_size("img")
    return lax.ppermute(block, "img", [(i, i ^ 1) for i in range(size)])


def chip_swap(block, distances, cross=lambda txt: 0):
    n_img, n_txt = lax.axis_size("img"), lax.axis_size("txt")
    along_img, along_txt = distances
    pairs = []
    for img in range(n_img):
        for txt in range(n_txt):
            other = cross(txt)
            if img % 2 == 0 and along_img < n_img // 2:
                pairs.append((img * n_txt + txt, (img ^ (2 * along_img) ^ other) * n_txt + txt))
            if img % 2 == 1 and along_txt < n_txt:
                pairs.append((img * n_txt + txt, (img ^ other) * n_txt + (txt ^ along_txt)))
    return lax.ppermute(block, ("img", "txt"), pairs)


def orders(blocks):
    return [*range(blocks - 2, 0, -1), blocks - 1]


def cross_first(distance):
    return (lax.axis_index("txt") % 2 == 0) | (distance % 2 == 1)


def is_even():
    return lax.axis_index("img") % 2 == 0


def call(kernel, outs, args, cost=None):
    sizes = [a.size * a.dtype.itemsize for a in list(args) + list(outs)]
    return pl.pallas_call(
        kernel,
        out_shape=outs,
        in_specs=[VMEM] * len(args),
        out_specs=[VMEM] * len(outs),
        cost_estimate=cost,
        compiler_params=pltpu.CompilerParams(
            vmem_limit_bytes=min(48 * 2**20, 8 * 2**20 + 6 * sum(sizes))
        ),
    )(*args)


def sides_kernel(own_ref, txt_ref, img_ref, mine_ref, other_ref):
    rows = txt_ref.shape[0]
    even = is_even()
    own = normalize(own_ref[...])[0].astype(bf16)
    own_txt, own_img = own[:rows], own[rows:]
    far_txt = normalize(txt_ref[...])[0].astype(bf16)
    far_img = normalize(img_ref[...])[0].astype(bf16)
    mine_ref[:rows, :] = jnp.where(even, own_txt, far_img)
    mine_ref[rows:, :] = jnp.where(even, far_txt, own_img)
    other_ref[:rows, :] = jnp.where(even, own_img, far_txt)
    other_ref[rows:, :] = jnp.where(even, far_img, own_txt)


def pack_kernel(ids_ref, piece_ref, out_ref):
    height, width = piece_ref.shape
    tiles = width // LANES
    count = ids_ref.shape[1]
    for k in range(tiles):
        out_ref[k * height:(k + 1) * height, :] = piece_ref[:, k * LANES:(k + 1) * LANES]
    rest = out_ref.shape[0] - tiles * height
    row = lax.broadcasted_iota(jnp.int32, (rest, LANES), 0)
    code = jnp.zeros((rest, LANES), f32)
    for k in range(0, count, LANES):
        ids = ids_ref[:, k:k + LANES]
        if ids.shape[1] < LANES:
            ids = jnp.concatenate([ids, jnp.zeros((1, LANES - ids.shape[1]), ids.dtype)], axis=1)
        code = jnp.where(row == 2 * k // LANES, (ids // 256).astype(f32), code)
        code = jnp.where(row == 2 * k // LANES + 1, (ids % 256).astype(f32), code)
    out_ref[tiles * height:, :] = code.astype(bf16)


def unpack(ref, height, width, count):
    tiles = width // LANES
    piece = jnp.concatenate(
        [ref[k * height:(k + 1) * height, :] for k in range(tiles)], axis=1
    )
    code = ref[tiles * height:, :].astype(f32)
    ids = [code[k:k + 1] * 256.0 + code[k + 1:k + 2] for k in range(0, 2 * count // LANES or 2, 2)]
    ids = jnp.concatenate(ids, axis=1)[:, :count].astype(jnp.int32)
    return piece, ids


def row_ids(rows, ids, far_ids, count):
    me_img = lax.axis_index("img")
    me_txt = lax.axis_index("txt")
    n_img = lax.axis_size("img")
    row = lax.broadcasted_iota(jnp.int32, (count, 1), 0)
    block, core, j = row // (2 * rows), row // rows % 2, row % rows
    chip = jnp.zeros_like(block)
    for k, distance in enumerate(orders(count // (2 * rows))):
        chip = jnp.where(block == k + 1, distance, chip)
    txt_ids = (me_txt * n_img + (((me_img // 2) ^ chip) * 2 + core)) * rows + j
    source = (me_txt ^ chip) * rows + j
    here = lax.broadcasted_iota(jnp.int32, (count, ids.shape[1]), 1) == source
    per_core = jnp.where(core == me_img % 2, ids, far_ids)
    img_ids = jnp.sum(jnp.where(here, per_core, 0), axis=1, keepdims=True)
    return txt_ids, img_ids


def side_ids(rows, ids, far_ids, count):
    even = is_even()
    txt_ids, img_ids = row_ids(rows, ids, far_ids, count)
    other_ids = jnp.where(even, img_ids, txt_ids)
    diagonal = lax.broadcasted_iota(jnp.int32, (count, count), 0) == lax.broadcasted_iota(
        jnp.int32, (count, count), 1
    )
    other_ids = jnp.sum(jnp.where(diagonal, other_ids, 0), axis=0, keepdims=True)
    return jnp.where(even, txt_ids, img_ids), other_ids


def scores_of(mine_refs, other):
    mine = jnp.concatenate([ref[...] for ref in mine_refs], axis=0)
    return lax.dot_general(mine, other, (((1,), (1,)), ((), ())), preferred_element_type=f32)


def most_kernel(blocks, *refs):
    mine_refs, other_refs, (other_ref, scores_ref) = refs[:blocks], refs[blocks:-2], refs[-2:]
    other = jnp.concatenate([ref[...] for ref in other_refs], axis=0)
    other_ref[...] = other
    scores_ref[...] = scores_of(mine_refs, other)


def pair_kernel(blocks, plan, ids_ref, other_ref, scores_ref, last_ref, *refs):
    mine_refs, (own_ref, first_ref, second_ref, *send_refs) = refs[:blocks], refs[blocks:]
    height, width = own_ref.shape
    rows = height // 2
    last, far_ids = unpack(last_ref, height, width, ids_ref.shape[1])
    mine_ids, other_ids = side_ids(rows, ids_ref[...], far_ids, blocks * height)
    scores = jnp.concatenate([scores_ref[...], scores_of(mine_refs, last)], axis=1)
    coeff = pair_coeff(scale_logit * scores + shift_logit, mine_ids == other_ids)
    other = jnp.concatenate([other_ref[...], last], axis=0)
    part = jnp.dot(coeff, other, preferred_element_type=f32)
    own_ref[...] = part[:height]
    even = is_even()

    def block_of(distance):
        start = (orders(blocks).index(distance) + 1) * height
        return part[start:start + height].astype(bf16)

    *whole, split = plan
    for distance, ref in zip(whole, send_refs):
        ref[...] = block_of(distance)
    block = block_of(split)
    first = jnp.logical_xor(even, cross_first(split))
    first_ref[...] = jnp.where(first, block[:rows], block[rows:])
    second_ref[...] = jnp.where(first, block[rows:], block[:rows])


def sum_kernel(own_ref, *refs):
    *got_refs, keep_ref, send_ref = refs
    rows = keep_ref.shape[0]
    total = own_ref[...]
    for ref in got_refs:
        total = total + ref[...].astype(f32)
    even = is_even()
    keep_ref[...] = jnp.where(even, total[:rows], total[rows:])
    send_ref[...] = jnp.where(even, total[rows:], total[:rows]).astype(bf16)


def unit_kernel(raw_ref, first_ref, unit_ref, inverse_ref, rest_ref):
    unit_ref[...], inverse_ref[...] = normalize(raw_ref[...])
    rest_ref[...] = first_ref[...].astype(f32)


def out_kernel(
    far, unit_ref, inverse_ref, first_ref, keep_ref, second_ref, got_ref, img_ref, txt_ref
):
    rows = keep_ref.shape[0]
    even = is_even()
    first, second = first_ref[...], second_ref[...].astype(f32)
    cross = cross_first(far)
    keep = keep_ref[...] + jnp.where(cross, second, first)
    got = got_ref[...].astype(f32) + jnp.where(cross, first, second)
    unit, inverse = unit_ref[...], inverse_ref[...]
    txt_ref[...] = back_norm(unit[:rows], inverse[:rows], jnp.where(even, keep, got))
    img_ref[...] = back_norm(unit[rows:], inverse[rows:], jnp.where(even, got, keep))


def local(image_embeds, text_embeds, pair_ids):
    rows, width = image_embeds.shape
    blocks = max(lax.axis_size("img") // 2, lax.axis_size("txt"))
    pair = jax.ShapeDtypeStruct((2 * rows, width), bf16)
    total = jax.ShapeDtypeStruct((2 * rows, width), f32)
    piece = jax.ShapeDtypeStruct((rows, width), bf16)
    single = jax.ShapeDtypeStruct((rows, width), f32)
    ids = pair_ids.reshape(1, -1)
    far_txt = core_swap(text_embeds)
    far_img = core_swap(image_embeds)
    near = jnp.concatenate([text_embeds, image_embeds])
    mine, *other = call(sides_kernel, [pair] * 2, [near, far_txt, far_img])
    order = orders(blocks)
    mine = [mine] + [chip_swap(mine, (k, k)) for k in order]
    tiles = jax.ShapeDtypeStruct((2 * rows * (width // LANES) + 16, LANES), bf16)
    (tiles,) = call(pack_kernel, [tiles], [ids, mine[-1]])
    near_block = chip_swap(mine[0], (1, 1), lambda txt: 1)
    other += [near_block if k == 1 else core_swap(x) for k, x in zip(order[:-1], mine[1:-1])]
    count = blocks * 2 * rows
    outs = [
        jax.ShapeDtypeStruct((count - 2 * rows, width), bf16),
        jax.ShapeDtypeStruct((count, count - 2 * rows), f32),
    ]
    most = call(functools.partial(most_kernel, blocks), outs, [*mine, *other], cost=LONG)
    plan = list(range(blocks - 1, 0, -1))
    far = plan[-1]
    own, first, second, *send = call(
        functools.partial(pair_kernel, blocks, plan),
        [total] + [piece] * 2 + [pair] * (blocks - 2),
        [ids, *most, core_swap(tiles), *mine],
    )
    got = [chip_swap(block, (k, k)) for k, block in zip(plan, send)]
    first = chip_swap(first, (far, far), lambda txt: int(txt % 2 == 0 or far % 2 == 1))
    second = chip_swap(second, (far, far), lambda txt: int(txt % 2 == 1 and far % 2 == 0))
    keep, send = call(sum_kernel, [single, piece], [own, *got])
    got = core_swap(send)
    column = jax.ShapeDtypeStruct((2 * rows, 1), f32)
    ready = call(unit_kernel, [total, column, single], [near, first], cost=LONG)
    kernel = functools.partial(out_kernel, far)
    return tuple(call(kernel, [single] * 2, [*ready, keep, second, got]))


def solution(mesh):
    return jax.shard_map(
        local,
        mesh=mesh,
        in_specs=(P(("img", "txt"), None), P(("txt", "img"), None), P("img")),
        out_specs=(P(("img", "txt"), None), P(("txt", "img"), None)),
        check_vma=False,
    )
```

```python
import functools

import jax
import jax.numpy as jnp
from jax import lax
from jax.experimental import pallas as pl
from jax.experimental.pallas import tpu as pltpu
from jax.sharding import PartitionSpec as P

scale_logit = 8.0
shift_logit = -4.0
epsilon = 1e-06
f32 = jnp.float32
bf16 = jnp.bfloat16
VMEM = pl.BlockSpec(memory_space=pltpu.VMEM)
LONG = pl.CostEstimate(flops=10**10, bytes_accessed=10**7, transcendentals=0)


def normalize(raw):
    values = raw.astype(f32)
    inverse = lax.rsqrt(jnp.sum(values * values, axis=-1, keepdims=True) + epsilon)
    return (values * inverse, inverse)


def back_norm(unit, inverse, grad):
    inner = jnp.sum(unit * grad, axis=-1, keepdims=True)
    return inverse * (grad - unit * inner)


def pair_coeff(logit, same):
    label = jnp.where(same, 1.0, -1.0).astype(f32)
    return (-scale_logit * label * jax.nn.sigmoid(-label * logit)).astype(bf16)


def core_swap(block):
    size = lax.axis_size("img")
    return lax.ppermute(block, "img", [(i, i ^ 1) for i in range(size)])


def chip_swap(block, distance, cross=lambda txt: 0):
    n_img, n_txt = lax.axis_size("img"), lax.axis_size("txt")
    pairs = []
    for img in range(n_img):
        for txt in range(n_txt):
            other = cross(txt)
            if img % 2 == 0 and distance < n_img // 2:
                pairs.append((img * n_txt + txt, (img ^ (2 * distance) ^ other) * n_txt + txt))
            if img % 2 == 1 and distance < n_txt:
                pairs.append((img * n_txt + txt, (img ^ other) * n_txt + (txt ^ distance)))
    return lax.ppermute(block, ("img", "txt"), pairs)


def is_even():
    return lax.axis_index("img") % 2 == 0


def call(kernel, outs, args, cost=None):
    sizes = [a.size * a.dtype.itemsize for a in list(args) + list(outs)]
    return pl.pallas_call(
        kernel,
        out_shape=outs,
        in_specs=[VMEM] * len(args),
        out_specs=[VMEM] * len(outs),
        cost_estimate=cost,
        compiler_params=pltpu.CompilerParams(
            vmem_limit_bytes=min(48 * 2**20, 8 * 2**20 + 6 * sum(sizes))
        ),
    )(*args)


def sides_kernel(own_ref, txt_ref, img_ref, mine_ref, other_ref):
    rows = txt_ref.shape[0]
    even = is_even()
    own = normalize(own_ref[...])[0].astype(bf16)
    own_txt, own_img = own[:rows], own[rows:]
    far_txt = normalize(txt_ref[...])[0].astype(bf16)
    far_img = normalize(img_ref[...])[0].astype(bf16)
    mine_ref[:rows, :] = jnp.where(even, own_txt, far_img)
    mine_ref[rows:, :] = jnp.where(even, far_txt, own_img)
    other_ref[:rows, :] = jnp.where(even, own_img, far_txt)
    other_ref[rows:, :] = jnp.where(even, far_img, own_txt)


def row_ids(rows, ids, far_ids, count):
    me_img = lax.axis_index("img")
    me_txt = lax.axis_index("txt")
    n_img = lax.axis_size("img")
    row = lax.broadcasted_iota(jnp.int32, (count, 1), 0)
    block, core, j = row // (2 * rows), row // rows % 2, row % rows
    chip = jnp.where(block == 0, 0, count // (2 * rows) - block)
    txt_ids = (me_txt * n_img + (((me_img // 2) ^ chip) * 2 + core)) * rows + j
    source = (me_txt ^ chip) * rows + j
    here = lax.broadcasted_iota(jnp.int32, (count, ids.shape[1]), 1) == source
    per_core = jnp.where(core == me_img % 2, ids, far_ids)
    img_ids = jnp.sum(jnp.where(here, per_core, 0), axis=1, keepdims=True)
    return txt_ids, img_ids


def side_ids(rows, ids, far_ids, count):
    even = is_even()
    txt_ids, img_ids = row_ids(rows, ids, far_ids, count)
    other_ids = jnp.where(even, img_ids, txt_ids)
    diagonal = lax.broadcasted_iota(jnp.int32, (count, count), 0) == lax.broadcasted_iota(
        jnp.int32, (count, count), 1
    )
    other_ids = jnp.sum(jnp.where(diagonal, other_ids, 0), axis=0, keepdims=True)
    return jnp.where(even, txt_ids, img_ids), other_ids


def scores_of(mine_refs, other_refs):
    mine = jnp.concatenate([ref[...] for ref in mine_refs], axis=0)
    other = jnp.concatenate([ref[...] for ref in other_refs], axis=0)
    return lax.dot_general(mine, other, (((1,), (1,)), ((), ())), preferred_element_type=f32)


def pair_kernel(blocks, ids_ref, far_ids_ref, *refs):
    mine_refs, other_refs = refs[:blocks], refs[blocks:2 * blocks]
    own_ref, *send_refs = refs[2 * blocks:]
    height = own_ref.shape[0]
    rows = height // 2
    mine_ids, other_ids = side_ids(rows, ids_ref[...], far_ids_ref[...], blocks * height)
    scores = scores_of(mine_refs, other_refs)
    coeff = pair_coeff(scale_logit * scores + shift_logit, mine_ids == other_ids)
    other = jnp.concatenate([ref[...] for ref in other_refs], axis=0)
    part = jnp.dot(coeff, other, preferred_element_type=f32)
    own_ref[...] = part[:height]
    for k, ref in enumerate(send_refs):
        ref[...] = part[(k + 1) * height:(k + 2) * height].astype(bf16)


def sum_kernel(own_ref, *refs):
    *got_refs, keep_ref, send_ref = refs
    rows = keep_ref.shape[0]
    total = own_ref[...]
    for ref in got_refs:
        total = total + ref[...].astype(f32)
    even = is_even()
    keep_ref[...] = jnp.where(even, total[:rows], total[rows:])
    send_ref[...] = jnp.where(even, total[rows:], total[:rows]).astype(bf16)


def keep_kernel(raw_ref, keep_ref, grad_ref, unit_ref, inverse_ref):
    rows = keep_ref.shape[0]
    even = is_even()
    unit, inverse = normalize(raw_ref[...])
    grad_ref[...] = back_norm(
        jnp.where(even, unit[:rows], unit[rows:]),
        jnp.where(even, inverse[:rows], inverse[rows:]),
        keep_ref[...],
    )
    unit_ref[...] = jnp.where(even, unit[rows:], unit[:rows])
    inverse_ref[...] = jnp.where(even, inverse[rows:], inverse[:rows])


def out_kernel(grad_ref, unit_ref, inverse_ref, got_ref, img_ref, txt_ref):
    even = is_even()
    keep = grad_ref[...]
    got = back_norm(unit_ref[...], inverse_ref[...], got_ref[...].astype(f32))
    txt_ref[...] = jnp.where(even, keep, got)
    img_ref[...] = jnp.where(even, got, keep)


def local(image_embeds, text_embeds, pair_ids):
    rows, width = image_embeds.shape
    blocks = max(lax.axis_size("img") // 2, lax.axis_size("txt"))
    pair = jax.ShapeDtypeStruct((2 * rows, width), bf16)
    total = jax.ShapeDtypeStruct((2 * rows, width), f32)
    piece = jax.ShapeDtypeStruct((rows, width), bf16)
    single = jax.ShapeDtypeStruct((rows, width), f32)
    ids = pair_ids.reshape(1, -1)
    far_txt = core_swap(text_embeds)
    far_img = core_swap(image_embeds)
    near = jnp.concatenate([text_embeds, image_embeds])
    mine, other = call(sides_kernel, [pair] * 2, [near, far_txt, far_img])
    order = list(range(blocks - 1, 0, -1))
    mine = [mine] + [chip_swap(mine, k) for k in order]
    other = [other, *[core_swap(block) for block in mine[1:-1]], chip_swap(mine[0], 1, lambda txt: 1)]
    own, *send = call(
        functools.partial(pair_kernel, blocks),
        [total] + [pair] * (blocks - 1),
        [ids, core_swap(ids), *mine, *other],
    )
    got = [chip_swap(block, k) for k, block in zip(order, send)]
    keep, send = call(sum_kernel, [single, piece], [own, *got])
    column = jax.ShapeDtypeStruct((rows, 1), f32)
    kept = call(keep_kernel, [single, single, column], [near, keep], cost=LONG)
    return tuple(call(out_kernel, [single] * 2, [*kept, core_swap(send)]))


def solution(mesh):
    return jax.shard_map(
        local,
        mesh=mesh,
        in_specs=(P(("img", "txt"), None), P(("txt", "img"), None), P("img")),
        out_specs=(P(("img", "txt"), None), P(("txt", "img"), None)),
        check_vma=False,
    )
```

```python
import functools

import jax
import jax.numpy as jnp
from jax import lax
from jax.experimental import pallas as pl
from jax.experimental.pallas import tpu as pltpu
from jax.sharding import PartitionSpec as P

scale_logit = 8.0
shift_logit = -4.0
epsilon = 1e-06
f32 = jnp.float32
bf16 = jnp.bfloat16
VMEM = pl.BlockSpec(memory_space=pltpu.VMEM)
LONG = pl.CostEstimate(flops=10**10, bytes_accessed=10**7, transcendentals=0)


def normalize(raw):
    values = raw.astype(f32)
    inverse = lax.rsqrt(jnp.sum(values * values, axis=-1, keepdims=True) + epsilon)
    return (values * inverse, inverse)


def back_norm(unit, inverse, grad):
    inner = jnp.sum(unit * grad, axis=-1, keepdims=True)
    return inverse * (grad - unit * inner)


def pair_coeff(logit, same):
    label = jnp.where(same, 1.0, -1.0).astype(f32)
    return (-scale_logit * label * jax.nn.sigmoid(-label * logit)).astype(bf16)


def core_swap(block):
    size = lax.axis_size("img")
    return lax.ppermute(block, "img", [(i, i ^ 1) for i in range(size)])


def core_send(block, source):
    size = lax.axis_size("img")
    return lax.ppermute(block, "img", [(i, i ^ 1) for i in range(source, size, 2)])


def chip_swap(block, distance, cross=lambda txt: 0):
    n_img, n_txt = lax.axis_size("img"), lax.axis_size("txt")
    pairs = []
    for img in range(n_img):
        for txt in range(n_txt):
            other = cross(txt)
            if img % 2 == 0 and distance < n_img // 2:
                pairs.append((img * n_txt + txt, (img ^ (2 * distance) ^ other) * n_txt + txt))
            if img % 2 == 1 and distance < n_txt:
                pairs.append((img * n_txt + txt, (img ^ other) * n_txt + (txt ^ distance)))
    return lax.ppermute(block, ("img", "txt"), pairs)


def cross_first(distance):
    return (lax.axis_index("txt") % 2 == 0) | (distance % 2 == 1)


def is_even():
    return lax.axis_index("img") % 2 == 0


def call(kernel, outs, args, cost=None):
    sizes = [a.size * a.dtype.itemsize for a in list(args) + list(outs)]
    return pl.pallas_call(
        kernel,
        out_shape=outs,
        in_specs=[VMEM] * len(args),
        out_specs=[VMEM] * len(outs),
        cost_estimate=cost,
        compiler_params=pltpu.CompilerParams(
            vmem_limit_bytes=min(48 * 2**20, 8 * 2**20 + 6 * sum(sizes))
        ),
    )(*args)


def mine_kernel(near_ref, txt_ref, img_ref, mine_ref):
    rows = txt_ref.shape[0]
    even = is_even()
    first = jnp.where(even, near_ref[:rows, :], img_ref[...])
    second = jnp.where(even, txt_ref[...], near_ref[rows:, :])
    mine_ref[:rows, :] = normalize(first)[0].astype(bf16)
    mine_ref[rows:, :] = normalize(second)[0].astype(bf16)


def other_kernel(near_ref, txt_ref, img_ref, mine_ref, other_ref, out_ref):
    rows = txt_ref.shape[0]
    even = is_even()
    first = jnp.where(even, near_ref[rows:, :], txt_ref[...])
    second = jnp.where(even, img_ref[...], near_ref[:rows, :])
    other_ref[:rows, :] = normalize(first)[0].astype(bf16)
    other_ref[rows:, :] = normalize(second)[0].astype(bf16)
    out_ref[...] = mine_ref[...]


def row_ids(rows, ids, far_ids, count):
    me_img = lax.axis_index("img")
    me_txt = lax.axis_index("txt")
    n_img = lax.axis_size("img")
    row = lax.broadcasted_iota(jnp.int32, (count, 1), 0)
    block, core, j = row // (2 * rows), row // rows % 2, row % rows
    chip = jnp.where(block == 0, 0, count // (2 * rows) - block)
    txt_ids = (me_txt * n_img + (((me_img // 2) ^ chip) * 2 + core)) * rows + j
    source = (me_txt ^ chip) * rows + j
    here = lax.broadcasted_iota(jnp.int32, (count, ids.shape[1]), 1) == source
    per_core = jnp.where(core == me_img % 2, ids, far_ids)
    img_ids = jnp.sum(jnp.where(here, per_core, 0), axis=1, keepdims=True)
    return txt_ids, img_ids


def side_ids(rows, ids, far_ids, count):
    even = is_even()
    txt_ids, img_ids = row_ids(rows, ids, far_ids, count)
    other_ids = jnp.where(even, img_ids, txt_ids)
    diagonal = lax.broadcasted_iota(jnp.int32, (count, count), 0) == lax.broadcasted_iota(
        jnp.int32, (count, count), 1
    )
    other_ids = jnp.sum(jnp.where(diagonal, other_ids, 0), axis=0, keepdims=True)
    return jnp.where(even, txt_ids, img_ids), other_ids


def scores_of(mine_refs, other_refs):
    mine = jnp.concatenate([ref[...] for ref in mine_refs], axis=0)
    other = jnp.concatenate([ref[...] for ref in other_refs], axis=0)
    return lax.dot_general(mine, other, (((1,), (1,)), ((), ())), preferred_element_type=f32)


def pair_kernel(blocks, split, ids_ref, far_ids_ref, *refs):
    mine_refs, other_refs = refs[:blocks], refs[blocks:2 * blocks]
    own_ref, first_ref, second_ref, *send_refs = refs[2 * blocks:]
    height = own_ref.shape[0]
    rows = height // 2
    mine_ids, other_ids = side_ids(rows, ids_ref[...], far_ids_ref[...], blocks * height)
    scores = scores_of(mine_refs, other_refs)
    coeff = pair_coeff(scale_logit * scores + shift_logit, mine_ids == other_ids)
    other = jnp.concatenate([ref[...] for ref in other_refs], axis=0)
    part = jnp.dot(coeff, other, preferred_element_type=f32)
    own_ref[...] = part[:height]
    whole = [k for k in range(1, blocks) if k != split]
    for k, ref in zip(whole, send_refs):
        ref[...] = part[k * height:(k + 1) * height].astype(bf16)
    block = part[split * height:(split + 1) * height].astype(bf16)
    even = is_even()
    first = jnp.logical_xor(even, cross_first(blocks - split))
    first_ref[...] = jnp.where(first, block[:rows], block[rows:])
    second_ref[...] = jnp.where(first, block[rows:], block[:rows])


def sum_kernel(own_ref, *refs):
    *got_refs, keep_ref, send_ref = refs
    rows = keep_ref.shape[0]
    total = own_ref[...]
    for ref in got_refs:
        total = total + ref[...].astype(f32)
    even = is_even()
    keep_ref[...] = jnp.where(even, total[:rows], total[rows:])
    send_ref[...] = jnp.where(even, total[rows:], total[:rows]).astype(bf16)


def unit_kernel(raw_ref, first_ref, unit_ref, inverse_ref, rest_ref):
    unit_ref[...], inverse_ref[...] = normalize(raw_ref[...])
    rest_ref[...] = first_ref[...].astype(f32)


def out_kernel(
    far, unit_ref, inverse_ref, first_ref, keep_ref, second_ref, got_ref, img_ref, txt_ref
):
    rows = keep_ref.shape[0]
    even = is_even()
    first, second = first_ref[...], second_ref[...].astype(f32)
    cross = cross_first(far)
    keep = keep_ref[...] + jnp.where(cross, second, first)
    got = got_ref[...].astype(f32) + jnp.where(cross, first, second)
    unit, inverse = unit_ref[...], inverse_ref[...]
    txt_ref[...] = back_norm(unit[:rows], inverse[:rows], jnp.where(even, keep, got))
    img_ref[...] = back_norm(unit[rows:], inverse[rows:], jnp.where(even, got, keep))


def local(image_embeds, text_embeds, pair_ids):
    rows, width = image_embeds.shape
    blocks = max(lax.axis_size("img") // 2, lax.axis_size("txt"))
    pair = jax.ShapeDtypeStruct((2 * rows, width), bf16)
    total = jax.ShapeDtypeStruct((2 * rows, width), f32)
    piece = jax.ShapeDtypeStruct((rows, width), bf16)
    single = jax.ShapeDtypeStruct((rows, width), f32)
    ids = pair_ids.reshape(1, -1)
    far_txt, far_img = core_send(text_embeds, 1), core_send(image_embeds, 0)
    late_txt, late_img = core_send(text_embeds, 0), core_send(image_embeds, 1)
    near = jnp.concatenate([text_embeds, image_embeds])
    (own,) = call(mine_kernel, [pair], [near, far_txt, far_img])
    other, again = call(other_kernel, [pair] * 2, [near, late_txt, late_img, own])
    order = list(range(blocks - 1, 0, -1))
    mine = [own] + [chip_swap(again if k == 1 else own, k) for k in order]
    other = [other, *[core_swap(block) for block in mine[1:-1]], chip_swap(mine[0], 1, lambda txt: 1)]
    split = blocks - 1
    own, first, second, *send = call(
        functools.partial(pair_kernel, blocks, split),
        [total] + [piece] * 2 + [pair] * (blocks - 2),
        [ids, core_swap(ids), *mine, *other],
    )
    far = order.pop(split - 1)
    got = [chip_swap(block, k) for k, block in zip(order, send)]
    first = chip_swap(first, far, lambda txt: int(txt % 2 == 0 or far % 2 == 1))
    second = chip_swap(second, far, lambda txt: int(txt % 2 == 1 and far % 2 == 0))
    keep, send = call(sum_kernel, [single, piece], [own, *got])
    got = core_swap(send)
    column = jax.ShapeDtypeStruct((2 * rows, 1), f32)
    ready = call(unit_kernel, [total, column, single], [near, first], cost=LONG)
    kernel = functools.partial(out_kernel, far)
    return tuple(call(kernel, [single] * 2, [*ready, keep, second, got]))


def solution(mesh):
    return jax.shard_map(
        local,
        mesh=mesh,
        in_specs=(P(("img", "txt"), None), P(("txt", "img"), None), P("img")),
        out_specs=(P(("img", "txt"), None), P(("txt", "img"), None)),
        check_vma=False,
    )
```

```python
import functools

import jax
import jax.numpy as jnp
from jax import lax
from jax.experimental import pallas as pl
from jax.experimental.pallas import tpu as pltpu
from jax.sharding import PartitionSpec as P

scale_logit = 8.0
shift_logit = -4.0
epsilon = 1e-06
f32 = jnp.float32
bf16 = jnp.bfloat16
VMEM = pl.BlockSpec(memory_space=pltpu.VMEM)
LONG = pl.CostEstimate(flops=10**10, bytes_accessed=10**7, transcendentals=0)


def normalize(raw):
    values = raw.astype(f32)
    inverse = lax.rsqrt(jnp.sum(values * values, axis=-1, keepdims=True) + epsilon)
    return (values * inverse, inverse)


def back_norm(unit, inverse, grad):
    inner = jnp.sum(unit * grad, axis=-1, keepdims=True)
    return inverse * (grad - unit * inner)


def pair_coeff(logit, same):
    label = jnp.where(same, 1.0, -1.0).astype(f32)
    return (-scale_logit * label * jax.nn.sigmoid(-label * logit)).astype(bf16)


def core_swap(block):
    size = lax.axis_size("img")
    return lax.ppermute(block, "img", [(i, i ^ 1) for i in range(size)])


def chip_swap(block, distances, cross=lambda txt: 0):
    n_img, n_txt = lax.axis_size("img"), lax.axis_size("txt")
    along_img, along_txt = distances
    pairs = []
    for img in range(n_img):
        for txt in range(n_txt):
            other = cross(txt)
            if img % 2 == 0 and along_img < n_img // 2:
                pairs.append((img * n_txt + txt, (img ^ (2 * along_img) ^ other) * n_txt + txt))
            if img % 2 == 1 and along_txt < n_txt:
                pairs.append((img * n_txt + txt, (img ^ other) * n_txt + (txt ^ along_txt)))
    return lax.ppermute(block, ("img", "txt"), pairs)


def orders(blocks):
    falling = list(range(blocks - 1, 0, -1))
    return falling, falling


def cross_first(distance):
    return (lax.axis_index("txt") % 2 == 0) | (distance % 2 == 1)


def is_even():
    return lax.axis_index("img") % 2 == 0


def call(kernel, outs, args, cost=None):
    sizes = [a.size * a.dtype.itemsize for a in list(args) + list(outs)]
    return pl.pallas_call(
        kernel,
        out_shape=outs,
        in_specs=[VMEM] * len(args),
        out_specs=[VMEM] * len(outs),
        cost_estimate=cost,
        compiler_params=pltpu.CompilerParams(
            vmem_limit_bytes=min(48 * 2**20, 8 * 2**20 + 6 * sum(sizes))
        ),
    )(*args)


def sides_kernel(own_ref, txt_ref, img_ref, mine_ref, other_ref):
    rows = txt_ref.shape[0]
    even = is_even()
    own = normalize(own_ref[...])[0].astype(bf16)
    own_txt, own_img = own[:rows], own[rows:]
    far_txt = normalize(txt_ref[...])[0].astype(bf16)
    far_img = normalize(img_ref[...])[0].astype(bf16)
    mine_ref[:rows, :] = jnp.where(even, own_txt, far_img)
    mine_ref[rows:, :] = jnp.where(even, far_txt, own_img)
    other_ref[:rows, :] = jnp.where(even, own_img, far_txt)
    other_ref[rows:, :] = jnp.where(even, far_img, own_txt)


def row_ids(rows, ids, far_ids, count):
    me_img = lax.axis_index("img")
    me_txt = lax.axis_index("txt")
    n_img = lax.axis_size("img")
    row = lax.broadcasted_iota(jnp.int32, (count, 1), 0)
    block, core, j = row // (2 * rows), row // rows % 2, row % rows
    chips = []
    for order in orders(count // (2 * rows)):
        chip = jnp.zeros_like(block)
        for k, distance in enumerate(order):
            chip = jnp.where(block == k + 1, distance, chip)
        chips.append(chip)
    txt_ids = (me_txt * n_img + (((me_img // 2) ^ chips[0]) * 2 + core)) * rows + j
    source = (me_txt ^ chips[1]) * rows + j
    here = lax.broadcasted_iota(jnp.int32, (count, ids.shape[1]), 1) == source
    per_core = jnp.where(core == me_img % 2, ids, far_ids)
    img_ids = jnp.sum(jnp.where(here, per_core, 0), axis=1, keepdims=True)
    return txt_ids, img_ids


def side_ids(rows, ids, far_ids, count):
    even = is_even()
    txt_ids, img_ids = row_ids(rows, ids, far_ids, count)
    other_ids = jnp.where(even, img_ids, txt_ids)
    diagonal = lax.broadcasted_iota(jnp.int32, (count, count), 0) == lax.broadcasted_iota(
        jnp.int32, (count, count), 1
    )
    other_ids = jnp.sum(jnp.where(diagonal, other_ids, 0), axis=0, keepdims=True)
    return jnp.where(even, txt_ids, img_ids), other_ids


def scores_of(mine_refs, other_refs):
    mine = jnp.concatenate([ref[...] for ref in mine_refs], axis=0)
    other = jnp.concatenate([ref[...] for ref in other_refs], axis=0)
    return lax.dot_general(mine, other, (((1,), (1,)), ((), ())), preferred_element_type=f32)


def pair_kernel(blocks, plan, ids_ref, far_ids_ref, *refs):
    mine_refs, other_refs = refs[:blocks], refs[blocks:2 * blocks]
    own_ref, first_ref, second_ref, *send_refs = refs[2 * blocks:]
    height = own_ref.shape[0]
    rows = height // 2
    mine_ids, other_ids = side_ids(rows, ids_ref[...], far_ids_ref[...], blocks * height)
    scores = scores_of(mine_refs, other_refs)
    coeff = pair_coeff(scale_logit * scores + shift_logit, mine_ids == other_ids)
    other = jnp.concatenate([ref[...] for ref in other_refs], axis=0)
    part = jnp.dot(coeff, other, preferred_element_type=f32)
    own_ref[...] = part[:height]
    even = is_even()
    txt_order, img_order = orders(blocks)

    def block_of(distances):
        starts = [
            (order.index(k) + 1) * height for order, k in zip((txt_order, img_order), distances)
        ]
        txt, img = [part[start:start + height] for start in starts]
        return jnp.where(even, txt, img).astype(bf16)

    *whole, split = plan
    for distances, ref in zip(whole, send_refs):
        ref[...] = block_of(distances)
    block = block_of(split)
    first = jnp.logical_xor(even, cross_first(split[0]))
    first_ref[...] = jnp.where(first, block[:rows], block[rows:])
    second_ref[...] = jnp.where(first, block[rows:], block[:rows])


def sum_kernel(own_ref, *refs):
    *got_refs, keep_ref, send_ref = refs
    rows = keep_ref.shape[0]
    total = own_ref[...]
    for ref in got_refs:
        total = total + ref[...].astype(f32)
    even = is_even()
    keep_ref[...] = jnp.where(even, total[:rows], total[rows:])
    send_ref[...] = jnp.where(even, total[rows:], total[:rows]).astype(bf16)


def keep_kernel(
    far, raw_ref, keep_ref, first_ref, second_ref, grad_ref, unit_ref, inverse_ref, rest_ref
):
    rows = keep_ref.shape[0]
    even = is_even()
    unit, inverse = normalize(raw_ref[...])
    first, second = first_ref[...].astype(f32), second_ref[...].astype(f32)
    cross = cross_first(far)
    grad_ref[...] = back_norm(
        jnp.where(even, unit[:rows], unit[rows:]),
        jnp.where(even, inverse[:rows], inverse[rows:]),
        keep_ref[...] + jnp.where(cross, second, first),
    )
    rest_ref[...] = jnp.where(cross, first, second)
    unit_ref[...] = jnp.where(even, unit[rows:], unit[:rows])
    inverse_ref[...] = jnp.where(even, inverse[rows:], inverse[:rows])


def out_kernel(grad_ref, unit_ref, inverse_ref, rest_ref, got_ref, img_ref, txt_ref):
    even = is_even()
    keep = grad_ref[...]
    got = back_norm(unit_ref[...], inverse_ref[...], got_ref[...].astype(f32) + rest_ref[...])
    txt_ref[...] = jnp.where(even, keep, got)
    img_ref[...] = jnp.where(even, got, keep)


def local(image_embeds, text_embeds, pair_ids):
    rows, width = image_embeds.shape
    blocks = max(lax.axis_size("img") // 2, lax.axis_size("txt"))
    pair = jax.ShapeDtypeStruct((2 * rows, width), bf16)
    total = jax.ShapeDtypeStruct((2 * rows, width), f32)
    piece = jax.ShapeDtypeStruct((rows, width), bf16)
    single = jax.ShapeDtypeStruct((rows, width), f32)
    ids = pair_ids.reshape(1, -1)
    far_txt = core_swap(text_embeds)
    far_img = core_swap(image_embeds)
    near = jnp.concatenate([text_embeds, image_embeds])
    mine, other = call(sides_kernel, [pair] * 2, [near, far_txt, far_img])
    mine = [mine] + [chip_swap(mine, distances) for distances in zip(*orders(blocks))]
    other = [other, *[core_swap(block) for block in mine[1:-1]], chip_swap(mine[0], (1, 1), lambda txt: 1)]
    txt_plan = list(range(blocks - 1, 0, -1))
    img_plan = txt_plan[1::-1] + txt_plan[2:]
    plan = list(zip(txt_plan, img_plan))
    far = plan[-1][0]
    own, first, second, *send = call(
        functools.partial(pair_kernel, blocks, plan),
        [total] + [piece] * 2 + [pair] * (blocks - 2),
        [ids, core_swap(ids), *mine, *other],
    )
    got = [chip_swap(block, distances) for distances, block in zip(plan, send)]
    first = chip_swap(first, (far, far), lambda txt: int(txt % 2 == 0 or far % 2 == 1))
    second = chip_swap(second, (far, far), lambda txt: int(txt % 2 == 1 and far % 2 == 0))
    keep, send = call(sum_kernel, [single, piece], [own, *got])
    got = core_swap(send)
    column = jax.ShapeDtypeStruct((rows, 1), f32)
    outs = [single, single, column, single]
    kept = call(functools.partial(keep_kernel, far), outs, [near, keep, first, second], cost=LONG)
    return tuple(call(out_kernel, [single] * 2, [*kept, got]))


def solution(mesh):
    return jax.shard_map(
        local,
        mesh=mesh,
        in_specs=(P(("img", "txt"), None), P(("txt", "img"), None), P("img")),
        out_specs=(P(("img", "txt"), None), P(("txt", "img"), None)),
        check_vma=False,
    )
```

```python
import functools

import jax
import jax.numpy as jnp
from jax import lax
from jax.experimental import pallas as pl
from jax.experimental.pallas import tpu as pltpu
from jax.sharding import PartitionSpec as P

scale_logit = 8.0
shift_logit = -4.0
epsilon = 1e-06
f32 = jnp.float32
bf16 = jnp.bfloat16
VMEM = pl.BlockSpec(memory_space=pltpu.VMEM)
LONG = pl.CostEstimate(flops=10**10, bytes_accessed=10**7, transcendentals=0)


def normalize(raw):
    values = raw.astype(f32)
    inverse = lax.rsqrt(jnp.sum(values * values, axis=-1, keepdims=True) + epsilon)
    return (values * inverse, inverse)


def back_norm(unit, inverse, grad):
    inner = jnp.sum(unit * grad, axis=-1, keepdims=True)
    return inverse * (grad - unit * inner)


def pair_coeff(logit, same):
    label = jnp.where(same, 1.0, -1.0).astype(f32)
    return (-scale_logit * label * jax.nn.sigmoid(-label * logit)).astype(bf16)


def core_swap(block):
    size = lax.axis_size("img")
    return lax.ppermute(block, "img", [(i, i ^ 1) for i in range(size)])


def chip_swap(block, distance, cross=lambda img, txt: 0):
    n_img, n_txt = lax.axis_size("img"), lax.axis_size("txt")
    pairs = []
    for img in range(n_img):
        for txt in range(n_txt):
            other = cross(img, txt)
            if img % 2 == 0 and distance < n_img // 2:
                pairs.append((img * n_txt + txt, (img ^ (2 * distance) ^ other) * n_txt + txt))
            if img % 2 == 1 and distance < n_txt:
                pairs.append((img * n_txt + txt, (img ^ other) * n_txt + (txt ^ distance)))
    return lax.ppermute(block, ("img", "txt"), pairs)


def cross_first(img, txt, distance):
    return (txt + img % 2 * distance) % 2 == 0


def gets_cross_first():
    return lax.axis_index("txt") % 2 == 0


def is_even():
    return lax.axis_index("img") % 2 == 0


def call(kernel, outs, args, cost=None):
    sizes = [a.size * a.dtype.itemsize for a in list(args) + list(outs)]
    return pl.pallas_call(
        kernel,
        out_shape=outs,
        in_specs=[VMEM] * len(args),
        out_specs=[VMEM] * len(outs),
        cost_estimate=cost,
        compiler_params=pltpu.CompilerParams(
            vmem_limit_bytes=min(48 * 2**20, 8 * 2**20 + 6 * sum(sizes))
        ),
    )(*args)


def sides_kernel(own_ref, txt_ref, img_ref, mine_ref, other_ref):
    rows = txt_ref.shape[0]
    even = is_even()
    own = normalize(own_ref[...])[0].astype(bf16)
    own_txt, own_img = own[:rows], own[rows:]
    far_txt = normalize(txt_ref[...])[0].astype(bf16)
    far_img = normalize(img_ref[...])[0].astype(bf16)
    mine_ref[:rows, :] = jnp.where(even, own_txt, far_img)
    mine_ref[rows:, :] = jnp.where(even, far_txt, own_img)
    other_ref[:rows, :] = jnp.where(even, own_img, far_txt)
    other_ref[rows:, :] = jnp.where(even, far_img, own_txt)


def row_ids(rows, ids, far_ids, count):
    me_img = lax.axis_index("img")
    me_txt = lax.axis_index("txt")
    n_img = lax.axis_size("img")
    row = lax.broadcasted_iota(jnp.int32, (count, 1), 0)
    block, core, j = row // (2 * rows), row // rows % 2, row % rows
    chip = jnp.where(block == 0, 0, count // (2 * rows) - block)
    txt_ids = (me_txt * n_img + (((me_img // 2) ^ chip) * 2 + core)) * rows + j
    source = (me_txt ^ chip) * rows + j
    here = lax.broadcasted_iota(jnp.int32, (count, ids.shape[1]), 1) == source
    per_core = jnp.where(core == me_img % 2, ids, far_ids)
    img_ids = jnp.sum(jnp.where(here, per_core, 0), axis=1, keepdims=True)
    return txt_ids, img_ids


def side_ids(rows, ids, far_ids, count):
    even = is_even()
    txt_ids, img_ids = row_ids(rows, ids, far_ids, count)
    other_ids = jnp.where(even, img_ids, txt_ids)
    diagonal = lax.broadcasted_iota(jnp.int32, (count, count), 0) == lax.broadcasted_iota(
        jnp.int32, (count, count), 1
    )
    other_ids = jnp.sum(jnp.where(diagonal, other_ids, 0), axis=0, keepdims=True)
    return jnp.where(even, txt_ids, img_ids), other_ids


def scores_of(mine_refs, other_refs):
    mine = jnp.concatenate([ref[...] for ref in mine_refs], axis=0)
    other = jnp.concatenate([ref[...] for ref in other_refs], axis=0)
    return lax.dot_general(mine, other, (((1,), (1,)), ((), ())), preferred_element_type=f32)


def pair_kernel(blocks, split, ids_ref, far_ids_ref, *refs):
    mine_refs, other_refs = refs[:blocks], refs[blocks:2 * blocks]
    own_ref, first_ref, second_ref, *send_refs = refs[2 * blocks:]
    height = own_ref.shape[0]
    rows = height // 2
    mine_ids, other_ids = side_ids(rows, ids_ref[...], far_ids_ref[...], blocks * height)
    scores = scores_of(mine_refs, other_refs)
    coeff = pair_coeff(scale_logit * scores + shift_logit, mine_ids == other_ids)
    other = jnp.concatenate([ref[...] for ref in other_refs], axis=0)
    part = jnp.dot(coeff, other, preferred_element_type=f32)
    own_ref[...] = part[:height]
    whole = [k for k in range(1, blocks) if k != split]
    for k, ref in zip(whole, send_refs):
        ref[...] = part[k * height:(k + 1) * height].astype(bf16)
    block = part[split * height:(split + 1) * height].astype(bf16)
    even = is_even()
    crosses = cross_first(lax.axis_index("img"), lax.axis_index("txt"), blocks - split)
    first = jnp.logical_xor(even, crosses)
    first_ref[...] = jnp.where(first, block[:rows], block[rows:])
    second_ref[...] = jnp.where(first, block[rows:], block[:rows])


def sum_kernel(own_ref, *refs):
    *got_refs, keep_ref, send_ref = refs
    rows = keep_ref.shape[0]
    total = own_ref[...]
    for ref in got_refs:
        total = total + ref[...].astype(f32)
    even = is_even()
    keep_ref[...] = jnp.where(even, total[:rows], total[rows:])
    send_ref[...] = jnp.where(even, total[rows:], total[:rows]).astype(bf16)


def unit_kernel(raw_ref, first_ref, unit_ref, inverse_ref, rest_ref):
    unit_ref[...], inverse_ref[...] = normalize(raw_ref[...])
    rest_ref[...] = first_ref[...].astype(f32)


def out_kernel(
    unit_ref, inverse_ref, first_ref, keep_ref, second_ref, got_ref, img_ref, txt_ref
):
    rows = keep_ref.shape[0]
    even = is_even()
    first, second = first_ref[...], second_ref[...].astype(f32)
    cross = gets_cross_first()
    keep = keep_ref[...] + jnp.where(cross, second, first)
    got = got_ref[...].astype(f32) + jnp.where(cross, first, second)
    unit, inverse = unit_ref[...], inverse_ref[...]
    txt_ref[...] = back_norm(unit[:rows], inverse[:rows], jnp.where(even, keep, got))
    img_ref[...] = back_norm(unit[rows:], inverse[rows:], jnp.where(even, got, keep))


def local(image_embeds, text_embeds, pair_ids):
    rows, width = image_embeds.shape
    blocks = max(lax.axis_size("img") // 2, lax.axis_size("txt"))
    pair = jax.ShapeDtypeStruct((2 * rows, width), bf16)
    total = jax.ShapeDtypeStruct((2 * rows, width), f32)
    piece = jax.ShapeDtypeStruct((rows, width), bf16)
    single = jax.ShapeDtypeStruct((rows, width), f32)
    ids = pair_ids.reshape(1, -1)
    far_txt = core_swap(text_embeds)
    far_img = core_swap(image_embeds)
    near = jnp.concatenate([text_embeds, image_embeds])
    mine, other = call(sides_kernel, [pair] * 2, [near, far_txt, far_img])
    order = list(range(blocks - 1, 0, -1))
    mine = [mine] + [chip_swap(mine, k) for k in order]
    other = [other, *[core_swap(block) for block in mine[1:-1]], chip_swap(mine[0], 1, lambda img, txt: 1)]
    split = blocks - 1
    own, first, second, *send = call(
        functools.partial(pair_kernel, blocks, split),
        [total] + [piece] * 2 + [pair] * (blocks - 2),
        [ids, core_swap(ids), *mine, *other],
    )
    far = order.pop(split - 1)
    got = [chip_swap(block, k) for k, block in zip(order, send)]
    first = chip_swap(first, far, lambda img, txt: int(cross_first(img, txt, far)))
    second = chip_swap(second, far, lambda img, txt: int(not cross_first(img, txt, far)))
    keep, send = call(sum_kernel, [single, piece], [own, *got])
    got = core_swap(send)
    column = jax.ShapeDtypeStruct((2 * rows, 1), f32)
    ready = call(unit_kernel, [total, column, single], [near, first], cost=LONG)
    return tuple(call(out_kernel, [single] * 2, [*ready, keep, second, got]))


def solution(mesh):
    return jax.shard_map(
        local,
        mesh=mesh,
        in_specs=(P(("img", "txt"), None), P(("txt", "img"), None), P("img")),
        out_specs=(P(("img", "txt"), None), P(("txt", "img"), None)),
        check_vma=False,
    )
```

```python
import functools

import jax
import jax.numpy as jnp
from jax import lax
from jax.experimental import pallas as pl
from jax.experimental.pallas import tpu as pltpu
from jax.sharding import PartitionSpec as P

scale_logit = 8.0
shift_logit = -4.0
epsilon = 1e-06
f32 = jnp.float32
bf16 = jnp.bfloat16
VMEM = pl.BlockSpec(memory_space=pltpu.VMEM)
LONG = pl.CostEstimate(flops=10**10, bytes_accessed=10**7, transcendentals=0)


def normalize(raw):
    values = raw.astype(f32)
    inverse = lax.rsqrt(jnp.sum(values * values, axis=-1, keepdims=True) + epsilon)
    return (values * inverse, inverse)


def back_norm(unit, inverse, grad):
    inner = jnp.sum(unit * grad, axis=-1, keepdims=True)
    return inverse * (grad - unit * inner)


def pair_coeff(logit, same):
    label = jnp.where(same, 1.0, -1.0).astype(f32)
    return (-scale_logit * label * jax.nn.sigmoid(-label * logit)).astype(bf16)


def core_swap(block):
    size = lax.axis_size("img")
    return lax.ppermute(block, "img", [(i, i ^ 1) for i in range(size)])


def chip_swap(block, distance, cross=lambda img, txt: 0):
    n_img, n_txt = lax.axis_size("img"), lax.axis_size("txt")
    pairs = []
    for img in range(n_img):
        for txt in range(n_txt):
            other = cross(img, txt)
            if img % 2 == 0 and distance < n_img // 2:
                pairs.append((img * n_txt + txt, (img ^ (2 * distance) ^ other) * n_txt + txt))
            if img % 2 == 1 and distance < n_txt:
                pairs.append((img * n_txt + txt, (img ^ other) * n_txt + (txt ^ distance)))
    return lax.ppermute(block, ("img", "txt"), pairs)


def cross_first(img, txt, distance):
    return (txt + img % 2 * distance) % 2 == 0


def gets_cross_first():
    return lax.axis_index("txt") % 2 == 0


def is_even():
    return lax.axis_index("img") % 2 == 0


def call(kernel, outs, args, cost=None):
    sizes = [a.size * a.dtype.itemsize for a in list(args) + list(outs)]
    return pl.pallas_call(
        kernel,
        out_shape=outs,
        in_specs=[VMEM] * len(args),
        out_specs=[VMEM] * len(outs),
        cost_estimate=cost,
        compiler_params=pltpu.CompilerParams(
            vmem_limit_bytes=min(48 * 2**20, 8 * 2**20 + 6 * sum(sizes))
        ),
    )(*args)


def sides_kernel(own_ref, txt_ref, img_ref, mine_ref, other_ref):
    rows = txt_ref.shape[0]
    even = is_even()
    own = normalize(own_ref[...])[0].astype(bf16)
    own_txt, own_img = own[:rows], own[rows:]
    far_txt = normalize(txt_ref[...])[0].astype(bf16)
    far_img = normalize(img_ref[...])[0].astype(bf16)
    mine_ref[:rows, :] = jnp.where(even, own_txt, far_img)
    mine_ref[rows:, :] = jnp.where(even, far_txt, own_img)
    other_ref[:rows, :] = jnp.where(even, own_img, far_txt)
    other_ref[rows:, :] = jnp.where(even, far_img, own_txt)


def row_ids(rows, ids, far_ids, count):
    me_img = lax.axis_index("img")
    me_txt = lax.axis_index("txt")
    n_img = lax.axis_size("img")
    row = lax.broadcasted_iota(jnp.int32, (count, 1), 0)
    block, core, j = row // (2 * rows), row // rows % 2, row % rows
    chip = jnp.where(block == 0, 0, count // (2 * rows) - block)
    txt_ids = (me_txt * n_img + (((me_img // 2) ^ chip) * 2 + core)) * rows + j
    source = (me_txt ^ chip) * rows + j
    here = lax.broadcasted_iota(jnp.int32, (count, ids.shape[1]), 1) == source
    per_core = jnp.where(core == me_img % 2, ids, far_ids)
    img_ids = jnp.sum(jnp.where(here, per_core, 0), axis=1, keepdims=True)
    return txt_ids, img_ids


def side_ids(rows, ids, far_ids, count):
    even = is_even()
    txt_ids, img_ids = row_ids(rows, ids, far_ids, count)
    other_ids = jnp.where(even, img_ids, txt_ids)
    diagonal = lax.broadcasted_iota(jnp.int32, (count, count), 0) == lax.broadcasted_iota(
        jnp.int32, (count, count), 1
    )
    other_ids = jnp.sum(jnp.where(diagonal, other_ids, 0), axis=0, keepdims=True)
    return jnp.where(even, txt_ids, img_ids), other_ids


def scores_of(mine_refs, other_refs):
    mine = jnp.concatenate([ref[...] for ref in mine_refs], axis=0)
    other = jnp.concatenate([ref[...] for ref in other_refs], axis=0)
    return lax.dot_general(mine, other, (((1,), (1,)), ((), ())), preferred_element_type=f32)


def pair_kernel(blocks, split, ids_ref, far_ids_ref, *refs):
    mine_refs, other_refs = refs[:blocks], refs[blocks:2 * blocks]
    own_ref, first_ref, second_ref, *send_refs = refs[2 * blocks:]
    height = own_ref.shape[0]
    rows = height // 2
    mine_ids, other_ids = side_ids(rows, ids_ref[...], far_ids_ref[...], blocks * height)
    scores = scores_of(mine_refs, other_refs)
    coeff = pair_coeff(scale_logit * scores + shift_logit, mine_ids == other_ids)
    other = jnp.concatenate([ref[...] for ref in other_refs], axis=0)
    part = jnp.dot(coeff, other, preferred_element_type=f32)
    own_ref[...] = part[:height]
    whole = [k for k in range(1, blocks) if k != split]
    for k, ref in zip(whole, send_refs):
        ref[...] = part[k * height:(k + 1) * height].astype(bf16)
    block = part[split * height:(split + 1) * height].astype(bf16)
    even = is_even()
    crosses = cross_first(lax.axis_index("img"), lax.axis_index("txt"), blocks - split)
    first = jnp.logical_xor(even, crosses)
    first_ref[...] = jnp.where(first, block[:rows], block[rows:])
    second_ref[...] = jnp.where(first, block[rows:], block[:rows])


def sum_kernel(own_ref, *refs):
    *got_refs, keep_ref, send_ref = refs
    rows = keep_ref.shape[0]
    total = own_ref[...]
    for ref in got_refs:
        total = total + ref[...].astype(f32)
    even = is_even()
    keep_ref[...] = jnp.where(even, total[:rows], total[rows:])
    send_ref[...] = jnp.where(even, total[rows:], total[:rows]).astype(bf16)


def keep_kernel(
    raw_ref, keep_ref, first_ref, second_ref, grad_ref, unit_ref, inverse_ref, rest_ref
):
    rows = keep_ref.shape[0]
    even = is_even()
    unit, inverse = normalize(raw_ref[...])
    first, second = first_ref[...].astype(f32), second_ref[...].astype(f32)
    cross = gets_cross_first()
    grad_ref[...] = back_norm(
        jnp.where(even, unit[:rows], unit[rows:]),
        jnp.where(even, inverse[:rows], inverse[rows:]),
        keep_ref[...] + jnp.where(cross, second, first),
    )
    rest_ref[...] = jnp.where(cross, first, second)
    unit_ref[...] = jnp.where(even, unit[rows:], unit[:rows])
    inverse_ref[...] = jnp.where(even, inverse[rows:], inverse[:rows])


def out_kernel(
    grad_ref, unit_ref, inverse_ref, rest_ref, got_ref, img_ref, txt_ref, other_ref, sems
):
    def write(keep_out, got_out):
        kept = pltpu.make_async_copy(grad_ref, keep_out, sems.at[0])
        kept.start()
        total = got_ref[...].astype(f32) + rest_ref[...]
        other_ref[...] = back_norm(unit_ref[...], inverse_ref[...], total)
        other = pltpu.make_async_copy(other_ref, got_out, sems.at[1])
        other.start()
        kept.wait()
        other.wait()

    @pl.when(is_even())
    def _():
        write(txt_ref, img_ref)

    @pl.when(jnp.logical_not(is_even()))
    def _():
        write(img_ref, txt_ref)


def local(image_embeds, text_embeds, pair_ids):
    rows, width = image_embeds.shape
    blocks = max(lax.axis_size("img") // 2, lax.axis_size("txt"))
    pair = jax.ShapeDtypeStruct((2 * rows, width), bf16)
    total = jax.ShapeDtypeStruct((2 * rows, width), f32)
    piece = jax.ShapeDtypeStruct((rows, width), bf16)
    single = jax.ShapeDtypeStruct((rows, width), f32)
    ids = pair_ids.reshape(1, -1)
    far_txt = core_swap(text_embeds)
    far_img = core_swap(image_embeds)
    near = jnp.concatenate([text_embeds, image_embeds])
    mine, other = call(sides_kernel, [pair] * 2, [near, far_txt, far_img])
    order = list(range(blocks - 1, 0, -1))
    mine = [mine] + [chip_swap(mine, k) for k in order]
    other = [other, *[core_swap(block) for block in mine[1:-1]], chip_swap(mine[0], 1, lambda img, txt: 1)]
    split = blocks - 1
    own, first, second, *send = call(
        functools.partial(pair_kernel, blocks, split),
        [total] + [piece] * 2 + [pair] * (blocks - 2),
        [ids, core_swap(ids), *mine, *other],
    )
    far = order.pop(split - 1)
    got = [chip_swap(block, k) for k, block in zip(order, send)]
    first = chip_swap(first, far, lambda img, txt: int(cross_first(img, txt, far)))
    second = chip_swap(second, far, lambda img, txt: int(not cross_first(img, txt, far)))
    keep, send = call(sum_kernel, [single, piece], [own, *got])
    got = core_swap(send)
    column = jax.ShapeDtypeStruct((rows, 1), f32)
    outs = [single, single, column, single]
    kept = call(keep_kernel, outs, [near, keep, first, second], cost=LONG)
    return tuple(
        pl.pallas_call(
            out_kernel,
            out_shape=[single] * 2,
            in_specs=[VMEM] * 5,
            out_specs=[pl.BlockSpec(memory_space=pl.ANY)] * 2,
            scratch_shapes=[pltpu.VMEM((rows, width), f32), pltpu.SemaphoreType.DMA((2,))],
        )(*kept, got)
    )


def solution(mesh):
    return jax.shard_map(
        local,
        mesh=mesh,
        in_specs=(P(("img", "txt"), None), P(("txt", "img"), None), P("img")),
        out_specs=(P(("img", "txt"), None), P(("txt", "img"), None)),
        check_vma=False,
    )
```

```python
import functools

import jax
import jax.numpy as jnp
from jax import lax
from jax.experimental import pallas as pl
from jax.experimental.pallas import tpu as pltpu
from jax.sharding import PartitionSpec as P

scale_logit = 8.0
shift_logit = -4.0
epsilon = 1e-06
f32 = jnp.float32
bf16 = jnp.bfloat16
VMEM = pl.BlockSpec(memory_space=pltpu.VMEM)
LONG = pl.CostEstimate(flops=10**10, bytes_accessed=10**7, transcendentals=0)


def normalize(raw):
    values = raw.astype(f32)
    inverse = lax.rsqrt(jnp.sum(values * values, axis=-1, keepdims=True) + epsilon)
    return (values * inverse, inverse)


def back_norm(unit, inverse, grad):
    inner = jnp.sum(unit * grad, axis=-1, keepdims=True)
    return inverse * (grad - unit * inner)


def pair_coeff(logit, same):
    label = jnp.where(same, 1.0, -1.0).astype(f32)
    return (-scale_logit * label * jax.nn.sigmoid(-label * logit)).astype(bf16)


def core_swap(block):
    size = lax.axis_size("img")
    return lax.ppermute(block, "img", [(i, i ^ 1) for i in range(size)])


def chip_swap(block, distance, cross=lambda img, txt: 0):
    n_img, n_txt = lax.axis_size("img"), lax.axis_size("txt")
    pairs = []
    for img in range(n_img):
        for txt in range(n_txt):
            other = cross(img, txt)
            if img % 2 == 0 and distance < n_img // 2:
                pairs.append((img * n_txt + txt, (img ^ (2 * distance) ^ other) * n_txt + txt))
            if img % 2 == 1 and distance < n_txt:
                pairs.append((img * n_txt + txt, (img ^ other) * n_txt + (txt ^ distance)))
    return lax.ppermute(block, ("img", "txt"), pairs)


def cross_first(img, txt, distance):
    return (txt + img % 2 * distance) % 2 == 1


def gets_cross_first():
    return lax.axis_index("txt") % 2 == 1


def is_even():
    return lax.axis_index("img") % 2 == 0


def call(kernel, outs, args, cost=None):
    sizes = [a.size * a.dtype.itemsize for a in list(args) + list(outs)]
    return pl.pallas_call(
        kernel,
        out_shape=outs,
        in_specs=[VMEM] * len(args),
        out_specs=[VMEM] * len(outs),
        cost_estimate=cost,
        compiler_params=pltpu.CompilerParams(
            vmem_limit_bytes=min(48 * 2**20, 8 * 2**20 + 6 * sum(sizes))
        ),
    )(*args)


def sides_kernel(own_ref, txt_ref, img_ref, mine_ref, other_ref):
    rows = txt_ref.shape[0]
    even = is_even()
    own = normalize(own_ref[...])[0].astype(bf16)
    own_txt, own_img = own[:rows], own[rows:]
    far_txt = normalize(txt_ref[...])[0].astype(bf16)
    far_img = normalize(img_ref[...])[0].astype(bf16)
    mine_ref[:rows, :] = jnp.where(even, own_txt, far_img)
    mine_ref[rows:, :] = jnp.where(even, far_txt, own_img)
    other_ref[:rows, :] = jnp.where(even, own_img, far_txt)
    other_ref[rows:, :] = jnp.where(even, far_img, own_txt)


def row_ids(rows, ids, far_ids, count):
    me_img = lax.axis_index("img")
    me_txt = lax.axis_index("txt")
    n_img = lax.axis_size("img")
    row = lax.broadcasted_iota(jnp.int32, (count, 1), 0)
    block, core, j = row // (2 * rows), row // rows % 2, row % rows
    chip = jnp.where(block == 0, 0, count // (2 * rows) - block)
    txt_ids = (me_txt * n_img + (((me_img // 2) ^ chip) * 2 + core)) * rows + j
    source = (me_txt ^ chip) * rows + j
    here = lax.broadcasted_iota(jnp.int32, (count, ids.shape[1]), 1) == source
    per_core = jnp.where(core == me_img % 2, ids, far_ids)
    img_ids = jnp.sum(jnp.where(here, per_core, 0), axis=1, keepdims=True)
    return txt_ids, img_ids


def side_ids(rows, ids, far_ids, count):
    even = is_even()
    txt_ids, img_ids = row_ids(rows, ids, far_ids, count)
    other_ids = jnp.where(even, img_ids, txt_ids)
    diagonal = lax.broadcasted_iota(jnp.int32, (count, count), 0) == lax.broadcasted_iota(
        jnp.int32, (count, count), 1
    )
    other_ids = jnp.sum(jnp.where(diagonal, other_ids, 0), axis=0, keepdims=True)
    return jnp.where(even, txt_ids, img_ids), other_ids


def scores_of(mine_refs, other_refs):
    mine = jnp.concatenate([ref[...] for ref in mine_refs], axis=0)
    other = jnp.concatenate([ref[...] for ref in other_refs], axis=0)
    return lax.dot_general(mine, other, (((1,), (1,)), ((), ())), preferred_element_type=f32)


def pair_kernel(blocks, split, ids_ref, far_ids_ref, *refs):
    mine_refs, other_refs = refs[:blocks], refs[blocks:2 * blocks]
    own_ref, first_ref, second_ref, *send_refs = refs[2 * blocks:]
    height = own_ref.shape[0]
    rows = height // 2
    mine_ids, other_ids = side_ids(rows, ids_ref[...], far_ids_ref[...], blocks * height)
    scores = scores_of(mine_refs, other_refs)
    coeff = pair_coeff(scale_logit * scores + shift_logit, mine_ids == other_ids)
    other = jnp.concatenate([ref[...] for ref in other_refs], axis=0)
    part = jnp.dot(coeff, other, preferred_element_type=f32)
    own_ref[...] = part[:height]
    whole = [k for k in range(1, blocks) if k != split]
    for k, ref in zip(whole, send_refs):
        ref[...] = part[k * height:(k + 1) * height].astype(bf16)
    block = part[split * height:(split + 1) * height].astype(bf16)
    even = is_even()
    crosses = cross_first(lax.axis_index("img"), lax.axis_index("txt"), blocks - split)
    first = jnp.logical_xor(even, crosses)
    first_ref[...] = jnp.where(first, block[:rows], block[rows:])
    second_ref[...] = jnp.where(first, block[rows:], block[:rows])


def sum_kernel(own_ref, *refs):
    *got_refs, keep_ref, send_ref = refs
    rows = keep_ref.shape[0]
    total = own_ref[...]
    for ref in got_refs:
        total = total + ref[...].astype(f32)
    even = is_even()
    keep_ref[...] = jnp.where(even, total[:rows], total[rows:])
    send_ref[...] = jnp.where(even, total[rows:], total[:rows]).astype(bf16)


def unit_kernel(raw_ref, first_ref, unit_ref, inverse_ref, rest_ref):
    unit_ref[...], inverse_ref[...] = normalize(raw_ref[...])
    rest_ref[...] = first_ref[...].astype(f32)


def out_kernel(
    unit_ref, inverse_ref, first_ref, keep_ref, second_ref, got_ref, img_ref, txt_ref
):
    rows = keep_ref.shape[0]
    even = is_even()
    first, second = first_ref[...], second_ref[...].astype(f32)
    cross = gets_cross_first()
    keep = keep_ref[...] + jnp.where(cross, second, first)
    got = got_ref[...].astype(f32) + jnp.where(cross, first, second)
    unit, inverse = unit_ref[...], inverse_ref[...]
    txt_ref[...] = back_norm(unit[:rows], inverse[:rows], jnp.where(even, keep, got))
    img_ref[...] = back_norm(unit[rows:], inverse[rows:], jnp.where(even, got, keep))


def local(image_embeds, text_embeds, pair_ids):
    rows, width = image_embeds.shape
    blocks = max(lax.axis_size("img") // 2, lax.axis_size("txt"))
    pair = jax.ShapeDtypeStruct((2 * rows, width), bf16)
    total = jax.ShapeDtypeStruct((2 * rows, width), f32)
    piece = jax.ShapeDtypeStruct((rows, width), bf16)
    single = jax.ShapeDtypeStruct((rows, width), f32)
    ids = pair_ids.reshape(1, -1)
    far_txt = core_swap(text_embeds)
    far_img = core_swap(image_embeds)
    near = jnp.concatenate([text_embeds, image_embeds])
    mine, other = call(sides_kernel, [pair] * 2, [near, far_txt, far_img])
    order = list(range(blocks - 1, 0, -1))
    mine = [mine] + [chip_swap(mine, k) for k in order]
    other = [other, *[core_swap(block) for block in mine[1:-1]], chip_swap(mine[0], 1, lambda img, txt: 1)]
    split = blocks - 1
    own, first, second, *send = call(
        functools.partial(pair_kernel, blocks, split),
        [total] + [piece] * 2 + [pair] * (blocks - 2),
        [ids, core_swap(ids), *mine, *other],
    )
    far = order.pop(split - 1)
    got = [chip_swap(block, k) for k, block in zip(order, send)]
    first = chip_swap(first, far, lambda img, txt: int(cross_first(img, txt, far)))
    second = chip_swap(second, far, lambda img, txt: int(not cross_first(img, txt, far)))
    keep, send = call(sum_kernel, [single, piece], [own, *got])
    got = core_swap(send)
    column = jax.ShapeDtypeStruct((2 * rows, 1), f32)
    ready = call(unit_kernel, [total, column, single], [near, first], cost=LONG)
    return tuple(call(out_kernel, [single] * 2, [*ready, keep, second, got]))


def solution(mesh):
    return jax.shard_map(
        local,
        mesh=mesh,
        in_specs=(P(("img", "txt"), None), P(("txt", "img"), None), P("img")),
        out_specs=(P(("img", "txt"), None), P(("txt", "img"), None)),
        check_vma=False,
    )
```
